32 devices in a mesh: sx: 4 (over z), sy: 8 (over y, x, core).
Axes of the slice: x: 2, y: 2, z: 4, core: 2. Of those that a mesh axis runs over, the one named last changes fastest.
Arguments:
- fine_matrix: bfloat16 [8, 16, 2, 7, 64, 64], P('sx', 'sy'), may hold values from -0.75 to 0.75
- prolongator: bfloat16 [8, 16, 2, 7, 64, 64], P('sx', 'sy'), may hold values from -2.5 to 2.5
- aggregate: int32 [8, 16, 2], P('sx', 'sy'), may hold values from 0 to 31, as said below
- face_links: int32 [8, 16, 2, 6], P('sx', 'sy'), may hold values from 0 to 1, as said below
Outputs:
- coarse: bfloat16 [4, 8, 7, 7, 64, 64], P('sx', 'sy')
The draws below stay inside these ranges and needn't reach their ends.
Inputs may be any that keep to these rules, and one draw needn't show every extreme that they name: aggregate[i] is the id bx 8 + by of a box of 2 x 2 x 2 elements: the box that holds element i, or the box beside it across a box face on which element i lies (faces along x or y). face_links[i, f] is the same on both sides of a face, and 0 on the outer faces of the grid.
All inputs are finite; a program needn't handle non-finite values.
Results may differ from the reference program's by a relative error of at most 0.007.
Values may be sent and summed in bfloat16 or wider, within the bound.
No kernel may reach another device: no remote copies, remote signals or barrier semaphores. Data moves between devices by JAX's collectives and lax.ppermute only.
A program may use at most 320 MiB of HBM per device.

```python
import jax
import jax.numpy as jnp
from jax import lax

B = 64
CB = 64
NX = 8
NY = 16
BOXES_X = 4
BOXES_Y = 8


def draw_face_links(key, part):
    key_x, key_y, key_z = jax.random.split(key, 3)
    link_x = (jax.random.randint(key_x, (NX - 1, NY, 2), 0, 20) < 17).astype(jnp.int32)
    link_y = (jax.random.randint(key_y, (NX, NY - 1, 2), 0, 20) < 17).astype(jnp.int32)
    link_z = (jax.random.randint(key_z, (NX, NY, 1), 0, 20) < 17).astype(jnp.int32)
    empty_x = jnp.zeros((1, NY, 2), jnp.int32)
    empty_y = jnp.zeros((NX, 1, 2), jnp.int32)
    empty_z = jnp.zeros((NX, NY, 1), jnp.int32)
    minus_x = jnp.concatenate([empty_x, link_x], axis=0)
    plus_x = jnp.concatenate([link_x, empty_x], axis=0)
    minus_y = jnp.concatenate([empty_y, link_y], axis=1)
    plus_y = jnp.concatenate([link_y, empty_y], axis=1)
    minus_z = jnp.concatenate([empty_z, link_z], axis=2)
    plus_z = jnp.concatenate([link_z, empty_z], axis=2)
    return jnp.stack([minus_x, plus_x, minus_y, plus_y, minus_z, plus_z], axis=-1)


def draw_aggregate(key, part):
    picked = jax.random.randint(key, (NX, NY, 2), 0, 8)
    row_x = jnp.arange(NX, dtype=jnp.int32)[:, None, None]
    row_y = jnp.arange(NY, dtype=jnp.int32)[None, :, None]
    box_x = row_x // 2
    box_y = row_y // 2
    step_x = jnp.where((picked == 4) & (row_x % 2 == 0) & (box_x > 0), -1, 0) + jnp.where((picked == 5) & (row_x % 2 == 1) & (box_x < BOXES_X - 1), 1, 0)
    step_y = jnp.where((picked == 6) & (row_y % 2 == 0) & (box_y > 0), -1, 0) + jnp.where((picked == 7) & (row_y % 2 == 1) & (box_y < BOXES_Y - 1), 1, 0)
    return ((box_x + step_x) * BOXES_Y + box_y + step_y).astype(jnp.int32)


def block_levels(own_key, shape, cuts, smallest, largest):
    factor_of = 1.0
    for position, blocks in cuts:
        draws = jax.random.uniform(jax.random.fold_in(jax.random.fold_in(own_key, 6), position), (blocks,), jnp.float32, smallest / len(cuts), largest / len(cuts))
        factor_of = factor_of * jnp.repeat(jnp.exp(draws), shape[position] // blocks).reshape((-1,) + (1,) * (len(shape) - 1 - position))
    return factor_of


def noise(stream_key, shape, scale, limit, cuts=(), held_as=jnp.bfloat16):
    level = block_levels(stream_key, shape, cuts, -0.22, 0.18) if cuts else 1.0
    drawn = jax.random.normal(stream_key, shape, jnp.float32) * scale * level
    return jnp.minimum(jnp.maximum(drawn, -limit), limit).astype(held_as)


def setup_inputs(seed: int = 0) -> dict:
    key_of = jax.random.split(jax.random.key(seed), 5)
    fine_matrix = noise(key_of[0], (NX, NY, 2, 7, B, B), B ** -0.5, 0.75, ((0, 4), (1, 8)))
    prolongator = noise(key_of[1], (NX, NY, 2, 7, B, CB), 0.35, 2.5, ((0, 4), (1, 8)))
    aggregate = draw_aggregate(jax.random.fold_in(key_of[4], 71), 0)
    face_links = draw_face_links(jax.random.fold_in(key_of[4], 71), 0)
    return {"fine_matrix": fine_matrix, "prolongator": prolongator, "aggregate": aggregate, "face_links": face_links}


def neighbour_views(extended):
    padded = jnp.pad(extended, [(0, 0), (0, 0), (1, 1)] + [(0, 0)] * (extended.ndim - 3))
    return [padded[1:-1, 1:-1, 1:3], padded[:-2, 1:-1, 1:3], padded[2:, 1:-1, 1:3],
            padded[1:-1, :-2, 1:3], padded[1:-1, 2:, 1:3], padded[1:-1, 1:-1, 0:2], padded[1:-1, 1:-1, 2:4]]


def slot_ids(aggregate_ext, face_links, first_x, first_y, boxes_y):
    neighbours = jnp.stack(neighbour_views(aggregate_ext), axis=-1)
    count_x, count_y = face_links.shape[0], face_links.shape[1]
    box_x = ((first_x + jnp.arange(count_x, dtype=jnp.int32)) // 2)[:, None, None, None]
    box_y = ((first_y + jnp.arange(count_y, dtype=jnp.int32)) // 2)[None, :, None, None]
    target_x = neighbours // boxes_y
    target_y = neighbours % boxes_y
    within = (target_x - box_x + 1) * 3 + (target_y - box_y + 1)
    present = jnp.concatenate([jnp.ones_like(face_links[..., :1]), face_links], axis=-1) == 1
    return jnp.where(present, within, -1).astype(jnp.int32)


def box_step(direction, parity_x, parity_y):
    shift_x = 0
    shift_y = 0
    if direction == 1 and parity_x == 0:
        shift_x = -1
    if direction == 2 and parity_x == 1:
        shift_x = 1
    if direction == 3 and parity_y == 0:
        shift_y = -1
    if direction == 4 and parity_y == 1:
        shift_y = 1
    return shift_x, shift_y


def image_blocks(fine_matrix, face_links, box_ext):
    views = neighbour_views(box_ext)
    count_x, count_y = fine_matrix.shape[0], fine_matrix.shape[1]
    half_x, half_y = count_x // 2, count_y // 2
    width, coarse_width = fine_matrix.shape[-1], box_ext.shape[-1]
    total = jnp.zeros((half_x, 2, half_y, 2, 2, 5, 5, width, coarse_width), jnp.float32)
    for direction in range(7):
        product = jnp.einsum('xyzpq,xyztqr->xyztpr', fine_matrix[:, :, :, direction].astype(jnp.float32),
                             views[direction].astype(jnp.float32))
        if direction > 0:
            product = product * face_links[:, :, :, direction - 1, None, None, None].astype(jnp.float32)
        product = product.reshape(half_x, 2, half_y, 2, 2, 3, 3, width, coarse_width)
        for parity_x in range(2):
            for parity_y in range(2):
                shift_x, shift_y = box_step(direction, parity_x, parity_y)
                total = total.at[:, parity_x, :, parity_y, :, 1 + shift_x:4 + shift_x, 1 + shift_y:4 + shift_y].add(
                    product[:, parity_x, :, parity_y])
    return total.astype(jnp.bfloat16).reshape(half_x, 2, half_y, 2, 2, 25, width, coarse_width)


def place_blocks(contrib):
    half_x, half_y = contrib.shape[0], contrib.shape[1]
    coarse_width = contrib.shape[-1]
    buffer = jnp.zeros((half_x + 2, half_y + 2, 7, 7, coarse_width, coarse_width), jnp.float32)
    for offset_x in range(3):
        for offset_y in range(3):
            piece = contrib[:, :, 3 * offset_x + offset_y].reshape(half_x, half_y, 5, 5, coarse_width, coarse_width)
            buffer = buffer.at[offset_x:offset_x + half_x, offset_y:offset_y + half_y,
                               2 - offset_x:7 - offset_x, 2 - offset_y:7 - offset_y].add(piece)
    return buffer


def reference(fine_matrix, prolongator, aggregate, face_links):
    boxes_y = NY // 2
    padded_agg = jnp.pad(aggregate, ((1, 1), (1, 1), (0, 0)))
    slot_table = slot_ids(padded_agg, face_links, jnp.int32(0), jnp.int32(0), boxes_y)

    def box_row(index):
        row_index = jnp.clip(index - 1, 0, NX - 1).astype(jnp.int32)
        valid = ((index >= 1) & (index <= NX)).astype(jnp.float32)
        blocks = lax.dynamic_index_in_dim(prolongator, row_index, 0, keepdims=False).astype(jnp.float32)
        table = lax.dynamic_index_in_dim(slot_table, row_index, 0, keepdims=False)
        selector = (table[..., None] == jnp.arange(9, dtype=jnp.int32)).astype(jnp.float32)
        return (jnp.einsum('yzmt,yzmpq->yztpq', selector, blocks) * valid).astype(jnp.bfloat16)

    box_rows = lax.map(box_row, jnp.arange(NX + 2, dtype=jnp.int32))

    def step_fn(window, index):
        start = (2 * index).astype(jnp.int32)
        matrix_rows = lax.dynamic_slice_in_dim(fine_matrix, start, 2, 0)
        link_rows = lax.dynamic_slice_in_dim(face_links, start, 2, 0)
        box_slab = lax.dynamic_slice_in_dim(box_rows, start, 4, 0)
        box_ext = jnp.pad(box_slab, ((0, 0), (1, 1), (0, 0), (0, 0), (0, 0), (0, 0)))
        image = image_blocks(matrix_rows, link_rows, box_ext)
        left = box_slab[1:3].reshape(1, 2, NY // 2, 2, 2, 9, B, CB)
        contrib = jnp.einsum('abcderkp,abcdeskq->acrspq', left.astype(jnp.float32), image.astype(jnp.float32))
        window = window + place_blocks(contrib)
        finished = window[0, 1:-1].astype(jnp.bfloat16)
        window = jnp.concatenate([window[1:], jnp.zeros_like(window[:1])], axis=0)
        return window, finished

    start_window = jnp.zeros((3, NY // 2 + 2, 7, 7, CB, CB), jnp.float32)
    window, finished = lax.scan(step_fn, start_window, jnp.arange(NX // 2, dtype=jnp.int32))
    last_row = window[0, 1:-1].astype(jnp.bfloat16)[None]
    return jnp.concatenate([finished[1:], last_row], axis=0)
```

```python
import functools

import jax
import jax.numpy as jnp
from jax import lax
from jax.experimental import pallas as pl
from jax.experimental.pallas import tpu as pltpu
from jax.sharding import PartitionSpec as P

B = 64
PAIR = 2 * B
BLOCK_ROWS = 7 * B
BODY = 2 * BLOCK_ROWS
VMEM_LIMIT = 48 * 1024 * 1024

FACES = [(0, 0), (-1, 0), (1, 0), (0, -1), (0, 1), (0, 0), (0, 0)]
COLUMNS = [(0, 0), (0, 1), (1, 0), (1, 1)]


def targets(px, py):
    table = []
    for dx, dy in FACES:
        ox, nx = divmod(px + dx, 2)
        oy, ny = divmod(py + dy, 2)
        table.append([(ox, oy), (ox + 2 * nx - 1, oy), (ox, oy + 2 * ny - 1)])
    return table


def box_set(px, py):
    return sorted({t for row in targets(px, py) for t in row})


def around(px, py):
    found = [((0, 0), (0, 0), (px, py))]
    for m in (2, 1) if px == 0 else (1, 2):
        ox, nx = divmod(px + FACES[m][0], 2)
        found.append(((m, m), (ox, 0), (nx, py)))
    for m in (4, 3) if py == 0 else (3, 4):
        oy, ny = divmod(py + FACES[m][1], 2)
        found.append(((m, m), (0, oy), (px, ny)))
    found.append(((6, 5), (0, 0), (px, py)))
    return found


def image_set(px, py):
    found = set()
    for _, (ox, oy), column in around(px, py):
        found |= {(ox + tx, oy + ty) for tx, ty in box_set(*column)}
    return sorted(found)


IMAGE = sorted({s for column in COLUMNS for s in image_set(*column)})
IMAGE_PAIRS = (len(IMAGE) + 1) // 2
STAR = [(0, 1), (0, -1), (0, 0), (1, 0), (-1, 0)]


def corner_of(tx, ty):
    return ((tx + 1) // 2, (ty + 1) // 2)


def blocks_of(tx, ty):
    return IMAGE if (tx, ty) in STAR else image_set(*corner_of(tx, ty))


def relay_list(ty):
    return [(tx, s) for tx in (0, -1, 1) for s in blocks_of(tx, ty)]


def coarse_list(tx):
    found = {(sx - tx, sy) for sx, sy in blocks_of(tx, 0)}
    for ty in (-1, 1):
        found |= {(sx - tx, sy - ty) for sx, sy in blocks_of(tx, ty)}
    return sorted(found)


def own_list():
    found = set(IMAGE)
    for ty in (-1, 1):
        found |= {(sx, sy - ty) for sx, sy in IMAGE}
    return sorted(found)


def low_half(shape):
    return lax.broadcasted_iota(jnp.int32, shape, len(shape) - 1) < B


def swap_halves(value):
    return pltpu.roll(value, B, value.ndim - 1)


def pair_lanes(left, right):
    return jnp.concatenate([left, right], axis=-1)


def state_of(aggregate_ref, px, py, z, own, boxes_y):
    shift = aggregate_ref[px, py, z] - own
    across_x = (shift == boxes_y) | (shift == -boxes_y)
    return jnp.where(shift == 0, 0, jnp.where(across_x, 1, 2)).astype(jnp.float32)


def fill_rows(rows, values):
    shape = (rows, PAIR)
    row = lax.broadcasted_iota(jnp.int32, shape, 0)
    half = low_half(shape)
    filled = jnp.zeros(shape, jnp.float32)
    for index, (low, high) in enumerate(values):
        filled = jnp.where(row == index, jnp.where(half, low, high), filled)
    return filled


def pack_kernel(boxes_y, place_ref, aggregate_ref, links_ref, p_ref, rows_ref, meta_ref, first_ref, second_ref):
    x = place_ref[0]
    own = x * boxes_y + place_ref[1]
    states = [
        tuple(state_of(aggregate_ref, px, py, z, own, boxes_y) for z in (0, 1)) for px, py in COLUMNS
    ]

    def link(px, py, face):
        return tuple(links_ref[px, py, z, face].astype(jnp.float32) for z in (0, 1))

    own_links = [link(px, py, face) for px, py in COLUMNS for face in range(6)]
    meta_ref[...] = fill_rows(32, states + own_links)
    for px, py in COLUMNS:
        for m in range(7):
            rows_ref[px, py, m * B : (m + 1) * B, :] = pair_lanes(p_ref[px, py, 0, m], p_ref[px, py, 1, m])
    for ref, face in ((first_ref, 1 - x % 2), (second_ref, x % 2)):
        ref[0:BLOCK_ROWS, :] = rows_ref[face, 0]
        ref[BLOCK_ROWS:BODY, :] = rows_ref[face, 1]
        face_links = [link(face, py, side) for py in (0, 1) for side in range(6)]
        ref[BODY : BODY + 16, :] = fill_rows(16, states + face_links).astype(jnp.bfloat16)


def pack_y_kernel(place_ref, links_ref, rows_ref, meta_ref, first_in, second_in, first_ref, second_ref):
    y = place_ref[1]

    def link(px, py, face):
        return tuple(links_ref[px, py, z, face].astype(jnp.float32) for z in (0, 1))

    row = lax.broadcasted_iota(jnp.int32, (16, PAIR), 0)
    from_first = first_in[BODY : BODY + 16, :].astype(jnp.float32)
    from_second = pltpu.roll(second_in[BODY : BODY + 16, :].astype(jnp.float32), 4, 0)
    corners = jnp.where(row < 4, from_first, from_second).astype(jnp.bfloat16)
    states = meta_ref[0:16, :]
    for ref, face in ((first_ref, 1 - y % 2), (second_ref, y % 2)):
        ref[0:BLOCK_ROWS, :] = rows_ref[0, face]
        ref[BLOCK_ROWS:BODY, :] = rows_ref[1, face]
        face_links = [link(px, face, side) for px in (0, 1) for side in range(6)]
        linked = fill_rows(16, [(0.0, 0.0)] * 4 + face_links)
        ref[BODY : BODY + 16, :] = jnp.where(row < 4, states, linked).astype(jnp.bfloat16)
        ref[BODY + 16 : BODY + 32, :] = corners


def pack_matrix_kernel(links_ref, a_ref, out_ref):
    for index, (px, py) in enumerate(COLUMNS):
        for z in (0, 1):
            blocks = []
            for slots, _, _ in around(px, py):
                m = slots[z]
                block = a_ref[px, py, z, m]
                if m > 0:
                    present = links_ref[px, py, z, m - 1] == 1
                    block = jnp.where(present, block, jnp.zeros_like(block))
                blocks.append(block)
            for pair in range(3):
                out_ref[index, z * B : (z + 1) * B, pair * PAIR : (pair + 1) * PAIR] = pair_lanes(
                    blocks[2 * pair], blocks[2 * pair + 1]
                )


def main_kernel(
    place_ref,
    a_ref,
    rows_ref,
    meta_ref,
    x_first,
    x_second,
    y_first,
    y_second,
    to_y_first,
    to_y_second,
    rest_ref,
    right,
    image,
    left_star,
    left_corner,
):
    x_even = place_ref[0] % 2 == 0
    y_even = place_ref[1] % 2 == 0

    def from_x(ox, rows):
        return jnp.where(x_even == (ox > 0), x_first[rows, :], x_second[rows, :])

    def from_y(oy, rows):
        return jnp.where(y_even == (oy > 0), y_first[rows, :], y_second[rows, :])

    tail = pl.ds(BODY, 16)
    tail_2 = pl.ds(BODY + 16, 16)
    own_meta = meta_ref[...]
    notes = {(0, 0): own_meta}
    for side in (-1, 1):
        notes[side, 0] = from_x(side, tail).astype(jnp.float32)
        notes[0, side] = from_y(side, tail).astype(jnp.float32)
    corner_notes = {side: from_y(side, tail_2).astype(jnp.float32) for side in (-1, 1)}

    def state_row(ox, oy, px, py):
        index = 2 * px + py
        if ox and oy:
            both = corner_notes[oy]
            first = both[index : index + 1]
            second = both[4 + index : 5 + index]
            return jnp.where(x_even == (ox > 0), first, second)
        return notes[ox, oy][index : index + 1]

    def link_row(ox, oy, px, py, face):
        if (ox, oy) == (0, 0):
            index = 4 + 6 * (2 * px + py) + face
        else:
            index = 4 + 6 * (py if ox else px) + face
        return notes[ox, oy][index : index + 1]

    def block(ox, oy, px, py, m, chunk):
        start = m * B + chunk * 16
        if (ox, oy) == (0, 0):
            return rows_ref[px, py, start : start + 16, :]
        start += (py if ox else px) * BLOCK_ROWS
        return (from_x(ox, pl.ds(start, 16)) if ox else from_y(oy, pl.ds(start, 16)))

    def box_rows(ox, oy, px, py):
        weights = []
        for m, (dx, dy) in enumerate(FACES):
            bx, nx = divmod(2 * ox + px + dx, 2)
            by, ny = divmod(2 * oy + py + dy, 2)
            state = state_row(bx, by, nx, ny)
            if m >= 5:
                state = swap_halves(state)
            rows = []
            for kind in range(3):
                weight = jnp.where(state == kind, 1.0, 0.0)
                if m > 0:
                    weight = weight * link_row(ox, oy, px, py, m - 1)
                rows.append(jnp.broadcast_to(weight, (16, PAIR)))
            weights.append(rows)
        reach = targets(px, py)
        chunks = {t: [] for t in box_set(px, py)}
        for chunk in range(4):
            values = [block(ox, oy, px, py, m, chunk).astype(jnp.float32) for m in range(7)]
            for t in chunks:
                total = None
                for m in range(7):
                    for kind in range(3):
                        if reach[m][kind] == t:
                            term = values[m] * weights[m][kind]
                            total = term if total is None else total + term
                chunks[t].append(total)
        return {t: jnp.concatenate(parts, axis=0) for t, parts in chunks.items()}

    images = {column: image_set(*column) for column in COLUMNS}
    users = {}
    for index, column in enumerate(COLUMNS):
        for place, (_, box, other) in enumerate(around(*column)):
            users.setdefault((box, other), []).append((index, column, place, box))
            reached = {(box[0] + tx, box[1] + ty) for tx, ty in box_set(*other)}
            for position, s in enumerate(images[column]):
                if s not in reached:
                    right[index, place * B : (place + 1) * B, position * PAIR : (position + 1) * PAIR] = jnp.zeros(
                        (B, PAIR), jnp.bfloat16
                    )
    for (box, other), uses in users.items():
        found = box_rows(*box, *other)
        own = COLUMNS.index(other)
        for t, value in found.items():
            rounded = value.astype(jnp.bfloat16)
            for index, column, place, _ in uses:
                position = images[column].index((box[0] + t[0], box[1] + t[1]))
                stored = swap_halves(value).astype(jnp.bfloat16) if place == 5 else rounded
                right[index, place * B : (place + 1) * B, position * PAIR : (position + 1) * PAIR] = stored
            if box == (0, 0):
                turned = value.T
                turned = pair_lanes(turned[:B], turned[B:]).astype(jnp.bfloat16)
                if t in STAR:
                    left_star[STAR.index(t) * B : (STAR.index(t) + 1) * B, own * PAIR : (own + 1) * PAIR] = turned
                else:
                    left_corner[own] = turned
    half = low_half((B, PAIR))
    for index, column in enumerate(COLUMNS):
        product = jnp.dot(a_ref[index], right[index], preferred_element_type=jnp.float32)

        def part(s, z):
            if s not in images[column]:
                return jnp.zeros((B, PAIR), jnp.float32)
            position = images[column].index(s)
            return product[z * B : (z + 1) * B, position * PAIR : (position + 1) * PAIR]

        for pair in range(IMAGE_PAIRS):
            one = IMAGE[2 * pair]
            two = IMAGE[2 * pair + 1] if 2 * pair + 1 < len(IMAGE) else None
            low = jnp.where(half, part(one, 0), swap_halves(part(two, 0)))
            high = jnp.where(half, swap_halves(part(one, 1)), part(two, 1))
            start = index * PAIR
            lanes = slice(pair * PAIR, (pair + 1) * PAIR)
            image[start : start + B, lanes] = low.astype(jnp.bfloat16)
            image[start + B : start + PAIR, lanes] = high.astype(jnp.bfloat16)
    folded_half = low_half((B // 2, PAIR))

    def fold(product):
        blocks = {}
        for pair in range(IMAGE_PAIRS):
            tile = product[:, pair * PAIR : (pair + 1) * PAIR]
            top, bottom = tile[: B // 2], tile[B // 2 :]
            blocks[IMAGE[2 * pair]] = jnp.where(folded_half, top, swap_halves(bottom))
            if 2 * pair + 1 < len(IMAGE):
                blocks[IMAGE[2 * pair + 1]] = jnp.where(folded_half, swap_halves(top), bottom)
        return blocks

    def contribution(tx, ty):
        if (tx, ty) in STAR:
            rows = STAR.index((tx, ty)) * B
            product = jnp.dot(left_star[rows : rows + B, :], image[...], preferred_element_type=jnp.float32)
        else:
            index = COLUMNS.index(corner_of(tx, ty))
            product = jnp.dot(
                left_corner[index], image[index * PAIR : (index + 1) * PAIR, :], preferred_element_type=jnp.float32
            )
        return fold(product)

    for ty in (-1, 1):
        parts = {tx: contribution(tx, ty) for tx in (0, -1, 1)}
        for position, (tx, s) in enumerate(relay_list(ty)):
            value = parts[tx][s].astype(jnp.bfloat16)
            rows = slice(position * (B // 2), (position + 1) * (B // 2))

            if ty > 0:
                goes_first = y_even
            else:
                goes_first = jnp.logical_not(y_even)

            @pl.when(goes_first)
            def _(rows=rows, value=value):
                to_y_first[rows, :] = value

            @pl.when(jnp.logical_not(goes_first))
            def _(rows=rows, value=value):
                to_y_second[rows, :] = value

    for group, tx in enumerate((0, -1, 1)):
        parts = contribution(tx, 0)
        for position, s in enumerate(IMAGE):
            rest_ref[group, position] = parts[s]


HALF = B // 2


def relay_kernel(place_ref, rest_ref, y_first, y_second, to_x_first, to_x_second, own_ref):
    x_even = place_ref[0] % 2 == 0
    y_even = place_ref[1] % 2 == 0

    def from_y(oy, tx, s):
        position = relay_list(-oy).index((tx, s))
        rows = pl.ds(position * HALF, HALF)
        value = jnp.where(y_even == (oy > 0), y_first[rows, :], y_second[rows, :]).astype(jnp.float32)
        return value * (place_ref[3] if oy > 0 else place_ref[2]).astype(jnp.float32)

    def total(tx, block):
        jx, jy = block
        terms = []
        if (jx + tx, jy) in IMAGE:
            terms.append(rest_ref[(0, -1, 1).index(tx), IMAGE.index((jx + tx, jy))])
        for oy in (-1, 1):
            s = (jx + tx, jy - oy)
            if (tx, s) in relay_list(-oy):
                terms.append(from_y(oy, tx, s))
        value = terms[0]
        for term in terms[1:]:
            value = value + term
        return value

    for tx in (-1, 1):
        goes_first = x_even if tx > 0 else jnp.logical_not(x_even)
        for position, block in enumerate(coarse_list(tx)):
            value = total(tx, block).astype(jnp.bfloat16)
            rows = slice(position * HALF, (position + 1) * HALF)

            @pl.when(goes_first)
            def _(rows=rows, value=value):
                to_x_first[rows, :] = value

            @pl.when(jnp.logical_not(goes_first))
            def _(rows=rows, value=value):
                to_x_second[rows, :] = value

    for position, block in enumerate(own_list()):
        own_ref[position] = total(0, block)


def finish_kernel(place_ref, own_ref, x_first, x_second, out_ref):
    x_even = place_ref[0] % 2 == 0
    own = own_list()
    lists = {ox: coarse_list(-ox) for ox in (-1, 1)}
    for jx in range(-3, 4):
        for jy in range(-3, 4):
            terms = []
            if (jx, jy) in own:
                terms.append(own_ref[own.index((jx, jy))])
            for ox in (-1, 1):
                if (jx, jy) in lists[ox]:
                    rows = pl.ds(lists[ox].index((jx, jy)) * HALF, HALF)
                    value = jnp.where(x_even == (ox > 0), x_first[rows, :], x_second[rows, :]).astype(jnp.float32)
                    terms.append(value * (place_ref[5] if ox > 0 else place_ref[4]).astype(jnp.float32))
            if not terms:
                out_ref[jx + 3, jy + 3] = jnp.zeros((B, B), jnp.bfloat16)
                continue
            value = terms[0]
            for term in terms[1:]:
                value = value + term
            out_ref[jx + 3, jy + 3, 0:HALF, :] = value[:, :B].astype(jnp.bfloat16)
            out_ref[jx + 3, jy + 3, HALF:B, :] = swap_halves(value)[:, :B].astype(jnp.bfloat16)


def swapped(value, axis, offset):
    count_x, count_y = lax.axis_size("sx"), lax.axis_size("sy")
    pairs = []
    for x in range(count_x):
        for y in range(count_y):
            if axis == "sx":
                partner = ((x + offset) ^ 1) - offset
                other = (partner, y) if 0 <= partner < count_x else (x, y ^ 1)
            else:
                partner = ((y + offset) ^ 1) - offset
                other = (x, partner) if 0 <= partner < count_y else (x ^ 1, y)
            pairs.append((x * count_y + y, other[0] * count_y + other[1]))
    return lax.ppermute(value, ("sx", "sy"), pairs)


SMEM = pl.BlockSpec(memory_space=pltpu.SMEM)
VMEM = pl.BlockSpec(memory_space=pltpu.VMEM)


def call(kernel, in_specs, outs, scratch=()):
    return pl.pallas_call(
        kernel,
        out_shape=[jax.ShapeDtypeStruct(shape, dtype) for shape, dtype in outs],
        in_specs=in_specs,
        out_specs=[VMEM] * len(outs),
        scratch_shapes=list(scratch),
        compiler_params=pltpu.CompilerParams(vmem_limit_bytes=VMEM_LIMIT),
    )


def per_device(fine_matrix, prolongator, aggregate, face_links):
    x, y = lax.axis_index("sx"), lax.axis_index("sy")
    count_x, count_y = lax.axis_size("sx"), lax.axis_size("sy")
    place = jnp.stack([x, y, y > 0, y < count_y - 1, x > 0, x < count_x - 1]).astype(jnp.int32)
    bf16, f32 = jnp.bfloat16, jnp.float32
    message = ((BODY + 16, PAIR), bf16)
    rows, meta, first, second = call(
        functools.partial(pack_kernel, count_y),
        [SMEM, SMEM, SMEM, VMEM],
        [((2, 2, BLOCK_ROWS, PAIR), bf16), ((32, PAIR), f32), message, message],
    )(place, aggregate, face_links, prolongator)
    x_first, x_second = swapped(first, "sx", 0), swapped(second, "sx", 1)
    (matrix,) = call(pack_matrix_kernel, [SMEM, VMEM], [((4, PAIR, 6 * B), bf16)])(face_links, fine_matrix)
    message = ((BODY + 32, PAIR), bf16)
    first, second = call(pack_y_kernel, [SMEM, SMEM, VMEM, VMEM, VMEM, VMEM], [message, message])(
        place, face_links, rows, meta, x_first, x_second
    )
    y_first, y_second = swapped(first, "sy", 0), swapped(second, "sy", 1)
    relay = ((len(relay_list(1)) * HALF, PAIR), bf16)
    first, second, rest = call(
        main_kernel,
        [SMEM] + [VMEM] * 7,
        [relay, relay, ((3, len(IMAGE), HALF, PAIR), f32)],
        [
            pltpu.VMEM((4, 6 * B, 10 * PAIR), bf16),
            pltpu.VMEM((4 * PAIR, IMAGE_PAIRS * PAIR), bf16),
            pltpu.VMEM((len(STAR) * B, 4 * PAIR), bf16),
            pltpu.VMEM((4, B, PAIR), bf16),
        ],
    )(place, matrix, rows, meta, x_first, x_second, y_first, y_second)
    y_first, y_second = swapped(first, "sy", 0), swapped(second, "sy", 1)
    sent = ((len(coarse_list(1)) * HALF, PAIR), bf16)
    first, second, own = call(
        relay_kernel, [SMEM] + [VMEM] * 3, [sent, sent, ((len(own_list()), HALF, PAIR), f32)]
    )(place, rest, y_first, y_second)
    x_first, x_second = swapped(first, "sx", 0), swapped(second, "sx", 1)
    (out,) = call(finish_kernel, [SMEM] + [VMEM] * 3, [((7, 7, B, B), bf16)])(place, own, x_first, x_second)
    return out[None, None]


def solution(mesh):
    return jax.shard_map(
        per_device,
        mesh=mesh,
        in_specs=(
            P("sx", "sy", None, None, None, None),
            P("sx", "sy", None, None, None, None),
            P("sx", "sy", None),
            P("sx", "sy", None, None),
        ),
        out_specs=P("sx", "sy", None, None, None, None),
        check_vma=False,
    )
```

```python
import functools

import jax
import jax.numpy as jnp
from jax import lax
from jax.experimental import pallas as pl
from jax.experimental.pallas import tpu as pltpu
from jax.sharding import PartitionSpec as P


B = 64
HALF = B // 2
PAIR = 2 * B
BLOCK_ROWS = 7 * B
BODY = 2 * BLOCK_ROWS
TAIL = 16
VMEM_LIMIT = 48 * 1024 * 1024

FACES = [(0, 0), (-1, 0), (1, 0), (0, -1), (0, 1), (0, 0), (0, 0)]
COLUMNS = [(0, 0), (0, 1), (1, 0), (1, 1)]
SIDES_X = (0, 2, 1, 3, 4, 5, 6)
SIDES_Y = (0, 1, 2, 4, 3, 5, 6)


def targets(px, py):
    table = []
    for dx, dy in FACES:
        ox, nx = divmod(px + dx, 2)
        oy, ny = divmod(py + dy, 2)
        table.append([(ox, oy), (ox + 2 * nx - 1, oy), (ox, oy + 2 * ny - 1)])
    return table


def box_set(px, py):
    return sorted({t for row in targets(px, py) for t in row})


def around(px, py):
    found = [((0, 0), (0, 0), (px, py))]
    for m in (2, 1) if px == 0 else (1, 2):
        ox, nx = divmod(px + FACES[m][0], 2)
        found.append(((m, m), (ox, 0), (nx, py)))
    for m in (4, 3) if py == 0 else (3, 4):
        oy, ny = divmod(py + FACES[m][1], 2)
        found.append(((m, m), (0, oy), (px, ny)))
    found.append(((6, 5), (0, 0), (px, py)))
    return found


def image_set(px, py):
    found = set()
    for _, (ox, oy), column in around(px, py):
        found |= {(ox + tx, oy + ty) for tx, ty in box_set(*column)}
    return sorted(found)


IMAGE = sorted({s for column in COLUMNS for s in image_set(*column)})
IMAGE_PAIRS = (len(IMAGE) + 1) // 2
STAR = [(0, 1), (0, -1), (0, 0), (1, 0), (-1, 0)]


def column_of(tx, ty):
    return ((tx + 1) // 2, (ty + 1) // 2)


def blocks_of(tx, ty):
    return IMAGE if (tx, ty) in STAR else image_set(*column_of(tx, ty))


TO_Y_FIRST = [((tx, 1), s) for tx in (0, -1, 1) for s in blocks_of(tx, 1)]
TO_Y_SECOND = [((0, -1), s) for s in blocks_of(0, -1)]
TO_C_FIRST = [((1, -1), s) for s in blocks_of(1, -1)]
TO_C_SECOND = [((-1, -1), s) for s in blocks_of(-1, -1)]


def relayed(tx):
    return {(s[0], 1 - s[1]): row for row, (t, s) in enumerate(TO_Y_FIRST) if t[0] == tx}


TO_X = {tx: sorted(set(IMAGE) | set(relayed(tx))) for tx in (1, -1)}
OWN = sorted(set(IMAGE) | set(relayed(0)))
STENCIL = [(jx, jy) for jx in range(-3, 4) for jy in range(-3, 4) if abs(jx) + abs(jy) <= 3]


def low_half(shape):
    return lax.broadcasted_iota(jnp.int32, shape, len(shape) - 1) < B


def swap_halves(value):
    return pltpu.roll(value, B, value.ndim - 1)


def pair_lanes(left, right):
    return jnp.concatenate([left, right], axis=-1)


def mirrored():
    return lax.axis_index("sx") % 2, lax.axis_index("sy") % 2


def slot_here(m, odd_x, odd_y):
    if m in (1, 2):
        return jnp.where(odd_x == 1, 3 - m, m)
    if m in (3, 4):
        return jnp.where(odd_y == 1, 7 - m, m)
    return m


def fill_rows(rows, values):
    shape = (rows, PAIR)
    row = lax.broadcasted_iota(jnp.int32, shape, 0)
    half = low_half(shape)
    filled = jnp.zeros(shape, jnp.float32)
    for index, (low, high) in enumerate(values):
        filled = jnp.where(row == index, jnp.where(half, low, high), filled)
    return filled


def pack_kernel(
    boxes_y,
    aggregate_hbm,
    links_hbm,
    p_hbm,
    rows_ref,
    meta_ref,
    x_first,
    x_second,
    y_first,
    y_second,
    p_ref,
    aggregate_ref,
    links_ref,
    p_sems,
    sems,
):
    odd_x, odd_y = mirrored()
    own = lax.axis_index("sx") * boxes_y + lax.axis_index("sy")
    place = {(px, py): (px ^ odd_x, py ^ odd_y) for px, py in COLUMNS}
    copies = [
        pltpu.make_async_copy(p_hbm.at[place[column]], p_ref.at[index], p_sems.at[index])
        for index, column in enumerate(COLUMNS)
    ]
    small = [
        pltpu.make_async_copy(aggregate_hbm, aggregate_ref, sems.at[0]),
        pltpu.make_async_copy(links_hbm, links_ref, sems.at[1]),
    ]
    for copy in small + copies:
        copy.start()
    for copy in small:
        copy.wait()

    def state(column, z):
        shift = aggregate_ref[place[column] + (z,)] - own
        across_x = (shift == boxes_y) | (shift == -boxes_y)
        return jnp.where(shift == 0, 0, jnp.where(across_x, 1, 2)).astype(jnp.float32)

    def link(column, m):
        face = slot_here(m, odd_x, odd_y) - 1
        return tuple(links_ref[place[column] + (z, face)].astype(jnp.float32) for z in (0, 1))

    states = [tuple(state(column, z) for z in (0, 1)) for column in COLUMNS]
    links = {column: [link(column, m) for m in range(1, 7)] for column in COLUMNS}
    meta_ref[...] = fill_rows(32, states + sum((links[column] for column in COLUMNS), []))
    messages = (
        (x_first, ((1, 0), (1, 1))),
        (x_second, ((0, 0), (0, 1))),
        (y_first, ((0, 1), (1, 1))),
        (y_second, ((0, 0), (1, 0))),
    )
    for ref, columns in messages:
        tail = fill_rows(TAIL, states + links[columns[0]] + links[columns[1]])
        ref[BODY : BODY + TAIL, :] = tail.astype(jnp.bfloat16)
    for index, column in enumerate(COLUMNS):
        copies[index].wait()
        for m in range(7):
            slot = slot_here(m, odd_x, odd_y)
            packed = pair_lanes(p_ref[index, 0, slot], p_ref[index, 1, slot])
            rows_ref[index, m * B : (m + 1) * B, :] = packed
            for ref, columns in messages:
                if column in columns:
                    start = columns.index(column) * BLOCK_ROWS + m * B
                    ref[start : start + B, :] = packed


def pack_matrix_kernel(links_ref, a_ref, out_ref):
    odd_x, odd_y = mirrored()
    for index, (px, py) in enumerate(COLUMNS):
        place = (px ^ odd_x, py ^ odd_y)
        for z in (0, 1):
            blocks = []
            for slots, _, _ in around(px, py):
                slot = slot_here(slots[z], odd_x, odd_y)
                block = a_ref[place + (z, slot)]
                if slots[z] > 0:
                    present = links_ref[place + (z, slot - 1)] == 1
                    block = jnp.where(present, block, jnp.zeros_like(block))
                blocks.append(block)
            for pair in range(3):
                out_ref[index, z * B : (z + 1) * B, pair * PAIR : (pair + 1) * PAIR] = pair_lanes(
                    blocks[2 * pair], blocks[2 * pair + 1]
                )


def main_kernel(
    a_ref,
    rows_ref,
    meta_ref,
    x_first,
    x_second,
    y_first,
    y_second,
    c_first,
    c_second,
    to_y_first,
    to_y_second,
    to_c_first,
    to_c_second,
    rest_ref,
    right,
    image,
    left_star,
    left_corner,
):
    from_x = {1: x_first, -1: x_second}
    from_y = {1: y_first, -1: y_second}
    notes = {(0, 0): meta_ref[...]}
    corner_notes = {}
    for side in (-1, 1):
        notes[side, 0] = from_x[side][BODY : BODY + TAIL, :].astype(jnp.float32)
        notes[0, side] = from_y[side][BODY : BODY + TAIL, :].astype(jnp.float32)
    for ref, oy in ((c_first, 1), (c_second, -1)):
        corner_notes[1, oy] = ref[0:TAIL, :].astype(jnp.float32)
        corner_notes[-1, oy] = ref[TAIL : 2 * TAIL, :].astype(jnp.float32)

    def there(ox, oy, px, py):
        return (1 - px if ox else px, 1 - py if oy else py)

    def slot_there(ox, oy, m):
        m = SIDES_X[m] if ox else m
        return SIDES_Y[m] if oy else m

    def state_row(ox, oy, px, py):
        index = COLUMNS.index(there(ox, oy, px, py))
        note = corner_notes[ox, oy] if ox and oy else notes[ox, oy]
        return note[index : index + 1]

    def link_row(ox, oy, px, py, m):
        if (ox, oy) == (0, 0):
            index = 6 * COLUMNS.index((px, py))
        else:
            index = 6 * (py if ox else px)
        index += 4 + slot_there(ox, oy, m) - 1
        return notes[ox, oy][index : index + 1]

    def block(ox, oy, px, py, m, chunk):
        start = slot_there(ox, oy, m) * B + chunk * 16
        if (ox, oy) == (0, 0):
            return rows_ref[COLUMNS.index((px, py)), start : start + 16, :]
        start += (py if ox else px) * BLOCK_ROWS
        ref = from_x[ox] if ox else from_y[oy]
        return ref[start : start + 16, :]

    def box_rows(ox, oy, px, py):
        weights = []
        for m, (dx, dy) in enumerate(FACES):
            bx, nx = divmod(2 * ox + px + dx, 2)
            by, ny = divmod(2 * oy + py + dy, 2)
            state = state_row(bx, by, nx, ny)
            if m >= 5:
                state = swap_halves(state)
            rows = []
            for kind in range(3):
                weight = jnp.where(state == kind, 1.0, 0.0)
                if m > 0:
                    weight = weight * link_row(ox, oy, px, py, m)
                rows.append(jnp.broadcast_to(weight, (16, PAIR)))
            weights.append(rows)
        reach = targets(px, py)
        chunks = {t: [] for t in box_set(px, py)}
        for chunk in range(4):
            values = [block(ox, oy, px, py, m, chunk).astype(jnp.float32) for m in range(7)]
            for t in chunks:
                total = None
                for m in range(7):
                    for kind in range(3):
                        if reach[m][kind] == t:
                            term = values[m] * weights[m][kind]
                            total = term if total is None else total + term
                chunks[t].append(total)
        return {t: jnp.concatenate(parts, axis=0) for t, parts in chunks.items()}

    images = {column: image_set(*column) for column in COLUMNS}
    users = {}
    for index, column in enumerate(COLUMNS):
        for place, (_, box, other) in enumerate(around(*column)):
            users.setdefault((box, other), []).append((index, column, place))
            reached = {(box[0] + tx, box[1] + ty) for tx, ty in box_set(*other)}
            for position, s in enumerate(images[column]):
                if s not in reached:
                    right[index, place * B : (place + 1) * B, position * PAIR : (position + 1) * PAIR] = jnp.zeros(
                        (B, PAIR), jnp.bfloat16
                    )
    for (box, other), uses in users.items():
        found = box_rows(*box, *other)
        own = COLUMNS.index(other)
        for t, value in found.items():
            rounded = value.astype(jnp.bfloat16)
            for index, column, place in uses:
                position = images[column].index((box[0] + t[0], box[1] + t[1]))
                stored = swap_halves(value).astype(jnp.bfloat16) if place == 5 else rounded
                right[index, place * B : (place + 1) * B, position * PAIR : (position + 1) * PAIR] = stored
            if box == (0, 0):
                turned = value.T
                turned = pair_lanes(turned[:B], turned[B:]).astype(jnp.bfloat16)
                if t in STAR:
                    left_star[STAR.index(t) * B : (STAR.index(t) + 1) * B, own * PAIR : (own + 1) * PAIR] = turned
                else:
                    left_corner[own] = turned
    half = low_half((B, PAIR))
    for index, column in enumerate(COLUMNS):
        product = jnp.dot(a_ref[index], right[index], preferred_element_type=jnp.float32)

        def part(s, z):
            if s not in images[column]:
                return jnp.zeros((B, PAIR), jnp.float32)
            position = images[column].index(s)
            return product[z * B : (z + 1) * B, position * PAIR : (position + 1) * PAIR]

        for pair in range(IMAGE_PAIRS):
            one = IMAGE[2 * pair]
            two = IMAGE[2 * pair + 1] if 2 * pair + 1 < len(IMAGE) else None
            low = jnp.where(half, part(one, 0), swap_halves(part(two, 0)))
            high = jnp.where(half, swap_halves(part(one, 1)), part(two, 1))
            start = index * PAIR
            lanes = slice(pair * PAIR, (pair + 1) * PAIR)
            image[start : start + B, lanes] = low.astype(jnp.bfloat16)
            image[start + B : start + PAIR, lanes] = high.astype(jnp.bfloat16)
    folded_half = low_half((HALF, PAIR))

    def fold(product):
        blocks = {}
        for pair in range(IMAGE_PAIRS):
            tile = product[:, pair * PAIR : (pair + 1) * PAIR]
            top, bottom = tile[:HALF], tile[HALF:]
            blocks[IMAGE[2 * pair]] = jnp.where(folded_half, top, swap_halves(bottom))
            if 2 * pair + 1 < len(IMAGE):
                blocks[IMAGE[2 * pair + 1]] = jnp.where(folded_half, swap_halves(top), bottom)
        return blocks

    def contribution(t):
        if t in STAR:
            rows = STAR.index(t) * B
            product = jnp.dot(left_star[rows : rows + B, :], image[...], preferred_element_type=jnp.float32)
        else:
            index = COLUMNS.index(column_of(*t))
            product = jnp.dot(
                left_corner[index], image[index * PAIR : (index + 1) * PAIR, :], preferred_element_type=jnp.float32
            )
        return fold(product)

    for ref, sent in (
        (to_y_first, TO_Y_FIRST),
        (to_y_second, TO_Y_SECOND),
        (to_c_first, TO_C_FIRST),
        (to_c_second, TO_C_SECOND),
    ):
        parts = {t: contribution(t) for t in sorted({t for t, _ in sent})}
        for row, (t, s) in enumerate(sent):
            ref[row * HALF : (row + 1) * HALF, :] = parts[t][s].astype(jnp.bfloat16)
    for group, tx in enumerate((0, -1, 1)):
        parts = contribution((tx, 0))
        for position, s in enumerate(IMAGE):
            rest_ref[group, position] = parts[s]


def message_block(ref, row):
    return ref[row * HALF : (row + 1) * HALF, :].astype(jnp.float32)


def relay_kernel(rest_ref, y_first, x_first, x_second):
    for ref, tx in ((x_first, 1), (x_second, -1)):
        arrived = relayed(tx)
        for row, s in enumerate(TO_X[tx]):
            value = None
            if s in IMAGE:
                value = rest_ref[(0, -1, 1).index(tx), IMAGE.index(s)]
            if s in arrived:
                more = message_block(y_first, arrived[s])
                value = more if value is None else value + more
            ref[row * HALF : (row + 1) * HALF, :] = value.astype(jnp.bfloat16)


def own_kernel(rest_ref, y_first, own_ref, out_hbm, zeros, sems):
    zeros[...] = jnp.zeros(zeros.shape, zeros.dtype)
    copies = []
    for jx in range(-3, 4):
        width = abs(jx)
        if width:
            for start in (0, 7 - width):
                copies.append(
                    pltpu.make_async_copy(
                        zeros.at[pl.ds(0, width)], out_hbm.at[jx + 3, pl.ds(start, width)], sems.at[len(copies)]
                    )
                )
    for copy in copies:
        copy.start()
    arrived = relayed(0)
    for position, s in enumerate(OWN):
        value = None
        if s in IMAGE:
            value = rest_ref[0, IMAGE.index(s)]
        if s in arrived:
            more = message_block(y_first, arrived[s])
            value = more if value is None else value + more
        own_ref[position] = value
    for copy in copies:
        copy.wait()


def finish_kernel(own_ref, y_second, c_first, c_second, x_first, x_second, _, out_hbm, rows, sems):
    odd_x, odd_y = mirrored()
    x, y = lax.axis_index("sx"), lax.axis_index("sy")
    has_x = ((x > 0) & (x < lax.axis_size("sx") - 1)).astype(jnp.float32)
    has_y = ((y > 0) & (y < lax.axis_size("sy") - 1)).astype(jnp.float32)
    terms = {block: [] for block in STENCIL}
    for position, block in enumerate(OWN):
        terms[block].append((own_ref, position, None))
    for row, s in enumerate(TO_X[1]):
        terms[1 - s[0], s[1]].append((x_first, row, None))
    for row, s in enumerate(TO_X[-1]):
        terms[-1 - s[0], s[1]].append((x_second, row, has_x))
    for row, (_, s) in enumerate(TO_Y_SECOND):
        terms[s[0], -1 - s[1]].append((y_second, row, has_y))
    for row, (_, s) in enumerate(TO_C_FIRST):
        terms[1 - s[0], -1 - s[1]].append((c_first, row, has_y))
    for row, (_, s) in enumerate(TO_C_SECOND):
        terms[-1 - s[0], -1 - s[1]].append((c_second, row, has_x * has_y))
    copies = []
    for jx in (0, 1, -1, 2, -2, 3, -3):
        row_here = jnp.where(odd_x == 1, 3 - jx, 3 + jx)
        reach = 3 - abs(jx)
        for jy in range(-reach, reach + 1):
            value = None
            for ref, row, flag in terms[jx, jy]:
                more = ref[row] if ref is own_ref else message_block(ref, row)
                if flag is not None:
                    more = more * flag
                value = more if value is None else value + more
            column_here = jnp.where(odd_y == 1, 3 - jy, 3 + jy)
            rows[jx + 3, column_here, 0:HALF, :] = value[:, :B].astype(jnp.bfloat16)
            rows[jx + 3, column_here, HALF:B, :] = swap_halves(value)[:, :B].astype(jnp.bfloat16)
        span = pl.ds(3 - reach, 2 * reach + 1)
        copy = pltpu.make_async_copy(rows.at[jx + 3, span], out_hbm.at[row_here, span], sems.at[jx + 3])
        copy.start()
        copies.append(copy)
    for copy in copies:
        copy.wait()


def swapped(value, move_x, move_y):
    count_x, count_y = lax.axis_size("sx"), lax.axis_size("sy")

    def partner(index, move, count):
        if move == 0:
            return index
        found = index ^ 1 if move == 1 else ((index + 1) ^ 1) - 1
        return found if 0 <= found < count else None

    pairs = []
    for x in range(count_x):
        for y in range(count_y):
            to_x, to_y = partner(x, move_x, count_x), partner(y, move_y, count_y)
            if to_x is None and to_y is None:
                to_x, to_y = x, count_y - 1 - y
            elif to_x is None:
                to_x, to_y = x, (y ^ 1 if move_y == 0 else to_y)
            elif to_y is None:
                to_x, to_y = (x ^ 1 if move_x == 0 else to_x), y
            pairs.append((x * count_y + y, to_x * count_y + to_y))
    return lax.ppermute(value, ("sx", "sy"), pairs)


SMEM = pl.BlockSpec(memory_space=pltpu.SMEM)
VMEM = pl.BlockSpec(memory_space=pltpu.VMEM)
HBM = pl.BlockSpec(memory_space=pl.ANY)


def call(kernel, in_specs, outs, scratch=(), out_specs=None, aliases=None):
    return pl.pallas_call(
        kernel,
        out_shape=[jax.ShapeDtypeStruct(shape, dtype) for shape, dtype in outs],
        in_specs=in_specs,
        out_specs=out_specs or [VMEM] * len(outs),
        scratch_shapes=list(scratch),
        input_output_aliases=aliases or {},
        compiler_params=pltpu.CompilerParams(vmem_limit_bytes=VMEM_LIMIT),
    )


def per_device(fine_matrix, prolongator, aggregate, face_links):
    bf16, f32 = jnp.bfloat16, jnp.float32
    message = ((BODY + TAIL, PAIR), bf16)
    rows, meta, x_first, x_second, y_first, y_second = call(
        functools.partial(pack_kernel, lax.axis_size("sy")),
        [HBM, HBM, HBM],
        [((4, BLOCK_ROWS, PAIR), bf16), ((32, PAIR), f32), message, message, message, message],
        [
            pltpu.VMEM((4, 2, 7, B, B), bf16),
            pltpu.SMEM((2, 2, 2), jnp.int32),
            pltpu.SMEM((2, 2, 2, 6), jnp.int32),
            pltpu.SemaphoreType.DMA((4,)),
            pltpu.SemaphoreType.DMA((2,)),
        ],
    )(aggregate, face_links, prolongator)
    x_first, x_second = swapped(x_first, 1, 0), swapped(x_second, 2, 0)
    y_first, y_second = swapped(y_first, 0, 1), swapped(y_second, 0, 2)
    notes = jnp.concatenate([x_first[BODY:], x_second[BODY:]], axis=0)
    c_first, c_second = swapped(notes, 0, 1), swapped(notes, 0, 2)
    (matrix,) = call(pack_matrix_kernel, [SMEM, VMEM], [((4, PAIR, 6 * B), bf16)])(face_links, fine_matrix)

    def sent(blocks):
        return ((len(blocks) * HALF, PAIR), bf16)

    y_first, y_second, c_first, c_second, rest = call(
        main_kernel,
        [VMEM] * 9,
        [
            sent(TO_Y_FIRST),
            sent(TO_Y_SECOND),
            sent(TO_C_FIRST),
            sent(TO_C_SECOND),
            ((3, len(IMAGE), HALF, PAIR), f32),
        ],
        [
            pltpu.VMEM((4, 6 * B, 10 * PAIR), bf16),
            pltpu.VMEM((4 * PAIR, IMAGE_PAIRS * PAIR), bf16),
            pltpu.VMEM((len(STAR) * B, 4 * PAIR), bf16),
            pltpu.VMEM((4, B, PAIR), bf16),
        ],
    )(matrix, rows, meta, x_first, x_second, y_first, y_second, c_first, c_second)
    y_second = swapped(y_second, 0, 2)
    c_first, c_second = swapped(c_first, 1, 2), swapped(c_second, 2, 2)
    y_first = swapped(y_first, 0, 1)
    x_first, x_second = call(relay_kernel, [VMEM] * 2, [sent(TO_X[1]), sent(TO_X[-1])])(rest, y_first)
    x_first, x_second = swapped(x_first, 1, 0), swapped(x_second, 2, 0)
    whole = ((7, 7, B, B), bf16)
    own, out = call(
        own_kernel,
        [VMEM] * 2,
        [((len(OWN), HALF, PAIR), f32), whole],
        [pltpu.VMEM((3, B, B), bf16), pltpu.SemaphoreType.DMA((12,))],
        [VMEM, HBM],
    )(rest, y_first)
    (out,) = call(
        finish_kernel,
        [VMEM] * 6 + [HBM],
        [whole],
        [pltpu.VMEM((7, 7, B, B), bf16), pltpu.SemaphoreType.DMA((7,))],
        [HBM],
        {6: 0},
    )(own, y_second, c_first, c_second, x_first, x_second, out)
    return out[None, None]


def solution(mesh):
    return jax.shard_map(
        per_device,
        mesh=mesh,
        in_specs=(
            P("sx", "sy", None, None, None, None),
            P("sx", "sy", None, None, None, None),
            P("sx", "sy", None),
            P("sx", "sy", None, None),
        ),
        out_specs=P("sx", "sy", None, None, None, None),
        check_vma=False,
    )
```

```python
import functools

import jax
import jax.numpy as jnp
from jax import lax
from jax.experimental import pallas as pl
from jax.experimental.pallas import tpu as pltpu
from jax.sharding import PartitionSpec as P


B = 64
HALF = B // 2
PAIR = 2 * B
SLOTS = 6
BLOCK_ROWS = SLOTS * B
BODY = 2 * BLOCK_ROWS
TAIL = 16
VMEM_LIMIT = 48 * 1024 * 1024

FACES = [(0, 0), (-1, 0), (1, 0), (0, -1), (0, 1), (0, 0)]
COLUMNS = [(0, 0), (0, 1), (1, 0), (1, 1)]
SIDES_X = (0, 2, 1, 3, 4, 5)
SIDES_Y = (0, 1, 2, 4, 3, 5)


def targets(px, py):
    table = []
    for dx, dy in FACES:
        ox, nx = divmod(px + dx, 2)
        oy, ny = divmod(py + dy, 2)
        table.append([(ox, oy), (ox + 2 * nx - 1, oy), (ox, oy + 2 * ny - 1)])
    return table


def box_set(px, py):
    return sorted({t for row in targets(px, py) for t in row})


def around(px, py):
    found = [(0, (0, 0), (px, py))]
    for m in (2, 1) if px == 0 else (1, 2):
        ox, nx = divmod(px + FACES[m][0], 2)
        found.append((m, (ox, 0), (nx, py)))
    for m in (4, 3) if py == 0 else (3, 4):
        oy, ny = divmod(py + FACES[m][1], 2)
        found.append((m, (0, oy), (px, ny)))
    found.append((5, (0, 0), (px, py)))
    return found


def image_set(px, py):
    found = set()
    for _, (ox, oy), column in around(px, py):
        found |= {(ox + tx, oy + ty) for tx, ty in box_set(*column)}
    return sorted(found)


IMAGE = sorted({s for column in COLUMNS for s in image_set(*column)})
IMAGE_PAIRS = (len(IMAGE) + 1) // 2
STAR = [(0, 1), (0, -1), (0, 0), (1, 0), (-1, 0)]


def column_of(tx, ty):
    return ((tx + 1) // 2, (ty + 1) // 2)


def blocks_of(tx, ty):
    return IMAGE if (tx, ty) in STAR else image_set(*column_of(tx, ty))


TO_Y_FIRST = [((tx, 1), s) for tx in (0, -1, 1) for s in blocks_of(tx, 1)]
TO_Y_SECOND = [((0, -1), s) for s in blocks_of(0, -1)]
TO_C_FIRST = [((1, -1), s) for s in blocks_of(1, -1)]
TO_C_SECOND = [((-1, -1), s) for s in blocks_of(-1, -1)]


def relayed(tx):
    return {(s[0], 1 - s[1]): row for row, (t, s) in enumerate(TO_Y_FIRST) if t[0] == tx}


TO_X = {tx: sorted(set(IMAGE) | set(relayed(tx))) for tx in (1, -1)}
STENCIL = [(jx, jy) for jx in range(-3, 4) for jy in range(-3, 4) if abs(jx) + abs(jy) <= 3]
OWN = sorted(
    set(IMAGE)
    | set(relayed(0))
    | {(s[0], -1 - s[1]) for _, s in TO_Y_SECOND}
    | {(1 - s[0], -1 - s[1]) for _, s in TO_C_FIRST}
    | {(-1 - s[0], -1 - s[1]) for _, s in TO_C_SECOND}
)


def low_half(shape):
    return lax.broadcasted_iota(jnp.int32, shape, len(shape) - 1) < B


def swap_halves(value):
    return pltpu.roll(value, B, value.ndim - 1)


def pair_lanes(left, right):
    return jnp.concatenate([left, right], axis=-1)


def mirrored():
    return lax.axis_index("sx") % 2, lax.axis_index("sy") % 2


def slot_here(m, z, odd_x, odd_y):
    if m in (1, 2):
        return jnp.where(odd_x == 1, 3 - m, m)
    if m in (3, 4):
        return jnp.where(odd_y == 1, 7 - m, m)
    return 6 - z if m == 5 else m


def fill_rows(rows, values):
    shape = (rows, PAIR)
    row = lax.broadcasted_iota(jnp.int32, shape, 0)
    half = low_half(shape)
    filled = jnp.zeros(shape, jnp.float32)
    for index, (low, high) in enumerate(values):
        filled = jnp.where(row == index, jnp.where(half, low, high), filled)
    return filled


def pack_kernel(
    boxes_y,
    aggregate_hbm,
    links_hbm,
    p_hbm,
    rows_ref,
    meta_ref,
    x_first,
    x_second,
    y_first,
    y_second,
    p_ref,
    aggregate_ref,
    links_ref,
    p_sems,
    sems,
):
    odd_x, odd_y = mirrored()
    own = lax.axis_index("sx") * boxes_y + lax.axis_index("sy")
    place = {(px, py): (px ^ odd_x, py ^ odd_y) for px, py in COLUMNS}
    copies = [
        pltpu.make_async_copy(p_hbm.at[place[column]], p_ref.at[index], p_sems.at[index])
        for index, column in enumerate(COLUMNS)
    ]
    small = [
        pltpu.make_async_copy(aggregate_hbm, aggregate_ref, sems.at[0]),
        pltpu.make_async_copy(links_hbm, links_ref, sems.at[1]),
    ]
    for copy in small + copies:
        copy.start()
    for copy in small:
        copy.wait()

    def state(column, z):
        shift = aggregate_ref[place[column] + (z,)] - own
        across_x = (shift == boxes_y) | (shift == -boxes_y)
        return jnp.where(shift == 0, 0, jnp.where(across_x, 1, 2)).astype(jnp.float32)

    def link(column, m):
        faces = [slot_here(m, z, odd_x, odd_y) - 1 for z in (0, 1)]
        return tuple(links_ref[place[column] + (z, faces[z])].astype(jnp.float32) for z in (0, 1))

    states = [tuple(state(column, z) for z in (0, 1)) for column in COLUMNS]
    links = {column: [link(column, m) for m in range(1, SLOTS)] for column in COLUMNS}
    meta_ref[...] = fill_rows(32, states + sum((links[column] for column in COLUMNS), []))
    messages = (
        (x_first, ((1, 0), (1, 1))),
        (x_second, ((0, 0), (0, 1))),
        (y_first, ((0, 1), (1, 1))),
        (y_second, ((0, 0), (1, 0))),
    )
    for ref, columns in messages:
        tail = fill_rows(TAIL, states + links[columns[0]] + links[columns[1]])
        ref[BODY : BODY + TAIL, :] = tail.astype(jnp.bfloat16)
    for index, column in enumerate(COLUMNS):
        copies[index].wait()
        for m in range(SLOTS):
            packed = pair_lanes(*(p_ref[index, z, slot_here(m, z, odd_x, odd_y)] for z in (0, 1)))
            rows_ref[index, m * B : (m + 1) * B, :] = packed
            for ref, columns in messages:
                if column in columns:
                    start = columns.index(column) * BLOCK_ROWS + m * B
                    ref[start : start + B, :] = packed


def pack_matrix_kernel(links_ref, a_ref, out_ref):
    odd_x, odd_y = mirrored()
    for index, (px, py) in enumerate(COLUMNS):
        place = (px ^ odd_x, py ^ odd_y)
        for z in (0, 1):
            blocks = []
            for m, _, _ in around(px, py):
                slot = slot_here(m, z, odd_x, odd_y)
                block = a_ref[place + (z, slot)]
                if m > 0:
                    present = links_ref[place + (z, slot - 1)] == 1
                    block = jnp.where(present, block, jnp.zeros_like(block))
                blocks.append(block)
            for pair in range(3):
                out_ref[index, z * B : (z + 1) * B, pair * PAIR : (pair + 1) * PAIR] = pair_lanes(
                    blocks[2 * pair], blocks[2 * pair + 1]
                )


def main_kernel(
    a_ref,
    rows_ref,
    meta_ref,
    x_first,
    x_second,
    y_first,
    y_second,
    c_first,
    c_second,
    to_y_first,
    to_y_second,
    to_c_first,
    to_c_second,
    rest_ref,
    right,
    image,
    left_star,
    left_corner,
):
    from_x = {1: x_first, -1: x_second}
    from_y = {1: y_first, -1: y_second}
    notes = {(0, 0): meta_ref[...]}
    corner_notes = {}
    for side in (-1, 1):
        notes[side, 0] = from_x[side][BODY : BODY + TAIL, :].astype(jnp.float32)
        notes[0, side] = from_y[side][BODY : BODY + TAIL, :].astype(jnp.float32)
    for ref, oy in ((c_first, 1), (c_second, -1)):
        corner_notes[1, oy] = ref[0:TAIL, :].astype(jnp.float32)
        corner_notes[-1, oy] = ref[TAIL : 2 * TAIL, :].astype(jnp.float32)

    def there(ox, oy, px, py):
        return (1 - px if ox else px, 1 - py if oy else py)

    def slot_there(ox, oy, m):
        m = SIDES_X[m] if ox else m
        return SIDES_Y[m] if oy else m

    def state_row(ox, oy, px, py):
        index = COLUMNS.index(there(ox, oy, px, py))
        note = corner_notes[ox, oy] if ox and oy else notes[ox, oy]
        return note[index : index + 1]

    def link_row(ox, oy, px, py, m):
        if (ox, oy) == (0, 0):
            index = (SLOTS - 1) * COLUMNS.index((px, py))
        else:
            index = (SLOTS - 1) * (py if ox else px)
        index += 4 + slot_there(ox, oy, m) - 1
        return notes[ox, oy][index : index + 1]

    def block(ox, oy, px, py, m, chunk):
        start = slot_there(ox, oy, m) * B + chunk * 16
        if (ox, oy) == (0, 0):
            return rows_ref[COLUMNS.index((px, py)), start : start + 16, :]
        start += (py if ox else px) * BLOCK_ROWS
        ref = from_x[ox] if ox else from_y[oy]
        return ref[start : start + 16, :]

    def box_rows(ox, oy, px, py):
        weights = []
        for m, (dx, dy) in enumerate(FACES):
            bx, nx = divmod(2 * ox + px + dx, 2)
            by, ny = divmod(2 * oy + py + dy, 2)
            state = state_row(bx, by, nx, ny)
            if m == 5:
                state = swap_halves(state)
            rows = []
            for kind in range(3):
                weight = jnp.where(state == kind, 1.0, 0.0)
                if m > 0:
                    weight = weight * link_row(ox, oy, px, py, m)
                rows.append(jnp.broadcast_to(weight, (16, PAIR)))
            weights.append(rows)
        reach = targets(px, py)
        chunks = {t: [] for t in box_set(px, py)}
        for chunk in range(4):
            values = [block(ox, oy, px, py, m, chunk).astype(jnp.float32) for m in range(SLOTS)]
            for t in chunks:
                total = None
                for m in range(SLOTS):
                    for kind in range(3):
                        if reach[m][kind] == t:
                            term = values[m] * weights[m][kind]
                            total = term if total is None else total + term
                chunks[t].append(total)
        return {t: jnp.concatenate(parts, axis=0) for t, parts in chunks.items()}

    images = {column: image_set(*column) for column in COLUMNS}
    users = {}
    for index, column in enumerate(COLUMNS):
        for place, (_, box, other) in enumerate(around(*column)):
            users.setdefault((box, other), []).append((index, column, place))
            reached = {(box[0] + tx, box[1] + ty) for tx, ty in box_set(*other)}
            for position, s in enumerate(images[column]):
                if s not in reached:
                    right[index, place * B : (place + 1) * B, position * PAIR : (position + 1) * PAIR] = jnp.zeros(
                        (B, PAIR), jnp.bfloat16
                    )
    for (box, other), uses in users.items():
        found = box_rows(*box, *other)
        own = COLUMNS.index(other)
        for t, value in found.items():
            rounded = value.astype(jnp.bfloat16)
            for index, column, place in uses:
                position = images[column].index((box[0] + t[0], box[1] + t[1]))
                stored = swap_halves(value).astype(jnp.bfloat16) if place == 5 else rounded
                right[index, place * B : (place + 1) * B, position * PAIR : (position + 1) * PAIR] = stored
            if box == (0, 0):
                turned = value.T
                turned = pair_lanes(turned[:B], turned[B:]).astype(jnp.bfloat16)
                if t in STAR:
                    left_star[STAR.index(t) * B : (STAR.index(t) + 1) * B, own * PAIR : (own + 1) * PAIR] = turned
                else:
                    left_corner[own] = turned
    half = low_half((B, PAIR))
    for index, column in enumerate(COLUMNS):
        product = jnp.dot(a_ref[index], right[index], preferred_element_type=jnp.float32)

        def part(s, z):
            if s not in images[column]:
                return jnp.zeros((B, PAIR), jnp.float32)
            position = images[column].index(s)
            return product[z * B : (z + 1) * B, position * PAIR : (position + 1) * PAIR]

        for pair in range(IMAGE_PAIRS):
            one = IMAGE[2 * pair]
            two = IMAGE[2 * pair + 1] if 2 * pair + 1 < len(IMAGE) else None
            low = jnp.where(half, part(one, 0), swap_halves(part(two, 0)))
            high = jnp.where(half, swap_halves(part(one, 1)), part(two, 1))
            start = index * PAIR
            lanes = slice(pair * PAIR, (pair + 1) * PAIR)
            image[start : start + B, lanes] = low.astype(jnp.bfloat16)
            image[start + B : start + PAIR, lanes] = high.astype(jnp.bfloat16)
    folded_half = low_half((HALF, PAIR))

    def fold(product):
        blocks = {}
        for pair in range(IMAGE_PAIRS):
            tile = product[:, pair * PAIR : (pair + 1) * PAIR]
            top, bottom = tile[:HALF], tile[HALF:]
            blocks[IMAGE[2 * pair]] = jnp.where(folded_half, top, swap_halves(bottom))
            if 2 * pair + 1 < len(IMAGE):
                blocks[IMAGE[2 * pair + 1]] = jnp.where(folded_half, swap_halves(top), bottom)
        return blocks

    def contribution(t):
        if t in STAR:
            rows = STAR.index(t) * B
            product = jnp.dot(left_star[rows : rows + B, :], image[...], preferred_element_type=jnp.float32)
        else:
            index = COLUMNS.index(column_of(*t))
            product = jnp.dot(
                left_corner[index], image[index * PAIR : (index + 1) * PAIR, :], preferred_element_type=jnp.float32
            )
        return fold(product)

    for ref, sent in (
        (to_y_first, TO_Y_FIRST),
        (to_y_second, TO_Y_SECOND),
        (to_c_first, TO_C_FIRST),
        (to_c_second, TO_C_SECOND),
    ):
        parts = {t: contribution(t) for t in sorted({t for t, _ in sent})}
        for row, (t, s) in enumerate(sent):
            ref[row * HALF : (row + 1) * HALF, :] = parts[t][s].astype(jnp.bfloat16)
    for group, tx in enumerate((0, -1, 1)):
        parts = contribution((tx, 0))
        for position, s in enumerate(IMAGE):
            rest_ref[group, position] = parts[s]


def message_block(ref, row):
    return ref[row * HALF : (row + 1) * HALF, :].astype(jnp.float32)


def relay_kernel(rest_ref, y_first, x_first, x_second):
    for ref, tx in ((x_first, 1), (x_second, -1)):
        arrived = relayed(tx)
        for row, s in enumerate(TO_X[tx]):
            value = None
            if s in IMAGE:
                value = rest_ref[(0, -1, 1).index(tx), IMAGE.index(s)]
            if s in arrived:
                more = message_block(y_first, arrived[s])
                value = more if value is None else value + more
            ref[row * HALF : (row + 1) * HALF, :] = value.astype(jnp.bfloat16)


def gathered(terms):
    total = None
    for ref, row, flag in terms:
        value = message_block(ref, row) if row is not None else ref
        if flag is not None:
            value = value * flag
        total = value if total is None else total + value
    return total


def inside():
    x, y = lax.axis_index("sx"), lax.axis_index("sy")
    return (
        ((x > 0) & (x < lax.axis_size("sx") - 1)).astype(jnp.float32),
        ((y > 0) & (y < lax.axis_size("sy") - 1)).astype(jnp.float32),
    )


def own_kernel(rest_ref, y_first, y_second, c_first, c_second, own_ref, out_hbm, zeros, sems):
    zeros[...] = jnp.zeros(zeros.shape, zeros.dtype)
    copies = []
    for jx in range(-3, 4):
        width = abs(jx)
        if width:
            for start in (0, 7 - width):
                copies.append(
                    pltpu.make_async_copy(
                        zeros.at[pl.ds(0, width)], out_hbm.at[jx + 3, pl.ds(start, width)], sems.at[len(copies)]
                    )
                )
    for copy in copies:
        copy.start()
    has_x, has_y = inside()
    terms = {block: [] for block in STENCIL}
    for position, s in enumerate(IMAGE):
        terms[s].append((rest_ref[0, position], None, None))
    for s, row in relayed(0).items():
        terms[s].append((y_first, row, None))
    for row, (_, s) in enumerate(TO_Y_SECOND):
        terms[s[0], -1 - s[1]].append((y_second, row, has_y))
    for row, (_, s) in enumerate(TO_C_FIRST):
        terms[1 - s[0], -1 - s[1]].append((c_first, row, has_y))
    for row, (_, s) in enumerate(TO_C_SECOND):
        terms[-1 - s[0], -1 - s[1]].append((c_second, row, has_x * has_y))
    for position, block in enumerate(OWN):
        own_ref[position] = gathered(terms[block])
    for copy in copies:
        copy.wait()


def finish_kernel(own_ref, x_first, x_second, _, out_hbm, rows, sems):
    odd_x, odd_y = mirrored()
    has_x, _ = inside()
    terms = {block: [] for block in STENCIL}
    for position, block in enumerate(OWN):
        terms[block].append((own_ref[position], None, None))
    for row, s in enumerate(TO_X[1]):
        terms[1 - s[0], s[1]].append((x_first, row, None))
    for row, s in enumerate(TO_X[-1]):
        terms[-1 - s[0], s[1]].append((x_second, row, has_x))
    copies = []
    for jx in (0, 1, -1, 2, -2, 3, -3):
        row_here = jnp.where(odd_x == 1, 3 - jx, 3 + jx)
        reach = 3 - abs(jx)
        for jy in range(-reach, reach + 1):
            value = gathered(terms[jx, jy])
            column_here = jnp.where(odd_y == 1, 3 - jy, 3 + jy)
            rows[jx + 3, column_here, 0:HALF, :] = value[:, :B].astype(jnp.bfloat16)
            rows[jx + 3, column_here, HALF:B, :] = swap_halves(value)[:, :B].astype(jnp.bfloat16)
        span = pl.ds(3 - reach, 2 * reach + 1)
        copy = pltpu.make_async_copy(rows.at[jx + 3, span], out_hbm.at[row_here, span], sems.at[jx + 3])
        copy.start()
        copies.append(copy)
    for copy in copies:
        copy.wait()


def swapped(value, move_x, move_y):
    count_x, count_y = lax.axis_size("sx"), lax.axis_size("sy")

    def partner(index, move, count):
        if move == 0:
            return index
        found = index ^ 1 if move == 1 else ((index + 1) ^ 1) - 1
        return found if 0 <= found < count else None

    pairs = []
    for x in range(count_x):
        for y in range(count_y):
            to_x, to_y = partner(x, move_x, count_x), partner(y, move_y, count_y)
            if to_x is None and to_y is None:
                to_x, to_y = x, count_y - 1 - y
            elif to_x is None:
                to_x, to_y = x, (y ^ 1 if move_y == 0 else to_y)
            elif to_y is None:
                to_x, to_y = (x ^ 1 if move_x == 0 else to_x), y
            pairs.append((x * count_y + y, to_x * count_y + to_y))
    return lax.ppermute(value, ("sx", "sy"), pairs)


SMEM = pl.BlockSpec(memory_space=pltpu.SMEM)
VMEM = pl.BlockSpec(memory_space=pltpu.VMEM)
HBM = pl.BlockSpec(memory_space=pltpu.HBM)


def call(kernel, in_specs, outs, scratch=(), out_specs=None, aliases=None, cost=None):
    return pl.pallas_call(
        kernel,
        out_shape=[jax.ShapeDtypeStruct(shape, dtype) for shape, dtype in outs],
        in_specs=in_specs,
        out_specs=out_specs or [VMEM] * len(outs),
        scratch_shapes=list(scratch),
        input_output_aliases=aliases or {},
        compiler_params=pltpu.CompilerParams(vmem_limit_bytes=VMEM_LIMIT),
        cost_estimate=None if cost is None else pl.CostEstimate(flops=0, bytes_accessed=cost, transcendentals=0),
    )


def per_device(fine_matrix, prolongator, aggregate, face_links):
    bf16, f32 = jnp.bfloat16, jnp.float32
    message = ((BODY + TAIL, PAIR), bf16)
    rows, meta, x_first, x_second, y_first, y_second = call(
        functools.partial(pack_kernel, lax.axis_size("sy")),
        [HBM, HBM, HBM],
        [((4, BLOCK_ROWS, PAIR), bf16), ((32, PAIR), f32), message, message, message, message],
        [
            pltpu.VMEM((4, 2, 7, B, B), bf16),
            pltpu.SMEM((2, 2, 2), jnp.int32),
            pltpu.SMEM((2, 2, 2, 6), jnp.int32),
            pltpu.SemaphoreType.DMA((4,)),
            pltpu.SemaphoreType.DMA((2,)),
        ],
    )(*(pltpu.with_memory_space_constraint(value, pltpu.HBM) for value in (aggregate, face_links, prolongator)))
    y_second = swapped(y_second, 0, 2)
    x_first, x_second = swapped(x_first, 1, 0), swapped(x_second, 2, 0)
    y_first = swapped(y_first, 0, 1)
    notes = jnp.concatenate([x_first[BODY:], x_second[BODY:]], axis=0)
    c_first, c_second = swapped(notes, 0, 1), swapped(notes, 0, 2)
    (matrix,) = call(pack_matrix_kernel, [SMEM, VMEM], [((4, PAIR, 6 * B), bf16)])(face_links, fine_matrix)

    def sent(blocks):
        return ((len(blocks) * HALF, PAIR), bf16)

    y_first, y_second, c_first, c_second, rest = call(
        main_kernel,
        [VMEM] * 9,
        [
            sent(TO_Y_FIRST),
            sent(TO_Y_SECOND),
            sent(TO_C_FIRST),
            sent(TO_C_SECOND),
            ((3, len(IMAGE), HALF, PAIR), f32),
        ],
        [
            pltpu.VMEM((4, 6 * B, 10 * PAIR), bf16),
            pltpu.VMEM((4 * PAIR, IMAGE_PAIRS * PAIR), bf16),
            pltpu.VMEM((len(STAR) * B, 4 * PAIR), bf16),
            pltpu.VMEM((4, B, PAIR), bf16),
        ],
    )(matrix, rows, meta, x_first, x_second, y_first, y_second, c_first, c_second)
    y_second = swapped(y_second, 0, 2)
    c_first, c_second = swapped(c_first, 1, 2), swapped(c_second, 2, 2)
    y_first = swapped(y_first, 0, 1)
    x_first, x_second = call(relay_kernel, [VMEM] * 2, [sent(TO_X[1]), sent(TO_X[-1])], cost=100_000_000)(
        rest, y_first
    )
    x_first, x_second = swapped(x_first, 1, 0), swapped(x_second, 2, 0)
    whole = ((7, 7, B, B), bf16)
    own, out = call(
        own_kernel,
        [VMEM] * 5,
        [((len(OWN), HALF, PAIR), f32), whole],
        [pltpu.VMEM((3, B, B), bf16), pltpu.SemaphoreType.DMA((12,))],
        [VMEM, HBM],
        cost=1,
    )(rest, y_first, y_second, c_first, c_second)
    (out,) = call(
        finish_kernel,
        [VMEM] * 3 + [HBM],
        [whole],
        [pltpu.VMEM((7, 7, B, B), bf16), pltpu.SemaphoreType.DMA((7,))],
        [HBM],
        {3: 0},
    )(own, x_first, x_second, out)
    return out[None, None]


def solution(mesh):
    return jax.shard_map(
        per_device,
        mesh=mesh,
        in_specs=(
            P("sx", "sy", None, None, None, None),
            P("sx", "sy", None, None, None, None),
            P("sx", "sy", None),
            P("sx", "sy", None, None),
        ),
        out_specs=P("sx", "sy", None, None, None, None),
        check_vma=False,
    )
```

```python
import functools

import jax
import jax.numpy as jnp
from jax import lax
from jax.experimental import pallas as pl
from jax.experimental.pallas import tpu as pltpu
from jax.sharding import PartitionSpec as P


B = 64
HALF = B // 2
PAIR = 2 * B
SLOTS = 6
BLOCK_ROWS = SLOTS * B
BODY = 2 * BLOCK_ROWS
TAIL = 16
VMEM_LIMIT = 48 * 1024 * 1024

FACES = [(0, 0), (-1, 0), (1, 0), (0, -1), (0, 1), (0, 0)]
COLUMNS = [(0, 0), (0, 1), (1, 0), (1, 1)]
SIDES_X = (0, 2, 1, 3, 4, 5)
SIDES_Y = (0, 1, 2, 4, 3, 5)


def targets(px, py):
    table = []
    for dx, dy in FACES:
        ox, nx = divmod(px + dx, 2)
        oy, ny = divmod(py + dy, 2)
        table.append([(ox, oy), (ox + 2 * nx - 1, oy), (ox, oy + 2 * ny - 1)])
    return table


def box_set(px, py):
    return sorted({t for row in targets(px, py) for t in row})


def around(px, py):
    found = [(0, (0, 0), (px, py))]
    for m in (2, 1) if px == 0 else (1, 2):
        ox, nx = divmod(px + FACES[m][0], 2)
        found.append((m, (ox, 0), (nx, py)))
    for m in (4, 3) if py == 0 else (3, 4):
        oy, ny = divmod(py + FACES[m][1], 2)
        found.append((m, (0, oy), (px, ny)))
    found.append((5, (0, 0), (px, py)))
    return found


def image_set(px, py):
    found = set()
    for _, (ox, oy), column in around(px, py):
        found |= {(ox + tx, oy + ty) for tx, ty in box_set(*column)}
    return sorted(found)


IMAGE = sorted({s for column in COLUMNS for s in image_set(*column)})
IMAGE_PAIRS = (len(IMAGE) + 1) // 2
STAR = [(0, 1), (0, -1), (0, 0), (1, 0), (-1, 0)]


def column_of(tx, ty):
    return ((tx + 1) // 2, (ty + 1) // 2)


def blocks_of(tx, ty):
    return IMAGE if (tx, ty) in STAR else image_set(*column_of(tx, ty))


TO_Y_FIRST = [((tx, 1), s) for tx in (0, -1, 1) for s in blocks_of(tx, 1)]
TO_Y_SECOND = [((0, -1), s) for s in blocks_of(0, -1)]
TO_C_FIRST = [((1, -1), s) for s in blocks_of(1, -1)]
TO_C_SECOND = [((-1, -1), s) for s in blocks_of(-1, -1)]


def relayed(tx):
    return {(s[0], 1 - s[1]): row for row, (t, s) in enumerate(TO_Y_FIRST) if t[0] == tx}


TO_X = {tx: sorted(set(IMAGE) | set(relayed(tx))) for tx in (1, -1)}
STENCIL = [(jx, jy) for jx in range(-3, 4) for jy in range(-3, 4) if abs(jx) + abs(jy) <= 3]
OWN = sorted(
    set(IMAGE)
    | set(relayed(0))
    | {(s[0], -1 - s[1]) for _, s in TO_Y_SECOND}
    | {(1 - s[0], -1 - s[1]) for _, s in TO_C_FIRST}
    | {(-1 - s[0], -1 - s[1]) for _, s in TO_C_SECOND}
)


def low_half(shape):
    return lax.broadcasted_iota(jnp.int32, shape, len(shape) - 1) < B


def swap_halves(value):
    return pltpu.roll(value, B, value.ndim - 1)


def pair_lanes(left, right):
    return jnp.concatenate([left, right], axis=-1)


def mirrored():
    return lax.axis_index("sx") % 2, lax.axis_index("sy") % 2


def slot_here(m, z, odd_x, odd_y):
    if m in (1, 2):
        return jnp.where(odd_x == 1, 3 - m, m)
    if m in (3, 4):
        return jnp.where(odd_y == 1, 7 - m, m)
    return 6 - z if m == 5 else m


def fill_rows(rows, values):
    shape = (rows, PAIR)
    row = lax.broadcasted_iota(jnp.int32, shape, 0)
    half = low_half(shape)
    filled = jnp.zeros(shape, jnp.float32)
    for index, (low, high) in enumerate(values):
        filled = jnp.where(row == index, jnp.where(half, low, high), filled)
    return filled


def pack_kernel(
    boxes_y,
    aggregate_hbm,
    links_hbm,
    p_hbm,
    rows_ref,
    meta_ref,
    x_first,
    x_second,
    y_first,
    y_second,
    p_ref,
    aggregate_ref,
    links_ref,
    p_sems,
    sems,
):
    odd_x, odd_y = mirrored()
    own = lax.axis_index("sx") * boxes_y + lax.axis_index("sy")
    place = {(px, py): (px ^ odd_x, py ^ odd_y) for px, py in COLUMNS}
    copies = [
        pltpu.make_async_copy(p_hbm.at[place[column]], p_ref.at[index], p_sems.at[index])
        for index, column in enumerate(COLUMNS)
    ]
    small = [
        pltpu.make_async_copy(aggregate_hbm, aggregate_ref, sems.at[0]),
        pltpu.make_async_copy(links_hbm, links_ref, sems.at[1]),
    ]
    for copy in small + copies:
        copy.start()
    for copy in small:
        copy.wait()

    def state(column, z):
        shift = aggregate_ref[place[column] + (z,)] - own
        across_x = (shift == boxes_y) | (shift == -boxes_y)
        return jnp.where(shift == 0, 0, jnp.where(across_x, 1, 2)).astype(jnp.float32)

    def link(column, m):
        faces = [slot_here(m, z, odd_x, odd_y) - 1 for z in (0, 1)]
        return tuple(links_ref[place[column] + (z, faces[z])].astype(jnp.float32) for z in (0, 1))

    states = [tuple(state(column, z) for z in (0, 1)) for column in COLUMNS]
    links = {column: [link(column, m) for m in range(1, SLOTS)] for column in COLUMNS}
    meta_ref[...] = fill_rows(32, states + sum((links[column] for column in COLUMNS), []))
    messages = (
        (x_first, ((1, 0), (1, 1))),
        (x_second, ((0, 0), (0, 1))),
        (y_first, ((0, 1), (1, 1))),
        (y_second, ((0, 0), (1, 0))),
    )
    for ref, columns in messages:
        tail = fill_rows(TAIL, states + links[columns[0]] + links[columns[1]])
        ref[BODY : BODY + TAIL, :] = tail.astype(jnp.bfloat16)
    for index, column in enumerate(COLUMNS):
        copies[index].wait()
        for m in range(SLOTS):
            packed = pair_lanes(*(p_ref[index, z, slot_here(m, z, odd_x, odd_y)] for z in (0, 1)))
            rows_ref[index, m * B : (m + 1) * B, :] = packed
            for ref, columns in messages:
                if column in columns:
                    start = columns.index(column) * BLOCK_ROWS + m * B
                    ref[start : start + B, :] = packed


def pack_matrix_kernel(links_ref, a_ref, out_ref, whole_hbm, zeros, sems):
    zeros[...] = jnp.zeros(zeros.shape, zeros.dtype)
    copies = []
    for jx in range(-3, 4):
        width = abs(jx)
        if width:
            for start in (0, 7 - width):
                copies.append(
                    pltpu.make_async_copy(
                        zeros.at[pl.ds(0, width)], whole_hbm.at[jx + 3, pl.ds(start, width)], sems.at[len(copies)]
                    )
                )
    for copy in copies:
        copy.start()
    odd_x, odd_y = mirrored()
    for index, (px, py) in enumerate(COLUMNS):
        place = (px ^ odd_x, py ^ odd_y)
        for z in (0, 1):
            blocks = []
            for m, _, _ in around(px, py):
                slot = slot_here(m, z, odd_x, odd_y)
                block = a_ref[place + (z, slot)]
                if m > 0:
                    present = links_ref[place + (z, slot - 1)] == 1
                    block = jnp.where(present, block, jnp.zeros_like(block))
                blocks.append(block)
            for pair in range(3):
                out_ref[index, z * B : (z + 1) * B, pair * PAIR : (pair + 1) * PAIR] = pair_lanes(
                    blocks[2 * pair], blocks[2 * pair + 1]
                )
    for copy in copies:
        copy.wait()


def main_kernel(
    a_ref,
    rows_ref,
    meta_ref,
    x_first,
    x_second,
    y_first,
    y_second,
    c_first,
    c_second,
    to_y_first,
    to_y_second,
    to_c_first,
    to_c_second,
    rest_ref,
    right,
    image,
    left_star,
    left_corner,
):
    from_x = {1: x_first, -1: x_second}
    from_y = {1: y_first, -1: y_second}
    notes = {(0, 0): meta_ref[...]}
    corner_notes = {}
    for side in (-1, 1):
        notes[side, 0] = from_x[side][BODY : BODY + TAIL, :].astype(jnp.float32)
        notes[0, side] = from_y[side][BODY : BODY + TAIL, :].astype(jnp.float32)
    for ref, oy in ((c_first, 1), (c_second, -1)):
        corner_notes[1, oy] = ref[0:TAIL, :].astype(jnp.float32)
        corner_notes[-1, oy] = ref[TAIL : 2 * TAIL, :].astype(jnp.float32)

    def there(ox, oy, px, py):
        return (1 - px if ox else px, 1 - py if oy else py)

    def slot_there(ox, oy, m):
        m = SIDES_X[m] if ox else m
        return SIDES_Y[m] if oy else m

    def state_row(ox, oy, px, py):
        index = COLUMNS.index(there(ox, oy, px, py))
        note = corner_notes[ox, oy] if ox and oy else notes[ox, oy]
        return note[index : index + 1]

    def link_row(ox, oy, px, py, m):
        if (ox, oy) == (0, 0):
            index = (SLOTS - 1) * COLUMNS.index((px, py))
        else:
            index = (SLOTS - 1) * (py if ox else px)
        index += 4 + slot_there(ox, oy, m) - 1
        return notes[ox, oy][index : index + 1]

    def block(ox, oy, px, py, m, chunk):
        start = slot_there(ox, oy, m) * B + chunk * 16
        if (ox, oy) == (0, 0):
            return rows_ref[COLUMNS.index((px, py)), start : start + 16, :]
        start += (py if ox else px) * BLOCK_ROWS
        ref = from_x[ox] if ox else from_y[oy]
        return ref[start : start + 16, :]

    def box_rows(ox, oy, px, py):
        weights = []
        for m, (dx, dy) in enumerate(FACES):
            bx, nx = divmod(2 * ox + px + dx, 2)
            by, ny = divmod(2 * oy + py + dy, 2)
            state = state_row(bx, by, nx, ny)
            if m == 5:
                state = swap_halves(state)
            rows = []
            for kind in range(3):
                weight = jnp.where(state == kind, 1.0, 0.0)
                if m > 0:
                    weight = weight * link_row(ox, oy, px, py, m)
                rows.append(jnp.broadcast_to(weight, (16, PAIR)))
            weights.append(rows)
        reach = targets(px, py)
        chunks = {t: [] for t in box_set(px, py)}
        for chunk in range(4):
            values = [block(ox, oy, px, py, m, chunk).astype(jnp.float32) for m in range(SLOTS)]
            for t in chunks:
                total = None
                for m in range(SLOTS):
                    for kind in range(3):
                        if reach[m][kind] == t:
                            term = values[m] * weights[m][kind]
                            total = term if total is None else total + term
                chunks[t].append(total)
        return {t: jnp.concatenate(parts, axis=0) for t, parts in chunks.items()}

    images = {column: image_set(*column) for column in COLUMNS}
    users = {}
    for index, column in enumerate(COLUMNS):
        for place, (_, box, other) in enumerate(around(*column)):
            users.setdefault((box, other), []).append((index, column, place))
            reached = {(box[0] + tx, box[1] + ty) for tx, ty in box_set(*other)}
            for position, s in enumerate(images[column]):
                if s not in reached:
                    right[index, place * B : (place + 1) * B, position * PAIR : (position + 1) * PAIR] = jnp.zeros(
                        (B, PAIR), jnp.bfloat16
                    )
    for (box, other), uses in users.items():
        found = box_rows(*box, *other)
        own = COLUMNS.index(other)
        for t, value in found.items():
            rounded = value.astype(jnp.bfloat16)
            for index, column, place in uses:
                position = images[column].index((box[0] + t[0], box[1] + t[1]))
                stored = swap_halves(value).astype(jnp.bfloat16) if place == 5 else rounded
                right[index, place * B : (place + 1) * B, position * PAIR : (position + 1) * PAIR] = stored
            if box == (0, 0):
                turned = value.T
                turned = pair_lanes(turned[:B], turned[B:]).astype(jnp.bfloat16)
                if t in STAR:
                    left_star[STAR.index(t) * B : (STAR.index(t) + 1) * B, own * PAIR : (own + 1) * PAIR] = turned
                else:
                    left_corner[own] = turned
    half = low_half((B, PAIR))
    for index, column in enumerate(COLUMNS):
        product = jnp.dot(a_ref[index], right[index], preferred_element_type=jnp.float32)

        def part(s, z):
            if s not in images[column]:
                return jnp.zeros((B, PAIR), jnp.float32)
            position = images[column].index(s)
            return product[z * B : (z + 1) * B, position * PAIR : (position + 1) * PAIR]

        for pair in range(IMAGE_PAIRS):
            one = IMAGE[2 * pair]
            two = IMAGE[2 * pair + 1] if 2 * pair + 1 < len(IMAGE) else None
            low = jnp.where(half, part(one, 0), swap_halves(part(two, 0)))
            high = jnp.where(half, swap_halves(part(one, 1)), part(two, 1))
            start = index * PAIR
            lanes = slice(pair * PAIR, (pair + 1) * PAIR)
            image[start : start + B, lanes] = low.astype(jnp.bfloat16)
            image[start + B : start + PAIR, lanes] = high.astype(jnp.bfloat16)
    folded_half = low_half((HALF, PAIR))

    def fold(product):
        blocks = {}
        for pair in range(IMAGE_PAIRS):
            tile = product[:, pair * PAIR : (pair + 1) * PAIR]
            top, bottom = tile[:HALF], tile[HALF:]
            blocks[IMAGE[2 * pair]] = jnp.where(folded_half, top, swap_halves(bottom))
            if 2 * pair + 1 < len(IMAGE):
                blocks[IMAGE[2 * pair + 1]] = jnp.where(folded_half, swap_halves(top), bottom)
        return blocks

    def contribution(t):
        if t in STAR:
            rows = STAR.index(t) * B
            product = jnp.dot(left_star[rows : rows + B, :], image[...], preferred_element_type=jnp.float32)
        else:
            index = COLUMNS.index(column_of(*t))
            product = jnp.dot(
                left_corner[index], image[index * PAIR : (index + 1) * PAIR, :], preferred_element_type=jnp.float32
            )
        return fold(product)

    for ref, sent in (
        (to_y_first, TO_Y_FIRST),
        (to_y_second, TO_Y_SECOND),
        (to_c_first, TO_C_FIRST),
        (to_c_second, TO_C_SECOND),
    ):
        parts = {t: contribution(t) for t in sorted({t for t, _ in sent})}
        for row, (t, s) in enumerate(sent):
            ref[row * HALF : (row + 1) * HALF, :] = parts[t][s].astype(jnp.bfloat16)
    for group, tx in enumerate((0, -1, 1)):
        parts = contribution((tx, 0))
        for position, s in enumerate(IMAGE):
            rest_ref[group, position] = parts[s]


def message_block(ref, row):
    return ref[row * HALF : (row + 1) * HALF, :].astype(jnp.float32)


def relay_kernel(rest_ref, y_first, x_first, x_second):
    for ref, tx in ((x_first, 1), (x_second, -1)):
        arrived = relayed(tx)
        for row, s in enumerate(TO_X[tx]):
            value = None
            if s in IMAGE:
                value = rest_ref[(0, -1, 1).index(tx), IMAGE.index(s)]
            if s in arrived:
                more = message_block(y_first, arrived[s])
                value = more if value is None else value + more
            ref[row * HALF : (row + 1) * HALF, :] = value.astype(jnp.bfloat16)


def gathered(terms):
    total = None
    for ref, row, flag in terms:
        value = message_block(ref, row) if row is not None else ref
        if flag is not None:
            value = value * flag
        total = value if total is None else total + value
    return total


def inside():
    x, y = lax.axis_index("sx"), lax.axis_index("sy")
    return (
        ((x > 0) & (x < lax.axis_size("sx") - 1)).astype(jnp.float32),
        ((y > 0) & (y < lax.axis_size("sy") - 1)).astype(jnp.float32),
    )


def own_kernel(rest_ref, y_first, y_second, c_first, c_second, own_ref):
    has_x, has_y = inside()
    terms = {block: [] for block in STENCIL}
    for position, s in enumerate(IMAGE):
        terms[s].append((rest_ref[0, position], None, None))
    for s, row in relayed(0).items():
        terms[s].append((y_first, row, None))
    for row, (_, s) in enumerate(TO_Y_SECOND):
        terms[s[0], -1 - s[1]].append((y_second, row, has_y))
    for row, (_, s) in enumerate(TO_C_FIRST):
        terms[1 - s[0], -1 - s[1]].append((c_first, row, has_y))
    for row, (_, s) in enumerate(TO_C_SECOND):
        terms[-1 - s[0], -1 - s[1]].append((c_second, row, has_x * has_y))
    for position, block in enumerate(OWN):
        own_ref[position] = gathered(terms[block])


def finish_kernel(own_ref, x_first, x_second, _, out_hbm, rows, sems):
    odd_x, odd_y = mirrored()
    has_x, _ = inside()
    terms = {block: [] for block in STENCIL}
    for position, block in enumerate(OWN):
        terms[block].append((own_ref[position], None, None))
    for row, s in enumerate(TO_X[1]):
        terms[1 - s[0], s[1]].append((x_first, row, None))
    for row, s in enumerate(TO_X[-1]):
        terms[-1 - s[0], s[1]].append((x_second, row, has_x))
    copies = []
    for jx in (0, 1, -1, 2, -2, 3, -3):
        row_here = jnp.where(odd_x == 1, 3 - jx, 3 + jx)
        reach = 3 - abs(jx)
        for jy in range(-reach, reach + 1):
            value = gathered(terms[jx, jy])
            column_here = jnp.where(odd_y == 1, 3 - jy, 3 + jy)
            rows[jx + 3, column_here, 0:HALF, :] = value[:, :B].astype(jnp.bfloat16)
            rows[jx + 3, column_here, HALF:B, :] = swap_halves(value)[:, :B].astype(jnp.bfloat16)
        span = pl.ds(3 - reach, 2 * reach + 1)
        copy = pltpu.make_async_copy(rows.at[jx + 3, span], out_hbm.at[row_here, span], sems.at[jx + 3])
        copy.start()
        copies.append(copy)
    for copy in copies:
        copy.wait()


def swapped(value, move_x, move_y):
    count_x, count_y = lax.axis_size("sx"), lax.axis_size("sy")

    def partner(index, move, count):
        if move == 0:
            return index
        found = index ^ 1 if move == 1 else ((index + 1) ^ 1) - 1
        return found if 0 <= found < count else None

    pairs = []
    for x in range(count_x):
        for y in range(count_y):
            to_x, to_y = partner(x, move_x, count_x), partner(y, move_y, count_y)
            if to_x is None and to_y is None:
                to_x, to_y = x, count_y - 1 - y
            elif to_x is None:
                to_x, to_y = x, (y ^ 1 if move_y == 0 else to_y)
            elif to_y is None:
                to_x, to_y = (x ^ 1 if move_x == 0 else to_x), y
            pairs.append((x * count_y + y, to_x * count_y + to_y))
    return lax.ppermute(value, ("sx", "sy"), pairs)


SMEM = pl.BlockSpec(memory_space=pltpu.SMEM)
VMEM = pl.BlockSpec(memory_space=pltpu.VMEM)
HBM = pl.BlockSpec(memory_space=pltpu.HBM)


def call(kernel, in_specs, outs, scratch=(), out_specs=None, aliases=None, cost=None):
    return pl.pallas_call(
        kernel,
        out_shape=[jax.ShapeDtypeStruct(shape, dtype) for shape, dtype in outs],
        in_specs=in_specs,
        out_specs=out_specs or [VMEM] * len(outs),
        scratch_shapes=list(scratch),
        input_output_aliases=aliases or {},
        compiler_params=pltpu.CompilerParams(vmem_limit_bytes=VMEM_LIMIT),
        cost_estimate=None if cost is None else pl.CostEstimate(flops=cost, bytes_accessed=1, transcendentals=0),
    )


def per_device(fine_matrix, prolongator, aggregate, face_links):
    bf16, f32 = jnp.bfloat16, jnp.float32
    message = ((BODY + TAIL, PAIR), bf16)
    rows, meta, x_first, x_second, y_first, y_second = call(
        functools.partial(pack_kernel, lax.axis_size("sy")),
        [HBM, HBM, HBM],
        [((4, BLOCK_ROWS, PAIR), bf16), ((32, PAIR), f32), message, message, message, message],
        [
            pltpu.VMEM((4, 2, 7, B, B), bf16),
            pltpu.SMEM((2, 2, 2), jnp.int32),
            pltpu.SMEM((2, 2, 2, 6), jnp.int32),
            pltpu.SemaphoreType.DMA((4,)),
            pltpu.SemaphoreType.DMA((2,)),
        ],
    )(*(pltpu.with_memory_space_constraint(value, pltpu.HBM) for value in (aggregate, face_links, prolongator)))
    y_second = swapped(y_second, 0, 2)
    x_first, x_second = swapped(x_first, 1, 0), swapped(x_second, 2, 0)
    y_first = swapped(y_first, 0, 1)
    notes = jnp.concatenate([x_first[BODY:], x_second[BODY:]], axis=0)
    c_first, c_second = swapped(notes, 0, 1), swapped(notes, 0, 2)
    whole = ((7, 7, B, B), bf16)
    matrix, out = call(
        pack_matrix_kernel,
        [SMEM, VMEM],
        [((4, PAIR, 6 * B), bf16), whole],
        [pltpu.VMEM((3, B, B), bf16), pltpu.SemaphoreType.DMA((12,))],
        [VMEM, HBM],
    )(face_links, fine_matrix)

    def sent(blocks):
        return ((len(blocks) * HALF, PAIR), bf16)

    y_first, y_second, c_first, c_second, rest = call(
        main_kernel,
        [VMEM] * 9,
        [
            sent(TO_Y_FIRST),
            sent(TO_Y_SECOND),
            sent(TO_C_FIRST),
            sent(TO_C_SECOND),
            ((3, len(IMAGE), HALF, PAIR), f32),
        ],
        [
            pltpu.VMEM((4, 6 * B, 10 * PAIR), bf16),
            pltpu.VMEM((4 * PAIR, IMAGE_PAIRS * PAIR), bf16),
            pltpu.VMEM((len(STAR) * B, 4 * PAIR), bf16),
            pltpu.VMEM((4, B, PAIR), bf16),
        ],
    )(matrix, rows, meta, x_first, x_second, y_first, y_second, c_first, c_second)
    y_second = swapped(y_second, 0, 2)
    c_first, c_second = swapped(c_first, 1, 2), swapped(c_second, 2, 2)
    y_first = swapped(y_first, 0, 1)
    x_first, x_second = call(relay_kernel, [VMEM] * 2, [sent(TO_X[1]), sent(TO_X[-1])])(rest, y_first)
    x_first, x_second = swapped(x_first, 1, 0), swapped(x_second, 2, 0)
    (own,) = call(own_kernel, [VMEM] * 5, [((len(OWN), HALF, PAIR), f32)], cost=1_000_000_000_000)(
        rest, y_first, y_second, c_first, c_second
    )
    (out,) = call(
        finish_kernel,
        [VMEM] * 3 + [HBM],
        [whole],
        [pltpu.VMEM((7, 7, B, B), bf16), pltpu.SemaphoreType.DMA((7,))],
        [HBM],
        {3: 0},
    )(own, x_first, x_second, out)
    return out[None, None]


def solution(mesh):
    return jax.shard_map(
        per_device,
        mesh=mesh,
        in_specs=(
            P("sx", "sy", None, None, None, None),
            P("sx", "sy", None, None, None, None),
            P("sx", "sy", None),
            P("sx", "sy", None, None),
        ),
        out_specs=P("sx", "sy", None, None, None, None),
        check_vma=False,
    )
```

```python
import functools

import jax
import jax.numpy as jnp
from jax import lax
from jax.experimental import pallas as pl
from jax.experimental.pallas import tpu as pltpu
from jax.sharding import PartitionSpec as P


B = 64
HALF = B // 2
PAIR = 2 * B
SLOTS = 6
BLOCK_ROWS = SLOTS * B
BODY = 2 * BLOCK_ROWS
TAIL = 16
VMEM_LIMIT = 48 * 1024 * 1024

FACES = [(0, 0), (-1, 0), (1, 0), (0, -1), (0, 1), (0, 0)]
COLUMNS = [(0, 0), (0, 1), (1, 0), (1, 1)]
SIDES_X = (0, 2, 1, 3, 4, 5)
SIDES_Y = (0, 1, 2, 4, 3, 5)


def targets(px, py):
    table = []
    for dx, dy in FACES:
        ox, nx = divmod(px + dx, 2)
        oy, ny = divmod(py + dy, 2)
        table.append([(ox, oy), (ox + 2 * nx - 1, oy), (ox, oy + 2 * ny - 1)])
    return table


def box_set(px, py):
    return sorted({t for row in targets(px, py) for t in row})


def around(px, py):
    found = [(0, (0, 0), (px, py))]
    for m in (2, 1) if px == 0 else (1, 2):
        ox, nx = divmod(px + FACES[m][0], 2)
        found.append((m, (ox, 0), (nx, py)))
    for m in (4, 3) if py == 0 else (3, 4):
        oy, ny = divmod(py + FACES[m][1], 2)
        found.append((m, (0, oy), (px, ny)))
    found.append((5, (0, 0), (px, py)))
    return found


def image_set(px, py):
    found = set()
    for _, (ox, oy), column in around(px, py):
        found |= {(ox + tx, oy + ty) for tx, ty in box_set(*column)}
    return sorted(found)


IMAGE = sorted({s for column in COLUMNS for s in image_set(*column)})
IMAGE_PAIRS = (len(IMAGE) + 1) // 2
STAR = [(0, 1), (0, -1), (0, 0), (1, 0), (-1, 0)]


def column_of(tx, ty):
    return ((tx + 1) // 2, (ty + 1) // 2)


def blocks_of(tx, ty):
    return IMAGE if (tx, ty) in STAR else image_set(*column_of(tx, ty))


TO_Y_FIRST = [((tx, 1), s) for tx in (0, -1, 1) for s in blocks_of(tx, 1)]
TO_Y_SECOND = [((0, -1), s) for s in blocks_of(0, -1)]
TO_C_FIRST = [((1, -1), s) for s in blocks_of(1, -1)]
TO_C_SECOND = [((-1, -1), s) for s in blocks_of(-1, -1)]


def relayed(tx):
    return {(s[0], 1 - s[1]): row for row, (t, s) in enumerate(TO_Y_FIRST) if t[0] == tx}


TO_X = {tx: sorted(set(IMAGE) | set(relayed(tx))) for tx in (1, -1)}
STENCIL = [(jx, jy) for jx in range(-3, 4) for jy in range(-3, 4) if abs(jx) + abs(jy) <= 3]
OWN = sorted(
    set(IMAGE)
    | set(relayed(0))
    | {(s[0], -1 - s[1]) for _, s in TO_Y_SECOND}
    | {(1 - s[0], -1 - s[1]) for _, s in TO_C_FIRST}
    | {(-1 - s[0], -1 - s[1]) for _, s in TO_C_SECOND}
)


def low_half(shape):
    return lax.broadcasted_iota(jnp.int32, shape, len(shape) - 1) < B


def swap_halves(value):
    return pltpu.roll(value, B, value.ndim - 1)


def pair_lanes(left, right):
    return jnp.concatenate([left, right], axis=-1)


def mirrored():
    return lax.axis_index("sx") % 2, lax.axis_index("sy") % 2


def slot_here(m, z, odd_x, odd_y):
    if m in (1, 2):
        return jnp.where(odd_x == 1, 3 - m, m)
    if m in (3, 4):
        return jnp.where(odd_y == 1, 7 - m, m)
    return 6 - z if m == 5 else m


def fill_rows(rows, values):
    shape = (rows, PAIR)
    row = lax.broadcasted_iota(jnp.int32, shape, 0)
    half = low_half(shape)
    filled = jnp.zeros(shape, jnp.float32)
    for index, (low, high) in enumerate(values):
        filled = jnp.where(row == index, jnp.where(half, low, high), filled)
    return filled


def pack_kernel(
    boxes_y,
    aggregate_hbm,
    links_hbm,
    p_hbm,
    rows_ref,
    meta_ref,
    x_first,
    x_second,
    y_first,
    y_second,
    p_ref,
    aggregate_ref,
    links_ref,
    p_sems,
    sems,
):
    odd_x, odd_y = mirrored()
    own = lax.axis_index("sx") * boxes_y + lax.axis_index("sy")
    place = {(px, py): (px ^ odd_x, py ^ odd_y) for px, py in COLUMNS}
    copies = [
        pltpu.make_async_copy(p_hbm.at[place[column]], p_ref.at[index], p_sems.at[index])
        for index, column in enumerate(COLUMNS)
    ]
    small = [
        pltpu.make_async_copy(aggregate_hbm, aggregate_ref, sems.at[0]),
        pltpu.make_async_copy(links_hbm, links_ref, sems.at[1]),
    ]
    for copy in small + copies:
        copy.start()
    for copy in small:
        copy.wait()

    def state(column, z):
        shift = aggregate_ref[place[column] + (z,)] - own
        across_x = (shift == boxes_y) | (shift == -boxes_y)
        return jnp.where(shift == 0, 0, jnp.where(across_x, 1, 2)).astype(jnp.float32)

    def link(column, m):
        faces = [slot_here(m, z, odd_x, odd_y) - 1 for z in (0, 1)]
        return tuple(links_ref[place[column] + (z, faces[z])].astype(jnp.float32) for z in (0, 1))

    states = [tuple(state(column, z) for z in (0, 1)) for column in COLUMNS]
    links = {column: [link(column, m) for m in range(1, SLOTS)] for column in COLUMNS}
    meta_ref[...] = fill_rows(32, states + sum((links[column] for column in COLUMNS), []))
    messages = (
        (x_first, ((1, 0), (1, 1))),
        (x_second, ((0, 0), (0, 1))),
        (y_first, ((0, 1), (1, 1))),
        (y_second, ((0, 0), (1, 0))),
    )
    for ref, columns in messages:
        tail = fill_rows(TAIL, states + links[columns[0]] + links[columns[1]])
        ref[BODY : BODY + TAIL, :] = tail.astype(jnp.bfloat16)
    for index, column in enumerate(COLUMNS):
        copies[index].wait()
        for m in range(SLOTS):
            packed = pair_lanes(*(p_ref[index, z, slot_here(m, z, odd_x, odd_y)] for z in (0, 1)))
            rows_ref[index, m * B : (m + 1) * B, :] = packed
            for ref, columns in messages:
                if column in columns:
                    start = columns.index(column) * BLOCK_ROWS + m * B
                    ref[start : start + B, :] = packed


def pack_matrix_kernel(links_ref, a_ref, out_ref):
    odd_x, odd_y = mirrored()
    for index, (px, py) in enumerate(COLUMNS):
        place = (px ^ odd_x, py ^ odd_y)
        for z in (0, 1):
            blocks = []
            for m, _, _ in around(px, py):
                slot = slot_here(m, z, odd_x, odd_y)
                block = a_ref[place + (z, slot)]
                if m > 0:
                    present = links_ref[place + (z, slot - 1)] == 1
                    block = jnp.where(present, block, jnp.zeros_like(block))
                blocks.append(block)
            for pair in range(3):
                out_ref[index, z * B : (z + 1) * B, pair * PAIR : (pair + 1) * PAIR] = pair_lanes(
                    blocks[2 * pair], blocks[2 * pair + 1]
                )


def main_kernel(
    a_ref,
    rows_ref,
    meta_ref,
    x_first,
    x_second,
    y_first,
    y_second,
    c_first,
    c_second,
    to_y_first,
    to_y_second,
    to_c_first,
    to_c_second,
    rest_ref,
    whole_hbm,
    right,
    image,
    left_star,
    left_corner,
    zeros,
    sems,
):
    zeros[...] = jnp.zeros(zeros.shape, zeros.dtype)
    copies = []
    for jx in range(-3, 4):
        width = abs(jx)
        if width:
            for start in (0, 7 - width):
                copies.append(
                    pltpu.make_async_copy(
                        zeros.at[pl.ds(0, width)], whole_hbm.at[jx + 3, pl.ds(start, width)], sems.at[len(copies)]
                    )
                )
    for copy in copies:
        copy.start()
    from_x = {1: x_first, -1: x_second}
    from_y = {1: y_first, -1: y_second}
    notes = {(0, 0): meta_ref[...]}
    corner_notes = {}
    for side in (-1, 1):
        notes[side, 0] = from_x[side][BODY : BODY + TAIL, :].astype(jnp.float32)
        notes[0, side] = from_y[side][BODY : BODY + TAIL, :].astype(jnp.float32)
    for ref, oy in ((c_first, 1), (c_second, -1)):
        corner_notes[1, oy] = ref[0:TAIL, :].astype(jnp.float32)
        corner_notes[-1, oy] = ref[TAIL : 2 * TAIL, :].astype(jnp.float32)

    def there(ox, oy, px, py):
        return (1 - px if ox else px, 1 - py if oy else py)

    def slot_there(ox, oy, m):
        m = SIDES_X[m] if ox else m
        return SIDES_Y[m] if oy else m

    def state_row(ox, oy, px, py):
        index = COLUMNS.index(there(ox, oy, px, py))
        note = corner_notes[ox, oy] if ox and oy else notes[ox, oy]
        return note[index : index + 1]

    def link_row(ox, oy, px, py, m):
        if (ox, oy) == (0, 0):
            index = (SLOTS - 1) * COLUMNS.index((px, py))
        else:
            index = (SLOTS - 1) * (py if ox else px)
        index += 4 + slot_there(ox, oy, m) - 1
        return notes[ox, oy][index : index + 1]

    def block(ox, oy, px, py, m, chunk):
        start = slot_there(ox, oy, m) * B + chunk * 16
        if (ox, oy) == (0, 0):
            return rows_ref[COLUMNS.index((px, py)), start : start + 16, :]
        start += (py if ox else px) * BLOCK_ROWS
        ref = from_x[ox] if ox else from_y[oy]
        return ref[start : start + 16, :]

    def box_rows(ox, oy, px, py):
        weights = []
        for m, (dx, dy) in enumerate(FACES):
            bx, nx = divmod(2 * ox + px + dx, 2)
            by, ny = divmod(2 * oy + py + dy, 2)
            state = state_row(bx, by, nx, ny)
            if m == 5:
                state = swap_halves(state)
            rows = []
            for kind in range(3):
                weight = jnp.where(state == kind, 1.0, 0.0)
                if m > 0:
                    weight = weight * link_row(ox, oy, px, py, m)
                rows.append(jnp.broadcast_to(weight, (16, PAIR)))
            weights.append(rows)
        reach = targets(px, py)
        chunks = {t: [] for t in box_set(px, py)}
        for chunk in range(4):
            values = [block(ox, oy, px, py, m, chunk).astype(jnp.float32) for m in range(SLOTS)]
            for t in chunks:
                total = None
                for m in range(SLOTS):
                    for kind in range(3):
                        if reach[m][kind] == t:
                            term = values[m] * weights[m][kind]
                            total = term if total is None else total + term
                chunks[t].append(total)
        return {t: jnp.concatenate(parts, axis=0) for t, parts in chunks.items()}

    images = {column: image_set(*column) for column in COLUMNS}
    users = {}
    for index, column in enumerate(COLUMNS):
        for place, (_, box, other) in enumerate(around(*column)):
            users.setdefault((box, other), []).append((index, column, place))
            reached = {(box[0] + tx, box[1] + ty) for tx, ty in box_set(*other)}
            for position, s in enumerate(images[column]):
                if s not in reached:
                    right[index, place * B : (place + 1) * B, position * PAIR : (position + 1) * PAIR] = jnp.zeros(
                        (B, PAIR), jnp.bfloat16
                    )
    for (box, other), uses in users.items():
        found = box_rows(*box, *other)
        own = COLUMNS.index(other)
        for t, value in found.items():
            rounded = value.astype(jnp.bfloat16)
            for index, column, place in uses:
                position = images[column].index((box[0] + t[0], box[1] + t[1]))
                stored = swap_halves(value).astype(jnp.bfloat16) if place == 5 else rounded
                right[index, place * B : (place + 1) * B, position * PAIR : (position + 1) * PAIR] = stored
            if box == (0, 0):
                turned = value.T
                turned = pair_lanes(turned[:B], turned[B:]).astype(jnp.bfloat16)
                if t in STAR:
                    left_star[STAR.index(t) * B : (STAR.index(t) + 1) * B, own * PAIR : (own + 1) * PAIR] = turned
                else:
                    left_corner[own] = turned
    half = low_half((B, PAIR))
    for index, column in enumerate(COLUMNS):
        product = jnp.dot(a_ref[index], right[index], preferred_element_type=jnp.float32)

        def part(s, z):
            if s not in images[column]:
                return jnp.zeros((B, PAIR), jnp.float32)
            position = images[column].index(s)
            return product[z * B : (z + 1) * B, position * PAIR : (position + 1) * PAIR]

        for pair in range(IMAGE_PAIRS):
            one = IMAGE[2 * pair]
            two = IMAGE[2 * pair + 1] if 2 * pair + 1 < len(IMAGE) else None
            low = jnp.where(half, part(one, 0), swap_halves(part(two, 0)))
            high = jnp.where(half, swap_halves(part(one, 1)), part(two, 1))
            start = index * PAIR
            lanes = slice(pair * PAIR, (pair + 1) * PAIR)
            image[start : start + B, lanes] = low.astype(jnp.bfloat16)
            image[start + B : start + PAIR, lanes] = high.astype(jnp.bfloat16)
    folded_half = low_half((HALF, PAIR))

    def fold(product):
        blocks = {}
        for pair in range(IMAGE_PAIRS):
            tile = product[:, pair * PAIR : (pair + 1) * PAIR]
            top, bottom = tile[:HALF], tile[HALF:]
            blocks[IMAGE[2 * pair]] = jnp.where(folded_half, top, swap_halves(bottom))
            if 2 * pair + 1 < len(IMAGE):
                blocks[IMAGE[2 * pair + 1]] = jnp.where(folded_half, swap_halves(top), bottom)
        return blocks

    def contribution(t):
        if t in STAR:
            rows = STAR.index(t) * B
            product = jnp.dot(left_star[rows : rows + B, :], image[...], preferred_element_type=jnp.float32)
        else:
            index = COLUMNS.index(column_of(*t))
            product = jnp.dot(
                left_corner[index], image[index * PAIR : (index + 1) * PAIR, :], preferred_element_type=jnp.float32
            )
        return fold(product)

    for ref, sent in (
        (to_y_first, TO_Y_FIRST),
        (to_y_second, TO_Y_SECOND),
        (to_c_first, TO_C_FIRST),
        (to_c_second, TO_C_SECOND),
    ):
        parts = {t: contribution(t) for t in sorted({t for t, _ in sent})}
        for row, (t, s) in enumerate(sent):
            ref[row * HALF : (row + 1) * HALF, :] = parts[t][s].astype(jnp.bfloat16)
    for group, tx in enumerate((0, -1, 1)):
        parts = contribution((tx, 0))
        for position, s in enumerate(IMAGE):
            rest_ref[group, position] = parts[s]
    for copy in copies:
        copy.wait()


def message_block(ref, row):
    return ref[row * HALF : (row + 1) * HALF, :].astype(jnp.float32)


def relay_kernel(rest_ref, y_first, x_first, x_second):
    for ref, tx in ((x_first, 1), (x_second, -1)):
        arrived = relayed(tx)
        for row, s in enumerate(TO_X[tx]):
            value = None
            if s in IMAGE:
                value = rest_ref[(0, -1, 1).index(tx), IMAGE.index(s)]
            if s in arrived:
                more = message_block(y_first, arrived[s])
                value = more if value is None else value + more
            ref[row * HALF : (row + 1) * HALF, :] = value.astype(jnp.bfloat16)


def gathered(terms):
    total = None
    for ref, row, flag in terms:
        value = message_block(ref, row) if row is not None else ref
        if flag is not None:
            value = value * flag
        total = value if total is None else total + value
    return total


def inside():
    x, y = lax.axis_index("sx"), lax.axis_index("sy")
    return (
        ((x > 0) & (x < lax.axis_size("sx") - 1)).astype(jnp.float32),
        ((y > 0) & (y < lax.axis_size("sy") - 1)).astype(jnp.float32),
    )


def own_kernel(rest_ref, y_first, y_second, c_first, c_second, own_ref):
    has_x, has_y = inside()
    terms = {block: [] for block in STENCIL}
    for position, s in enumerate(IMAGE):
        terms[s].append((rest_ref[0, position], None, None))
    for s, row in relayed(0).items():
        terms[s].append((y_first, row, None))
    for row, (_, s) in enumerate(TO_Y_SECOND):
        terms[s[0], -1 - s[1]].append((y_second, row, has_y))
    for row, (_, s) in enumerate(TO_C_FIRST):
        terms[1 - s[0], -1 - s[1]].append((c_first, row, has_y))
    for row, (_, s) in enumerate(TO_C_SECOND):
        terms[-1 - s[0], -1 - s[1]].append((c_second, row, has_x * has_y))
    for position, block in enumerate(OWN):
        own_ref[position] = gathered(terms[block])


def finish_kernel(own_ref, x_first, x_second, _, out_hbm, rows, sems):
    odd_x, odd_y = mirrored()
    has_x, _ = inside()
    terms = {block: [] for block in STENCIL}
    for position, block in enumerate(OWN):
        terms[block].append((own_ref[position], None, None))
    for row, s in enumerate(TO_X[1]):
        terms[1 - s[0], s[1]].append((x_first, row, None))
    for row, s in enumerate(TO_X[-1]):
        terms[-1 - s[0], s[1]].append((x_second, row, has_x))
    copies = []
    for jx in (0, 1, -1, 2, -2, 3, -3):
        row_here = jnp.where(odd_x == 1, 3 - jx, 3 + jx)
        reach = 3 - abs(jx)
        for jy in range(-reach, reach + 1):
            value = gathered(terms[jx, jy])
            column_here = jnp.where(odd_y == 1, 3 - jy, 3 + jy)
            rows[jx + 3, column_here, 0:HALF, :] = value[:, :B].astype(jnp.bfloat16)
            rows[jx + 3, column_here, HALF:B, :] = swap_halves(value)[:, :B].astype(jnp.bfloat16)
        span = pl.ds(3 - reach, 2 * reach + 1)
        copy = pltpu.make_async_copy(rows.at[jx + 3, span], out_hbm.at[row_here, span], sems.at[jx + 3])
        copy.start()
        copies.append(copy)
    for copy in copies:
        copy.wait()


def swapped(value, move_x, move_y):
    count_x, count_y = lax.axis_size("sx"), lax.axis_size("sy")

    def partner(index, move, count):
        if move == 0:
            return index
        found = index ^ 1 if move == 1 else ((index + 1) ^ 1) - 1
        return found if 0 <= found < count else None

    pairs = []
    for x in range(count_x):
        for y in range(count_y):
            to_x, to_y = partner(x, move_x, count_x), partner(y, move_y, count_y)
            if to_x is None and to_y is None:
                to_x, to_y = x, count_y - 1 - y
            elif to_x is None:
                to_x, to_y = x, (y ^ 1 if move_y == 0 else to_y)
            elif to_y is None:
                to_x, to_y = (x ^ 1 if move_x == 0 else to_x), y
            pairs.append((x * count_y + y, to_x * count_y + to_y))
    return lax.ppermute(value, ("sx", "sy"), pairs)


SMEM = pl.BlockSpec(memory_space=pltpu.SMEM)
VMEM = pl.BlockSpec(memory_space=pltpu.VMEM)
HBM = pl.BlockSpec(memory_space=pltpu.HBM)


def call(kernel, in_specs, outs, scratch=(), out_specs=None, aliases=None, cost=None):
    return pl.pallas_call(
        kernel,
        out_shape=[jax.ShapeDtypeStruct(shape, dtype) for shape, dtype in outs],
        in_specs=in_specs,
        out_specs=out_specs or [VMEM] * len(outs),
        scratch_shapes=list(scratch),
        input_output_aliases=aliases or {},
        compiler_params=pltpu.CompilerParams(vmem_limit_bytes=VMEM_LIMIT),
        cost_estimate=None if cost is None else pl.CostEstimate(flops=cost, bytes_accessed=1, transcendentals=0),
    )


def per_device(fine_matrix, prolongator, aggregate, face_links):
    bf16, f32 = jnp.bfloat16, jnp.float32
    message = ((BODY + TAIL, PAIR), bf16)
    rows, meta, x_first, x_second, y_first, y_second = call(
        functools.partial(pack_kernel, lax.axis_size("sy")),
        [HBM, HBM, HBM],
        [((4, BLOCK_ROWS, PAIR), bf16), ((32, PAIR), f32), message, message, message, message],
        [
            pltpu.VMEM((4, 2, 7, B, B), bf16),
            pltpu.SMEM((2, 2, 2), jnp.int32),
            pltpu.SMEM((2, 2, 2, 6), jnp.int32),
            pltpu.SemaphoreType.DMA((4,)),
            pltpu.SemaphoreType.DMA((2,)),
        ],
    )(*(pltpu.with_memory_space_constraint(value, pltpu.HBM) for value in (aggregate, face_links, prolongator)))
    y_second = swapped(y_second, 0, 2)
    x_first, x_second = swapped(x_first, 1, 0), swapped(x_second, 2, 0)
    y_first = swapped(y_first, 0, 1)
    notes = jnp.concatenate([x_first[BODY:], x_second[BODY:]], axis=0)
    c_first, c_second = swapped(notes, 0, 1), swapped(notes, 0, 2)
    (matrix,) = call(pack_matrix_kernel, [SMEM, VMEM], [((4, PAIR, 6 * B), bf16)])(face_links, fine_matrix)
    whole = ((7, 7, B, B), bf16)

    def sent(blocks):
        return ((len(blocks) * HALF, PAIR), bf16)

    y_first, y_second, c_first, c_second, rest, out = call(
        main_kernel,
        [VMEM] * 9,
        [
            sent(TO_Y_FIRST),
            sent(TO_Y_SECOND),
            sent(TO_C_FIRST),
            sent(TO_C_SECOND),
            ((3, len(IMAGE), HALF, PAIR), f32),
            whole,
        ],
        [
            pltpu.VMEM((4, 6 * B, 10 * PAIR), bf16),
            pltpu.VMEM((4 * PAIR, IMAGE_PAIRS * PAIR), bf16),
            pltpu.VMEM((len(STAR) * B, 4 * PAIR), bf16),
            pltpu.VMEM((4, B, PAIR), bf16),
            pltpu.VMEM((3, B, B), bf16),
            pltpu.SemaphoreType.DMA((12,)),
        ],
        [VMEM] * 5 + [HBM],
    )(matrix, rows, meta, x_first, x_second, y_first, y_second, c_first, c_second)
    y_second = swapped(y_second, 0, 2)
    c_first, c_second = swapped(c_first, 1, 2), swapped(c_second, 2, 2)
    y_first = swapped(y_first, 0, 1)
    x_first, x_second = call(relay_kernel, [VMEM] * 2, [sent(TO_X[1]), sent(TO_X[-1])])(rest, y_first)
    x_first, x_second = swapped(x_first, 1, 0), swapped(x_second, 2, 0)
    (own,) = call(own_kernel, [VMEM] * 5, [((len(OWN), HALF, PAIR), f32)], cost=3_000_000_000)(
        rest, y_first, y_second, c_first, c_second
    )
    (out,) = call(
        finish_kernel,
        [VMEM] * 3 + [HBM],
        [whole],
        [pltpu.VMEM((7, 7, B, B), bf16), pltpu.SemaphoreType.DMA((7,))],
        [HBM],
        {3: 0},
    )(own, x_first, x_second, out)
    return out[None, None]


def solution(mesh):
    return jax.shard_map(
        per_device,
        mesh=mesh,
        in_specs=(
            P("sx", "sy", None, None, None, None),
            P("sx", "sy", None, None, None, None),
            P("sx", "sy", None),
            P("sx", "sy", None, None),
        ),
        out_specs=P("sx", "sy", None, None, None, None),
        check_vma=False,
    )
```

```python
import functools

import jax
import jax.numpy as jnp
from jax import lax
from jax.experimental import pallas as pl
from jax.experimental.pallas import tpu as pltpu
from jax.sharding import PartitionSpec as P


B = 64
HALF = B // 2
PAIR = 2 * B
SLOTS = 6
BLOCK_ROWS = SLOTS * B
BODY = 2 * BLOCK_ROWS
TAIL = 16
VMEM_LIMIT = 48 * 1024 * 1024

FACES = [(0, 0), (-1, 0), (1, 0), (0, -1), (0, 1), (0, 0)]
COLUMNS = [(0, 0), (0, 1), (1, 0), (1, 1)]
SIDES_X = (0, 2, 1, 3, 4, 5)
SIDES_Y = (0, 1, 2, 4, 3, 5)


def targets(px, py):
    table = []
    for dx, dy in FACES:
        ox, nx = divmod(px + dx, 2)
        oy, ny = divmod(py + dy, 2)
        table.append([(ox, oy), (ox + 2 * nx - 1, oy), (ox, oy + 2 * ny - 1)])
    return table


def box_set(px, py):
    return sorted({t for row in targets(px, py) for t in row})


def around(px, py):
    found = [(0, (0, 0), (px, py))]
    for m in (2, 1) if px == 0 else (1, 2):
        ox, nx = divmod(px + FACES[m][0], 2)
        found.append((m, (ox, 0), (nx, py)))
    for m in (4, 3) if py == 0 else (3, 4):
        oy, ny = divmod(py + FACES[m][1], 2)
        found.append((m, (0, oy), (px, ny)))
    found.append((5, (0, 0), (px, py)))
    return found


def image_set(px, py):
    found = set()
    for _, (ox, oy), column in around(px, py):
        found |= {(ox + tx, oy + ty) for tx, ty in box_set(*column)}
    return sorted(found)


IMAGE = sorted({s for column in COLUMNS for s in image_set(*column)})
IMAGE_PAIRS = (len(IMAGE) + 1) // 2
STAR = [(0, 1), (0, -1), (0, 0), (1, 0), (-1, 0)]


def column_of(tx, ty):
    return ((tx + 1) // 2, (ty + 1) // 2)


def blocks_of(tx, ty):
    return IMAGE if (tx, ty) in STAR else image_set(*column_of(tx, ty))


TO_Y_FIRST = [((tx, 1), s) for tx in (0, -1, 1) for s in blocks_of(tx, 1)]
TO_Y_SECOND = [((0, -1), s) for s in blocks_of(0, -1)]
TO_C_FIRST = [((1, -1), s) for s in blocks_of(1, -1)]
TO_C_SECOND = [((-1, -1), s) for s in blocks_of(-1, -1)]


def relayed(tx):
    return {(s[0], 1 - s[1]): row for row, (t, s) in enumerate(TO_Y_FIRST) if t[0] == tx}


TO_X = {tx: sorted(set(IMAGE) | set(relayed(tx))) for tx in (1, -1)}
STENCIL = [(jx, jy) for jx in range(-3, 4) for jy in range(-3, 4) if abs(jx) + abs(jy) <= 3]
OWN = sorted(
    set(IMAGE)
    | set(relayed(0))
    | {(s[0], -1 - s[1]) for _, s in TO_Y_SECOND}
    | {(1 - s[0], -1 - s[1]) for _, s in TO_C_FIRST}
    | {(-1 - s[0], -1 - s[1]) for _, s in TO_C_SECOND}
)


def low_half(shape):
    return lax.broadcasted_iota(jnp.int32, shape, len(shape) - 1) < B


def swap_halves(value):
    return pltpu.roll(value, B, value.ndim - 1)


def pair_lanes(left, right):
    return jnp.concatenate([left, right], axis=-1)


def mirrored():
    return lax.axis_index("sx") % 2, lax.axis_index("sy") % 2


def slot_here(m, z, odd_x, odd_y):
    if m in (1, 2):
        return jnp.where(odd_x == 1, 3 - m, m)
    if m in (3, 4):
        return jnp.where(odd_y == 1, 7 - m, m)
    return 6 - z if m == 5 else m


def fill_rows(rows, values):
    shape = (rows, PAIR)
    row = lax.broadcasted_iota(jnp.int32, shape, 0)
    half = low_half(shape)
    filled = jnp.zeros(shape, jnp.float32)
    for index, (low, high) in enumerate(values):
        filled = jnp.where(row == index, jnp.where(half, low, high), filled)
    return filled


def pack_kernel(
    boxes_y,
    aggregate_hbm,
    links_hbm,
    p_hbm,
    rows_ref,
    meta_ref,
    x_first,
    x_second,
    y_first,
    y_second,
    p_ref,
    aggregate_ref,
    links_ref,
    p_sems,
    sems,
):
    odd_x, odd_y = mirrored()
    own = lax.axis_index("sx") * boxes_y + lax.axis_index("sy")
    place = {(px, py): (px ^ odd_x, py ^ odd_y) for px, py in COLUMNS}
    copies = [
        pltpu.make_async_copy(p_hbm.at[place[column]], p_ref.at[index], p_sems.at[index])
        for index, column in enumerate(COLUMNS)
    ]
    small = [
        pltpu.make_async_copy(aggregate_hbm, aggregate_ref, sems.at[0]),
        pltpu.make_async_copy(links_hbm, links_ref, sems.at[1]),
    ]
    for copy in small + copies:
        copy.start()
    for copy in small:
        copy.wait()

    def state(column, z):
        shift = aggregate_ref[place[column] + (z,)] - own
        across_x = (shift == boxes_y) | (shift == -boxes_y)
        return jnp.where(shift == 0, 0, jnp.where(across_x, 1, 2)).astype(jnp.float32)

    def link(column, m):
        faces = [slot_here(m, z, odd_x, odd_y) - 1 for z in (0, 1)]
        return tuple(links_ref[place[column] + (z, faces[z])].astype(jnp.float32) for z in (0, 1))

    states = [tuple(state(column, z) for z in (0, 1)) for column in COLUMNS]
    links = {column: [link(column, m) for m in range(1, SLOTS)] for column in COLUMNS}
    meta_ref[...] = fill_rows(32, states + sum((links[column] for column in COLUMNS), []))
    messages = (
        (x_first, ((1, 0), (1, 1))),
        (x_second, ((0, 0), (0, 1))),
        (y_first, ((0, 1), (1, 1))),
        (y_second, ((0, 0), (1, 0))),
    )
    for ref, columns in messages:
        tail = fill_rows(TAIL, states + links[columns[0]] + links[columns[1]])
        ref[BODY : BODY + TAIL, :] = tail.astype(jnp.bfloat16)
    for index, column in enumerate(COLUMNS):
        copies[index].wait()
        for m in range(SLOTS):
            packed = pair_lanes(*(p_ref[index, z, slot_here(m, z, odd_x, odd_y)] for z in (0, 1)))
            rows_ref[index, m * B : (m + 1) * B, :] = packed
            for ref, columns in messages:
                if column in columns:
                    start = columns.index(column) * BLOCK_ROWS + m * B
                    ref[start : start + B, :] = packed


def pack_matrix_kernel(links_ref, a_ref, out_ref, whole_hbm, zeros, sems):
    zeros[...] = jnp.zeros(zeros.shape, zeros.dtype)
    copies = []
    for jx in range(-3, 4):
        width = abs(jx)
        if width:
            for start in (0, 7 - width):
                copies.append(
                    pltpu.make_async_copy(
                        zeros.at[pl.ds(0, width)], whole_hbm.at[jx + 3, pl.ds(start, width)], sems.at[len(copies)]
                    )
                )
    for copy in copies:
        copy.start()
    odd_x, odd_y = mirrored()
    for index, (px, py) in enumerate(COLUMNS):
        place = (px ^ odd_x, py ^ odd_y)
        for z in (0, 1):
            blocks = []
            for m, _, _ in around(px, py):
                slot = slot_here(m, z, odd_x, odd_y)
                block = a_ref[place + (z, slot)]
                if m > 0:
                    present = links_ref[place + (z, slot - 1)] == 1
                    block = jnp.where(present, block, jnp.zeros_like(block))
                blocks.append(block)
            for pair in range(3):
                out_ref[index, z * B : (z + 1) * B, pair * PAIR : (pair + 1) * PAIR] = pair_lanes(
                    blocks[2 * pair], blocks[2 * pair + 1]
                )
    for copy in copies:
        copy.wait()


def main_kernel(
    a_ref,
    rows_ref,
    meta_ref,
    x_first,
    x_second,
    y_first,
    y_second,
    c_first,
    c_second,
    to_y_first,
    to_y_second,
    to_c_first,
    to_c_second,
    rest_ref,
    right,
    image,
    left_star,
    left_corner,
):
    from_x = {1: x_first, -1: x_second}
    from_y = {1: y_first, -1: y_second}
    notes = {(0, 0): meta_ref[...]}
    corner_notes = {}
    for side in (-1, 1):
        notes[side, 0] = from_x[side][BODY : BODY + TAIL, :].astype(jnp.float32)
        notes[0, side] = from_y[side][BODY : BODY + TAIL, :].astype(jnp.float32)
    for ref, oy in ((c_first, 1), (c_second, -1)):
        corner_notes[1, oy] = ref[0:TAIL, :].astype(jnp.float32)
        corner_notes[-1, oy] = ref[TAIL : 2 * TAIL, :].astype(jnp.float32)

    def there(ox, oy, px, py):
        return (1 - px if ox else px, 1 - py if oy else py)

    def slot_there(ox, oy, m):
        m = SIDES_X[m] if ox else m
        return SIDES_Y[m] if oy else m

    def state_row(ox, oy, px, py):
        index = COLUMNS.index(there(ox, oy, px, py))
        note = corner_notes[ox, oy] if ox and oy else notes[ox, oy]
        return note[index : index + 1]

    def link_row(ox, oy, px, py, m):
        if (ox, oy) == (0, 0):
            index = (SLOTS - 1) * COLUMNS.index((px, py))
        else:
            index = (SLOTS - 1) * (py if ox else px)
        index += 4 + slot_there(ox, oy, m) - 1
        return notes[ox, oy][index : index + 1]

    def block(ox, oy, px, py, m, chunk):
        start = slot_there(ox, oy, m) * B + chunk * 16
        if (ox, oy) == (0, 0):
            return rows_ref[COLUMNS.index((px, py)), start : start + 16, :]
        start += (py if ox else px) * BLOCK_ROWS
        ref = from_x[ox] if ox else from_y[oy]
        return ref[start : start + 16, :]

    def box_rows(ox, oy, px, py):
        weights = []
        for m, (dx, dy) in enumerate(FACES):
            bx, nx = divmod(2 * ox + px + dx, 2)
            by, ny = divmod(2 * oy + py + dy, 2)
            state = state_row(bx, by, nx, ny)
            if m == 5:
                state = swap_halves(state)
            rows = []
            for kind in range(3):
                weight = jnp.where(state == kind, 1.0, 0.0)
                if m > 0:
                    weight = weight * link_row(ox, oy, px, py, m)
                rows.append(jnp.broadcast_to(weight, (16, PAIR)))
            weights.append(rows)
        reach = targets(px, py)
        chunks = {t: [] for t in box_set(px, py)}
        for chunk in range(4):
            values = [block(ox, oy, px, py, m, chunk).astype(jnp.float32) for m in range(SLOTS)]
            for t in chunks:
                total = None
                for m in range(SLOTS):
                    for kind in range(3):
                        if reach[m][kind] == t:
                            term = values[m] * weights[m][kind]
                            total = term if total is None else total + term
                chunks[t].append(total)
        return {t: jnp.concatenate(parts, axis=0) for t, parts in chunks.items()}

    images = {column: image_set(*column) for column in COLUMNS}
    users = {}
    for index, column in enumerate(COLUMNS):
        for place, (_, box, other) in enumerate(around(*column)):
            users.setdefault((box, other), []).append((index, column, place))
            reached = {(box[0] + tx, box[1] + ty) for tx, ty in box_set(*other)}
            for position, s in enumerate(images[column]):
                if s not in reached:
                    right[index, place * B : (place + 1) * B, position * PAIR : (position + 1) * PAIR] = jnp.zeros(
                        (B, PAIR), jnp.bfloat16
                    )
    square = (PAIR, PAIR)
    diagonal = lax.broadcasted_iota(jnp.int32, square, 0) == lax.broadcasted_iota(jnp.int32, square, 1)
    unit = jnp.where(diagonal, 1.0, 0.0).astype(jnp.bfloat16)
    for (box, other), uses in users.items():
        found = box_rows(*box, *other)
        own = COLUMNS.index(other)
        for t, value in found.items():
            rounded = value.astype(jnp.bfloat16)
            for index, column, place in uses:
                position = images[column].index((box[0] + t[0], box[1] + t[1]))
                stored = swap_halves(value).astype(jnp.bfloat16) if place == 5 else rounded
                right[index, place * B : (place + 1) * B, position * PAIR : (position + 1) * PAIR] = stored
            if box == (0, 0):
                turned = lax.dot_general(
                    unit, rounded, (((1,), (1,)), ((), ())), preferred_element_type=jnp.float32
                ).astype(jnp.bfloat16)
                turned = pair_lanes(turned[:B], turned[B:])
                if t in STAR:
                    left_star[STAR.index(t) * B : (STAR.index(t) + 1) * B, own * PAIR : (own + 1) * PAIR] = turned
                else:
                    left_corner[own] = turned
    half = low_half((B, PAIR))
    for index, column in enumerate(COLUMNS):
        product = jnp.dot(a_ref[index], right[index], preferred_element_type=jnp.float32)

        def part(s, z):
            if s not in images[column]:
                return jnp.zeros((B, PAIR), jnp.float32)
            position = images[column].index(s)
            return product[z * B : (z + 1) * B, position * PAIR : (position + 1) * PAIR]

        for pair in range(IMAGE_PAIRS):
            one = IMAGE[2 * pair]
            two = IMAGE[2 * pair + 1] if 2 * pair + 1 < len(IMAGE) else None
            low = jnp.where(half, part(one, 0), swap_halves(part(two, 0)))
            high = jnp.where(half, swap_halves(part(one, 1)), part(two, 1))
            start = index * PAIR
            lanes = slice(pair * PAIR, (pair + 1) * PAIR)
            image[start : start + B, lanes] = low.astype(jnp.bfloat16)
            image[start + B : start + PAIR, lanes] = high.astype(jnp.bfloat16)
    folded_half = low_half((HALF, PAIR))

    def fold(product):
        blocks = {}
        for pair in range(IMAGE_PAIRS):
            tile = product[:, pair * PAIR : (pair + 1) * PAIR]
            top, bottom = tile[:HALF], tile[HALF:]
            blocks[IMAGE[2 * pair]] = jnp.where(folded_half, top, swap_halves(bottom))
            if 2 * pair + 1 < len(IMAGE):
                blocks[IMAGE[2 * pair + 1]] = jnp.where(folded_half, swap_halves(top), bottom)
        return blocks

    star = jnp.dot(left_star[...], image[...], preferred_element_type=jnp.float32)

    def contribution(t):
        if t in STAR:
            return fold(star[STAR.index(t) * B : (STAR.index(t) + 1) * B])
        index = COLUMNS.index(column_of(*t))
        return fold(
            jnp.dot(
                left_corner[index], image[index * PAIR : (index + 1) * PAIR, :], preferred_element_type=jnp.float32
            )
        )

    for ref, sent in (
        (to_y_first, TO_Y_FIRST),
        (to_y_second, TO_Y_SECOND),
        (to_c_first, TO_C_FIRST),
        (to_c_second, TO_C_SECOND),
    ):
        parts = {t: contribution(t) for t in sorted({t for t, _ in sent})}
        for row, (t, s) in enumerate(sent):
            ref[row * HALF : (row + 1) * HALF, :] = parts[t][s].astype(jnp.bfloat16)
    for group, tx in enumerate((0, -1, 1)):
        parts = contribution((tx, 0))
        for position, s in enumerate(IMAGE):
            rest_ref[group, position] = parts[s]


def message_block(ref, row):
    return ref[row * HALF : (row + 1) * HALF, :].astype(jnp.float32)


def relay_kernel(rest_ref, y_first, x_first, x_second):
    for ref, tx in ((x_first, 1), (x_second, -1)):
        arrived = relayed(tx)
        for row, s in enumerate(TO_X[tx]):
            value = None
            if s in IMAGE:
                value = rest_ref[(0, -1, 1).index(tx), IMAGE.index(s)]
            if s in arrived:
                more = message_block(y_first, arrived[s])
                value = more if value is None else value + more
            ref[row * HALF : (row + 1) * HALF, :] = value.astype(jnp.bfloat16)


def gathered(terms):
    total = None
    for ref, row, flag in terms:
        value = message_block(ref, row) if row is not None else ref
        if flag is not None:
            value = value * flag
        total = value if total is None else total + value
    return total


def inside():
    x, y = lax.axis_index("sx"), lax.axis_index("sy")
    return (
        ((x > 0) & (x < lax.axis_size("sx") - 1)).astype(jnp.float32),
        ((y > 0) & (y < lax.axis_size("sy") - 1)).astype(jnp.float32),
    )


def own_kernel(rest_ref, y_first, y_second, c_first, c_second, own_ref):
    has_x, has_y = inside()
    terms = {block: [] for block in STENCIL}
    for position, s in enumerate(IMAGE):
        terms[s].append((rest_ref[0, position], None, None))
    for s, row in relayed(0).items():
        terms[s].append((y_first, row, None))
    for row, (_, s) in enumerate(TO_Y_SECOND):
        terms[s[0], -1 - s[1]].append((y_second, row, has_y))
    for row, (_, s) in enumerate(TO_C_FIRST):
        terms[1 - s[0], -1 - s[1]].append((c_first, row, has_y))
    for row, (_, s) in enumerate(TO_C_SECOND):
        terms[-1 - s[0], -1 - s[1]].append((c_second, row, has_x * has_y))
    for position, block in enumerate(OWN):
        own_ref[position] = gathered(terms[block])


def finish_kernel(own_ref, x_first, x_second, _, out_hbm, rows, sems):
    odd_x, odd_y = mirrored()
    has_x, _ = inside()
    terms = {block: [] for block in STENCIL}
    for position, block in enumerate(OWN):
        terms[block].append((own_ref[position], None, None))
    for row, s in enumerate(TO_X[1]):
        terms[1 - s[0], s[1]].append((x_first, row, None))
    for row, s in enumerate(TO_X[-1]):
        terms[-1 - s[0], s[1]].append((x_second, row, has_x))
    copies = []
    for jx in (0, 1, -1, 2, -2, 3, -3):
        row_here = jnp.where(odd_x == 1, 3 - jx, 3 + jx)
        reach = 3 - abs(jx)
        for jy in range(-reach, reach + 1):
            value = gathered(terms[jx, jy])
            column_here = jnp.where(odd_y == 1, 3 - jy, 3 + jy)
            rows[jx + 3, column_here, 0:HALF, :] = value[:, :B].astype(jnp.bfloat16)
            rows[jx + 3, column_here, HALF:B, :] = swap_halves(value)[:, :B].astype(jnp.bfloat16)
        span = pl.ds(3 - reach, 2 * reach + 1)
        copy = pltpu.make_async_copy(rows.at[jx + 3, span], out_hbm.at[row_here, span], sems.at[jx + 3])
        copy.start()
        copies.append(copy)
    for copy in copies:
        copy.wait()


def swapped(value, move_x, move_y):
    count_x, count_y = lax.axis_size("sx"), lax.axis_size("sy")

    def partner(index, move, count):
        if move == 0:
            return index
        found = index ^ 1 if move == 1 else ((index + 1) ^ 1) - 1
        return found if 0 <= found < count else None

    pairs = []
    for x in range(count_x):
        for y in range(count_y):
            to_x, to_y = partner(x, move_x, count_x), partner(y, move_y, count_y)
            if to_x is None and to_y is None:
                to_x, to_y = x, count_y - 1 - y
            elif to_x is None:
                to_x, to_y = x, (y ^ 1 if move_y == 0 else to_y)
            elif to_y is None:
                to_x, to_y = (x ^ 1 if move_x == 0 else to_x), y
            pairs.append((x * count_y + y, to_x * count_y + to_y))
    return lax.ppermute(value, ("sx", "sy"), pairs)


SMEM = pl.BlockSpec(memory_space=pltpu.SMEM)
VMEM = pl.BlockSpec(memory_space=pltpu.VMEM)
HBM = pl.BlockSpec(memory_space=pltpu.HBM)


def call(kernel, in_specs, outs, scratch=(), out_specs=None, aliases=None, cost=None):
    return pl.pallas_call(
        kernel,
        out_shape=[jax.ShapeDtypeStruct(shape, dtype) for shape, dtype in outs],
        in_specs=in_specs,
        out_specs=out_specs or [VMEM] * len(outs),
        scratch_shapes=list(scratch),
        input_output_aliases=aliases or {},
        compiler_params=pltpu.CompilerParams(vmem_limit_bytes=VMEM_LIMIT),
        cost_estimate=None if cost is None else pl.CostEstimate(flops=cost, bytes_accessed=1, transcendentals=0),
    )


def per_device(fine_matrix, prolongator, aggregate, face_links):
    bf16, f32 = jnp.bfloat16, jnp.float32
    message = ((BODY + TAIL, PAIR), bf16)
    rows, meta, x_first, x_second, y_first, y_second = call(
        functools.partial(pack_kernel, lax.axis_size("sy")),
        [HBM, HBM, HBM],
        [((4, BLOCK_ROWS, PAIR), bf16), ((32, PAIR), f32), message, message, message, message],
        [
            pltpu.VMEM((4, 2, 7, B, B), bf16),
            pltpu.SMEM((2, 2, 2), jnp.int32),
            pltpu.SMEM((2, 2, 2, 6), jnp.int32),
            pltpu.SemaphoreType.DMA((4,)),
            pltpu.SemaphoreType.DMA((2,)),
        ],
    )(*(pltpu.with_memory_space_constraint(value, pltpu.HBM) for value in (aggregate, face_links, prolongator)))
    y_second = swapped(y_second, 0, 2)
    x_first, x_second = swapped(x_first, 1, 0), swapped(x_second, 2, 0)
    y_first = swapped(y_first, 0, 1)
    notes = jnp.concatenate([x_first[BODY:], x_second[BODY:]], axis=0)
    c_first, c_second = swapped(notes, 0, 1), swapped(notes, 0, 2)
    whole = ((7, 7, B, B), bf16)
    matrix, out = call(
        pack_matrix_kernel,
        [SMEM, VMEM],
        [((4, PAIR, 6 * B), bf16), whole],
        [pltpu.VMEM((3, B, B), bf16), pltpu.SemaphoreType.DMA((12,))],
        [VMEM, HBM],
    )(face_links, fine_matrix)

    def sent(blocks):
        return ((len(blocks) * HALF, PAIR), bf16)

    y_first, y_second, c_first, c_second, rest = call(
        main_kernel,
        [VMEM] * 9,
        [
            sent(TO_Y_FIRST),
            sent(TO_Y_SECOND),
            sent(TO_C_FIRST),
            sent(TO_C_SECOND),
            ((3, len(IMAGE), HALF, PAIR), f32),
        ],
        [
            pltpu.VMEM((4, 6 * B, 10 * PAIR), bf16),
            pltpu.VMEM((4 * PAIR, IMAGE_PAIRS * PAIR), bf16),
            pltpu.VMEM((len(STAR) * B, 4 * PAIR), bf16),
            pltpu.VMEM((4, B, PAIR), bf16),
        ],
    )(matrix, rows, meta, x_first, x_second, y_first, y_second, c_first, c_second)
    y_second = swapped(y_second, 0, 2)
    c_first, c_second = swapped(c_first, 1, 2), swapped(c_second, 2, 2)
    y_first = swapped(y_first, 0, 1)
    x_first, x_second = call(relay_kernel, [VMEM] * 2, [sent(TO_X[1]), sent(TO_X[-1])])(rest, y_first)
    x_first, x_second = swapped(x_first, 1, 0), swapped(x_second, 2, 0)
    (own,) = call(own_kernel, [VMEM] * 5, [((len(OWN), HALF, PAIR), f32)], cost=3_000_000_000)(
        rest, y_first, y_second, c_first, c_second
    )
    (out,) = call(
        finish_kernel,
        [VMEM] * 3 + [HBM],
        [whole],
        [pltpu.VMEM((7, 7, B, B), bf16), pltpu.SemaphoreType.DMA((7,))],
        [HBM],
        {3: 0},
    )(own, x_first, x_second, out)
    return out[None, None]


def solution(mesh):
    return jax.shard_map(
        per_device,
        mesh=mesh,
        in_specs=(
            P("sx", "sy", None, None, None, None),
            P("sx", "sy", None, None, None, None),
            P("sx", "sy", None),
            P("sx", "sy", None, None),
        ),
        out_specs=P("sx", "sy", None, None, None, None),
        check_vma=False,
    )
```

```python
import functools

import jax
import jax.numpy as jnp
from jax import lax
from jax.experimental import pallas as pl
from jax.experimental.pallas import tpu as pltpu
from jax.sharding import PartitionSpec as P


B = 64
HALF = B // 2
PAIR = 2 * B
SLOTS = 6
BLOCK_ROWS = SLOTS * B
BODY = 2 * BLOCK_ROWS
TAIL = 16
VMEM_LIMIT = 20 * 1024 * 1024

FACES = [(0, 0), (-1, 0), (1, 0), (0, -1), (0, 1), (0, 0)]
COLUMNS = [(0, 0), (0, 1), (1, 0), (1, 1)]
SIDES_X = (0, 2, 1, 3, 4, 5)
SIDES_Y = (0, 1, 2, 4, 3, 5)


def targets(px, py):
    table = []
    for dx, dy in FACES:
        ox, nx = divmod(px + dx, 2)
        oy, ny = divmod(py + dy, 2)
        table.append([(ox, oy), (ox + 2 * nx - 1, oy), (ox, oy + 2 * ny - 1)])
    return table


def box_set(px, py):
    return sorted({t for row in targets(px, py) for t in row})


def around(px, py):
    found = [(0, (0, 0), (px, py))]
    for m in (2, 1) if px == 0 else (1, 2):
        ox, nx = divmod(px + FACES[m][0], 2)
        found.append((m, (ox, 0), (nx, py)))
    for m in (4, 3) if py == 0 else (3, 4):
        oy, ny = divmod(py + FACES[m][1], 2)
        found.append((m, (0, oy), (px, ny)))
    found.append((5, (0, 0), (px, py)))
    return found


def image_set(px, py):
    found = set()
    for _, (ox, oy), column in around(px, py):
        found |= {(ox + tx, oy + ty) for tx, ty in box_set(*column)}
    return sorted(found)


IMAGE = sorted({s for column in COLUMNS for s in image_set(*column)})
IMAGE_PAIRS = (len(IMAGE) + 1) // 2
STAR = [(0, 1), (0, -1), (0, 0), (1, 0), (-1, 0)]


def column_of(tx, ty):
    return ((tx + 1) // 2, (ty + 1) // 2)


def blocks_of(tx, ty):
    return IMAGE if (tx, ty) in STAR else image_set(*column_of(tx, ty))


TO_Y_FIRST = [((tx, 1), s) for tx in (0, -1, 1) for s in blocks_of(tx, 1)]
TO_Y_SECOND = [((0, -1), s) for s in blocks_of(0, -1)]
TO_C_FIRST = [((1, -1), s) for s in blocks_of(1, -1)]
TO_C_SECOND = [((-1, -1), s) for s in blocks_of(-1, -1)]


def relayed(tx):
    return {(s[0], 1 - s[1]): row for row, (t, s) in enumerate(TO_Y_FIRST) if t[0] == tx}


TO_X = {tx: sorted(set(IMAGE) | set(relayed(tx))) for tx in (1, -1)}
STENCIL = [(jx, jy) for jx in range(-3, 4) for jy in range(-3, 4) if abs(jx) + abs(jy) <= 3]
OWN = sorted(
    set(IMAGE)
    | set(relayed(0))
    | {(s[0], -1 - s[1]) for _, s in TO_Y_SECOND}
    | {(1 - s[0], -1 - s[1]) for _, s in TO_C_FIRST}
    | {(-1 - s[0], -1 - s[1]) for _, s in TO_C_SECOND}
)


def low_half(shape):
    return lax.broadcasted_iota(jnp.int32, shape, len(shape) - 1) < B


def swap_halves(value):
    return pltpu.roll(value, B, value.ndim - 1)


def pair_lanes(left, right):
    return jnp.concatenate([left, right], axis=-1)


def mirrored():
    return lax.axis_index("sx") % 2, lax.axis_index("sy") % 2


def slot_here(m, z, odd_x, odd_y):
    if m in (1, 2):
        return jnp.where(odd_x == 1, 3 - m, m)
    if m in (3, 4):
        return jnp.where(odd_y == 1, 7 - m, m)
    return 6 - z if m == 5 else m


def fill_rows(rows, values):
    shape = (rows, PAIR)
    row = lax.broadcasted_iota(jnp.int32, shape, 0)
    half = low_half(shape)
    filled = jnp.zeros(shape, jnp.float32)
    for index, (low, high) in enumerate(values):
        filled = jnp.where(row == index, jnp.where(half, low, high), filled)
    return filled


def pack_kernel(
    boxes_y,
    aggregate_hbm,
    links_hbm,
    p_hbm,
    rows_ref,
    meta_ref,
    x_first,
    x_second,
    y_first,
    y_second,
    p_ref,
    aggregate_ref,
    links_ref,
    p_sems,
    sems,
):
    odd_x, odd_y = mirrored()
    own = lax.axis_index("sx") * boxes_y + lax.axis_index("sy")
    place = {(px, py): (px ^ odd_x, py ^ odd_y) for px, py in COLUMNS}
    copies = [
        pltpu.make_async_copy(p_hbm.at[place[column]], p_ref.at[index], p_sems.at[index])
        for index, column in enumerate(COLUMNS)
    ]
    small = [
        pltpu.make_async_copy(aggregate_hbm, aggregate_ref, sems.at[0]),
        pltpu.make_async_copy(links_hbm, links_ref, sems.at[1]),
    ]
    for copy in small + copies:
        copy.start()
    for copy in small:
        copy.wait()

    def state(column, z):
        shift = aggregate_ref[place[column] + (z,)] - own
        across_x = (shift == boxes_y) | (shift == -boxes_y)
        return jnp.where(shift == 0, 0, jnp.where(across_x, 1, 2)).astype(jnp.float32)

    def link(column, m):
        faces = [slot_here(m, z, odd_x, odd_y) - 1 for z in (0, 1)]
        return tuple(links_ref[place[column] + (z, faces[z])].astype(jnp.float32) for z in (0, 1))

    states = [tuple(state(column, z) for z in (0, 1)) for column in COLUMNS]
    links = {column: [link(column, m) for m in range(1, SLOTS)] for column in COLUMNS}
    meta_ref[...] = fill_rows(32, states + sum((links[column] for column in COLUMNS), []))
    messages = (
        (x_first, ((1, 0), (1, 1))),
        (x_second, ((0, 0), (0, 1))),
        (y_first, ((0, 1), (1, 1))),
        (y_second, ((0, 0), (1, 0))),
    )
    for ref, columns in messages:
        tail = fill_rows(TAIL, states + links[columns[0]] + links[columns[1]])
        ref[BODY : BODY + TAIL, :] = tail.astype(jnp.bfloat16)
    for index, column in enumerate(COLUMNS):
        copies[index].wait()
        for m in range(SLOTS):
            packed = pair_lanes(*(p_ref[index, z, slot_here(m, z, odd_x, odd_y)] for z in (0, 1)))
            rows_ref[index, m * B : (m + 1) * B, :] = packed
            for ref, columns in messages:
                if column in columns:
                    start = columns.index(column) * BLOCK_ROWS + m * B
                    ref[start : start + B, :] = packed


def notes_kernel(x_first, x_second, _, notes_ref):
    notes_ref[0:TAIL, :] = x_first[BODY : BODY + TAIL, :]
    notes_ref[TAIL : 2 * TAIL, :] = x_second[BODY : BODY + TAIL, :]


def pack_matrix_kernel(links_hbm, a_hbm, out_ref, whole_hbm, a_ref, links_ref, zeros, a_sems, sems):
    fetches = [
        pltpu.make_async_copy(links_hbm, links_ref, a_sems.at[4]),
        *(
            pltpu.make_async_copy(a_hbm.at[px, py], a_ref.at[px, py], a_sems.at[index])
            for index, (px, py) in enumerate(COLUMNS)
        ),
    ]
    for fetch in fetches:
        fetch.start()
    zeros[...] = jnp.zeros(zeros.shape, zeros.dtype)
    copies = []
    for jx in range(-3, 4):
        width = abs(jx)
        if width:
            for start in (0, 7 - width):
                copies.append(
                    pltpu.make_async_copy(
                        zeros.at[pl.ds(0, width)], whole_hbm.at[jx + 3, pl.ds(start, width)], sems.at[len(copies)]
                    )
                )
    for copy in copies:
        copy.start()
    for fetch in fetches:
        fetch.wait()
    odd_x, odd_y = mirrored()
    for index, (px, py) in enumerate(COLUMNS):
        place = (px ^ odd_x, py ^ odd_y)
        for z in (0, 1):
            blocks = []
            for m, _, _ in around(px, py):
                slot = slot_here(m, z, odd_x, odd_y)
                block = a_ref[place + (z, slot)]
                if m > 0:
                    present = links_ref[place + (z, slot - 1)] == 1
                    block = jnp.where(present, block, jnp.zeros_like(block))
                blocks.append(block)
            for pair in range(3):
                out_ref[index, z * B : (z + 1) * B, pair * PAIR : (pair + 1) * PAIR] = pair_lanes(
                    blocks[2 * pair], blocks[2 * pair + 1]
                )
    for copy in copies:
        copy.wait()


def there(ox, oy, px, py):
    return (1 - px if ox else px, 1 - py if oy else py)


def slot_there(ox, oy, m):
    m = SIDES_X[m] if ox else m
    return SIDES_Y[m] if oy else m


class Rows:
    def __init__(self, rows_ref, meta_ref, from_x, from_y, corners):
        self.rows_ref, self.from_x, self.from_y = rows_ref, from_x, from_y
        self.notes = {(0, 0): meta_ref[...]}
        for side, ref in from_x.items():
            self.notes[side, 0] = ref[BODY : BODY + TAIL, :].astype(jnp.float32)
        for side, ref in from_y.items():
            self.notes[0, side] = ref[BODY : BODY + TAIL, :].astype(jnp.float32)
        for oy, ref in corners.items():
            self.notes[1, oy] = ref[0:TAIL, :].astype(jnp.float32)
            self.notes[-1, oy] = ref[TAIL : 2 * TAIL, :].astype(jnp.float32)

    def state_row(self, ox, oy, px, py):
        index = COLUMNS.index(there(ox, oy, px, py))
        return self.notes[ox, oy][index : index + 1]

    def link_row(self, ox, oy, px, py, m):
        if (ox, oy) == (0, 0):
            index = (SLOTS - 1) * COLUMNS.index((px, py))
        else:
            index = (SLOTS - 1) * (py if ox else px)
        index += 4 + slot_there(ox, oy, m) - 1
        return self.notes[ox, oy][index : index + 1]

    def block(self, ox, oy, px, py, m, chunk):
        start = slot_there(ox, oy, m) * B + chunk * 16
        if (ox, oy) == (0, 0):
            return self.rows_ref[COLUMNS.index((px, py)), start : start + 16, :]
        start += (py if ox else px) * BLOCK_ROWS
        ref = self.from_x[ox] if ox else self.from_y[oy]
        return ref[start : start + 16, :]

    def sums(self, box, column, slots, begun=None):
        (ox, oy), (px, py) = box, column
        weights = {}
        for m in slots:
            dx, dy = FACES[m]
            bx, nx = divmod(2 * ox + px + dx, 2)
            by, ny = divmod(2 * oy + py + dy, 2)
            state = self.state_row(bx, by, nx, ny)
            if m == 5:
                state = swap_halves(state)
            for kind in range(3):
                weight = jnp.where(state == kind, 1.0, 0.0)
                if m > 0:
                    weight = weight * self.link_row(ox, oy, px, py, m)
                weights[m, kind] = jnp.broadcast_to(weight, (16, PAIR))
        reach = targets(px, py)
        chunks = {}
        for chunk in range(4):
            values = {m: self.block(ox, oy, px, py, m, chunk).astype(jnp.float32) for m in slots}
            for t in box_set(px, py):
                total = begun[t][chunk * 16 : chunk * 16 + 16] if begun and t in begun else None
                for m in slots:
                    for kind in range(3):
                        if reach[m][kind] == t:
                            term = values[m] * weights[m, kind]
                            total = term if total is None else total + term
                if total is not None:
                    chunks.setdefault(t, []).append(total)
        return {t: jnp.concatenate(parts, axis=0) for t, parts in chunks.items()}


IMAGES = {column: image_set(*column) for column in COLUMNS}
USERS = {}
for _index, _column in enumerate(COLUMNS):
    for _place, (_, _box, _other) in enumerate(around(*_column)):
        USERS.setdefault((_box, _other), []).append((_index, _column, _place))
BEGUN = [key for key in USERS if key[1][1] == 0 and key[0][1] == 0]
LATE = [key for key in USERS if key[0][1] == -1]
BEGUN_SLOT = 3


def place_rows(found, box, other, right, left_star, left_corner):
    unit = None
    if box == (0, 0):
        square = (PAIR, PAIR)
        diagonal = lax.broadcasted_iota(jnp.int32, square, 0) == lax.broadcasted_iota(jnp.int32, square, 1)
        unit = jnp.where(diagonal, 1.0, 0.0).astype(jnp.bfloat16)
    own = COLUMNS.index(other)
    for t, value in found.items():
        rounded = value.astype(jnp.bfloat16)
        for index, column, place in USERS[box, other]:
            position = IMAGES[column].index((box[0] + t[0], box[1] + t[1]))
            stored = swap_halves(value).astype(jnp.bfloat16) if place == 5 else rounded
            right[index, place * B : (place + 1) * B, position * PAIR : (position + 1) * PAIR] = stored
        if box == (0, 0):
            turned = lax.dot_general(
                unit, rounded, (((1,), (1,)), ((), ())), preferred_element_type=jnp.float32
            ).astype(jnp.bfloat16)
            turned = pair_lanes(turned[:B], turned[B:])
            if t in STAR:
                left_star[STAR.index(t) * B : (STAR.index(t) + 1) * B, own * PAIR : (own + 1) * PAIR] = turned
            else:
                left_corner[own] = turned


def begin_kernel(rows_ref, meta_ref, x_first, x_second, y_first, c_first, right, left_star, left_corner, begun_ref):
    rows = Rows(rows_ref, meta_ref, {1: x_first, -1: x_second}, {1: y_first}, {1: c_first})
    for index, column in enumerate(COLUMNS):
        for place, (_, box, other) in enumerate(around(*column)):
            reached = {(box[0] + tx, box[1] + ty) for tx, ty in box_set(*other)}
            for position, s in enumerate(IMAGES[column]):
                if s not in reached:
                    right[index, place * B : (place + 1) * B, position * PAIR : (position + 1) * PAIR] = jnp.zeros(
                        (B, PAIR), jnp.bfloat16
                    )
    for box, other in USERS:
        if (box, other) in LATE:
            continue
        slots = list(range(SLOTS))
        open_targets = []
        if (box, other) in BEGUN:
            slots.remove(BEGUN_SLOT)
            open_targets = targets(*other)[BEGUN_SLOT]
        found = rows.sums(box, other, slots)
        for place, t in enumerate(open_targets):
            begun_ref[BEGUN.index((box, other)), place] = found.pop(t)
        place_rows(found, box, other, right, left_star, left_corner)


def main_kernel(
    a_ref,
    rows_ref,
    meta_ref,
    x_first,
    x_second,
    y_second,
    c_second,
    begun_ref,
    right_in,
    left_star_in,
    left_corner_in,
    to_y_first,
    to_y_second,
    to_c_first,
    to_c_second,
    rest_ref,
    right,
    left_star,
    left_corner,
    image,
):
    images = IMAGES
    rows = Rows(rows_ref, meta_ref, {1: x_first, -1: x_second}, {-1: y_second}, {-1: c_second})
    for box, other in BEGUN:
        begun = {
            t: begun_ref[BEGUN.index((box, other)), place] for place, t in enumerate(targets(*other)[BEGUN_SLOT])
        }
        place_rows(rows.sums(box, other, [BEGUN_SLOT], begun), box, other, right, left_star, left_corner)
    for box, other in LATE:
        place_rows(rows.sums(box, other, list(range(SLOTS))), box, other, right, left_star, left_corner)
    half = low_half((B, PAIR))
    for index, column in enumerate(COLUMNS):
        product = jnp.dot(a_ref[index], right[index], preferred_element_type=jnp.float32)

        def part(s, z):
            if s not in images[column]:
                return jnp.zeros((B, PAIR), jnp.float32)
            position = images[column].index(s)
            return product[z * B : (z + 1) * B, position * PAIR : (position + 1) * PAIR]

        for pair in range(IMAGE_PAIRS):
            one = IMAGE[2 * pair]
            two = IMAGE[2 * pair + 1] if 2 * pair + 1 < len(IMAGE) else None
            low = jnp.where(half, part(one, 0), swap_halves(part(two, 0)))
            high = jnp.where(half, swap_halves(part(one, 1)), part(two, 1))
            start = index * PAIR
            lanes = slice(pair * PAIR, (pair + 1) * PAIR)
            image[start : start + B, lanes] = low.astype(jnp.bfloat16)
            image[start + B : start + PAIR, lanes] = high.astype(jnp.bfloat16)
    folded_half = low_half((HALF, PAIR))

    def fold(product):
        blocks = {}
        for pair in range(IMAGE_PAIRS):
            tile = product[:, pair * PAIR : (pair + 1) * PAIR]
            top, bottom = tile[:HALF], tile[HALF:]
            blocks[IMAGE[2 * pair]] = jnp.where(folded_half, top, swap_halves(bottom))
            if 2 * pair + 1 < len(IMAGE):
                blocks[IMAGE[2 * pair + 1]] = jnp.where(folded_half, swap_halves(top), bottom)
        return blocks

    star = jnp.dot(left_star[...], image[...], preferred_element_type=jnp.float32)

    def contribution(t):
        if t in STAR:
            return fold(star[STAR.index(t) * B : (STAR.index(t) + 1) * B])
        index = COLUMNS.index(column_of(*t))
        return fold(
            jnp.dot(
                left_corner[index], image[index * PAIR : (index + 1) * PAIR, :], preferred_element_type=jnp.float32
            )
        )

    for ref, sent in (
        (to_y_first, TO_Y_FIRST),
        (to_y_second, TO_Y_SECOND),
        (to_c_first, TO_C_FIRST),
        (to_c_second, TO_C_SECOND),
    ):
        parts = {t: contribution(t) for t in sorted({t for t, _ in sent})}
        for row, (t, s) in enumerate(sent):
            ref[row * HALF : (row + 1) * HALF, :] = parts[t][s].astype(jnp.bfloat16)
    for group, tx in enumerate((0, -1, 1)):
        parts = contribution((tx, 0))
        for position, s in enumerate(IMAGE):
            rest_ref[group, position] = parts[s]


def message_block(ref, row):
    return ref[row * HALF : (row + 1) * HALF, :].astype(jnp.float32)


def relay_kernel(rest_ref, y_first, x_first, x_second):
    for ref, tx in ((x_first, 1), (x_second, -1)):
        arrived = relayed(tx)
        for row, s in enumerate(TO_X[tx]):
            value = None
            if s in IMAGE:
                value = rest_ref[(0, -1, 1).index(tx), IMAGE.index(s)]
            if s in arrived:
                more = message_block(y_first, arrived[s])
                value = more if value is None else value + more
            ref[row * HALF : (row + 1) * HALF, :] = value.astype(jnp.bfloat16)


def gathered(terms):
    total = None
    for ref, row, flag in terms:
        value = message_block(ref, row) if row is not None else ref
        if flag is not None:
            value = value * flag
        total = value if total is None else total + value
    return total


def inside():
    x, y = lax.axis_index("sx"), lax.axis_index("sy")
    return (
        ((x > 0) & (x < lax.axis_size("sx") - 1)).astype(jnp.float32),
        ((y > 0) & (y < lax.axis_size("sy") - 1)).astype(jnp.float32),
    )


def own_kernel(rest_ref, y_first, y_second, c_first, c_second, own_ref):
    has_x, has_y = inside()
    terms = {block: [] for block in STENCIL}
    for position, s in enumerate(IMAGE):
        terms[s].append((rest_ref[0, position], None, None))
    for s, row in relayed(0).items():
        terms[s].append((y_first, row, None))
    for row, (_, s) in enumerate(TO_Y_SECOND):
        terms[s[0], -1 - s[1]].append((y_second, row, has_y))
    for row, (_, s) in enumerate(TO_C_FIRST):
        terms[1 - s[0], -1 - s[1]].append((c_first, row, has_y))
    for row, (_, s) in enumerate(TO_C_SECOND):
        terms[-1 - s[0], -1 - s[1]].append((c_second, row, has_x * has_y))
    for position, block in enumerate(OWN):
        own_ref[position] = gathered(terms[block])


def finish_kernel(own_ref, x_first, x_second, _, out_hbm, rows, sems):
    odd_x, odd_y = mirrored()
    has_x, _ = inside()
    terms = {block: [] for block in STENCIL}
    for position, block in enumerate(OWN):
        terms[block].append((own_ref[position], None, None))
    for row, s in enumerate(TO_X[1]):
        terms[1 - s[0], s[1]].append((x_first, row, None))
    for row, s in enumerate(TO_X[-1]):
        terms[-1 - s[0], s[1]].append((x_second, row, has_x))
    copies = []
    for jx in (0, 1, -1, 2, -2, 3, -3):
        row_here = jnp.where(odd_x == 1, 3 - jx, 3 + jx)
        reach = 3 - abs(jx)
        for jy in range(-reach, reach + 1):
            value = gathered(terms[jx, jy])
            column_here = jnp.where(odd_y == 1, 3 - jy, 3 + jy)
            rows[jx + 3, column_here, 0:HALF, :] = value[:, :B].astype(jnp.bfloat16)
            rows[jx + 3, column_here, HALF:B, :] = swap_halves(value)[:, :B].astype(jnp.bfloat16)
        span = pl.ds(3 - reach, 2 * reach + 1)
        copy = pltpu.make_async_copy(rows.at[jx + 3, span], out_hbm.at[row_here, span], sems.at[jx + 3])
        copy.start()
        copies.append(copy)
    for copy in copies:
        copy.wait()


def swapped(value, move_x, move_y):
    count_x, count_y = lax.axis_size("sx"), lax.axis_size("sy")

    def partner(index, move, count):
        if move == 0:
            return index
        found = index ^ 1 if move == 1 else ((index + 1) ^ 1) - 1
        return found if 0 <= found < count else None

    pairs = []
    for x in range(count_x):
        for y in range(count_y):
            to_x, to_y = partner(x, move_x, count_x), partner(y, move_y, count_y)
            if to_x is None:
                to_x, to_y = x, y ^ 1
            elif to_y is None:
                to_x, to_y = (x ^ 1 if move_x == 0 else to_x), y
            pairs.append((x * count_y + y, to_x * count_y + to_y))
    return lax.ppermute(value, ("sx", "sy"), pairs)


SMEM = pl.BlockSpec(memory_space=pltpu.SMEM)
VMEM = pl.BlockSpec(memory_space=pltpu.VMEM)
HBM = pl.BlockSpec(memory_space=pltpu.HBM)
ANY = pl.BlockSpec(memory_space=pl.ANY)


def call(kernel, in_specs, outs, scratch=(), out_specs=None, aliases=None, cost=None):
    return pl.pallas_call(
        kernel,
        out_shape=[jax.ShapeDtypeStruct(shape, dtype) for shape, dtype in outs],
        in_specs=in_specs,
        out_specs=out_specs or [VMEM] * len(outs),
        scratch_shapes=list(scratch),
        input_output_aliases=aliases or {},
        compiler_params=pltpu.CompilerParams(vmem_limit_bytes=VMEM_LIMIT),
        cost_estimate=None if cost is None else pl.CostEstimate(flops=cost, bytes_accessed=1, transcendentals=0),
    )


def in_hbm(*values):
    return [pltpu.with_memory_space_constraint(value, pltpu.HBM) for value in values]


def per_device(fine_matrix, prolongator, aggregate, face_links):
    bf16, f32 = jnp.bfloat16, jnp.float32
    message = ((BODY + TAIL, PAIR), bf16)
    longer = ((BODY + 2 * TAIL, PAIR), bf16)
    rows, meta, x_first, x_second, y_first, y_second = call(
        functools.partial(pack_kernel, lax.axis_size("sy")),
        [HBM, HBM, HBM],
        [((4, BLOCK_ROWS, PAIR), bf16), ((32, PAIR), f32), message, message, message, longer],
        [
            pltpu.VMEM((4, 2, 7, B, B), bf16),
            pltpu.SMEM((2, 2, 2), jnp.int32),
            pltpu.SMEM((2, 2, 2, 6), jnp.int32),
            pltpu.SemaphoreType.DMA((4,)),
            pltpu.SemaphoreType.DMA((2,)),
        ],
    )(*in_hbm(aggregate, face_links, prolongator))
    y_second = swapped(y_second, 0, 2)
    x_first, x_second = swapped(x_first, 1, 0), swapped(x_second, 2, 0)
    y_first = swapped(y_first, 0, 1)
    whole = ((7, 7, B, B), bf16)
    matrix, out = call(
        pack_matrix_kernel,
        [HBM, HBM],
        [((4, PAIR, 6 * B), bf16), whole],
        [
            pltpu.VMEM((2, 2, 2, 7, B, B), bf16),
            pltpu.SMEM((2, 2, 2, 6), jnp.int32),
            pltpu.VMEM((3, B, B), bf16),
            pltpu.SemaphoreType.DMA((5,)),
            pltpu.SemaphoreType.DMA((12,)),
        ],
        [VMEM, HBM],
    )(*in_hbm(face_links, fine_matrix))
    (notes,) = call(notes_kernel, [VMEM, VMEM, ANY], [((2 * TAIL, PAIR), bf16)])(x_first, x_second, matrix)
    c_first, c_second = swapped(notes, 0, 1), swapped(notes, 0, 2)

    def sent(blocks):
        return ((len(blocks) * HALF, PAIR), bf16)

    lefts = [
        ((4, SLOTS * B, 10 * PAIR), bf16),
        ((len(STAR) * B, 4 * PAIR), bf16),
        ((4, B, PAIR), bf16),
    ]
    *lefts_begun, begun = call(begin_kernel, [VMEM] * 6, lefts + [((len(BEGUN), 3, B, PAIR), f32)])(
        rows, meta, x_first, x_second, y_first, c_first
    )
    y_first, y_second, c_first, c_second, rest, *_ = call(
        main_kernel,
        [VMEM] * 11,
        [
            sent(TO_Y_FIRST),
            sent(TO_Y_SECOND),
            sent(TO_C_FIRST),
            sent(TO_C_SECOND),
            ((3, len(IMAGE), HALF, PAIR), f32),
        ]
        + lefts,
        [pltpu.VMEM((4 * PAIR, IMAGE_PAIRS * PAIR), bf16)],
        aliases={8: 5, 9: 6, 10: 7},
    )(
        matrix,
        rows,
        meta,
        x_first,
        x_second,
        y_second,
        c_second,
        begun,
        *(pltpu.with_memory_space_constraint(left, pltpu.VMEM) for left in lefts_begun),
    )
    y_second = swapped(y_second, 0, 2)
    c_first, c_second = swapped(c_first, 1, 2), swapped(c_second, 2, 2)
    y_first = swapped(y_first, 0, 1)
    x_first, x_second = call(relay_kernel, [VMEM] * 2, [sent(TO_X[1]), sent(TO_X[-1])])(rest, y_first)
    x_first, x_second = swapped(x_first, 1, 0), swapped(x_second, 2, 0)
    (own,) = call(own_kernel, [VMEM] * 5, [((len(OWN), HALF, PAIR), f32)], cost=3_000_000_000)(
        rest, y_first, y_second, c_first, c_second
    )
    (out,) = call(
        finish_kernel,
        [VMEM] * 3 + [HBM],
        [whole],
        [pltpu.VMEM((7, 7, B, B), bf16), pltpu.SemaphoreType.DMA((7,))],
        [HBM],
        {3: 0},
    )(own, x_first, x_second, out)
    return out[None, None]


def solution(mesh):
    return jax.shard_map(
        per_device,
        mesh=mesh,
        in_specs=(
            P("sx", "sy", None, None, None, None),
            P("sx", "sy", None, None, None, None),
            P("sx", "sy", None),
            P("sx", "sy", None, None),
        ),
        out_specs=P("sx", "sy", None, None, None, None),
        check_vma=False,
    )
```

```python
import functools

import jax
import jax.numpy as jnp
from jax import lax
from jax.experimental import pallas as pl
from jax.experimental.pallas import tpu as pltpu
from jax.sharding import PartitionSpec as P


B = 64
HALF = B // 2
PAIR = 2 * B
SLOTS = 6
BLOCK_ROWS = SLOTS * B
BODY = 2 * BLOCK_ROWS
TAIL = 16
VMEM_LIMIT = 20 * 1024 * 1024

FACES = [(0, 0), (-1, 0), (1, 0), (0, -1), (0, 1), (0, 0)]
COLUMNS = [(0, 0), (0, 1), (1, 0), (1, 1)]
SIDES_X = (0, 2, 1, 3, 4, 5)
SIDES_Y = (0, 1, 2, 4, 3, 5)


def targets(px, py):
    table = []
    for dx, dy in FACES:
        ox, nx = divmod(px + dx, 2)
        oy, ny = divmod(py + dy, 2)
        table.append([(ox, oy), (ox + 2 * nx - 1, oy), (ox, oy + 2 * ny - 1)])
    return table


def box_set(px, py):
    return sorted({t for row in targets(px, py) for t in row})


def around(px, py):
    found = [(0, (0, 0), (px, py))]
    for m in (2, 1) if px == 0 else (1, 2):
        ox, nx = divmod(px + FACES[m][0], 2)
        found.append((m, (ox, 0), (nx, py)))
    for m in (4, 3) if py == 0 else (3, 4):
        oy, ny = divmod(py + FACES[m][1], 2)
        found.append((m, (0, oy), (px, ny)))
    found.append((5, (0, 0), (px, py)))
    return found


def image_set(px, py):
    found = set()
    for _, (ox, oy), column in around(px, py):
        found |= {(ox + tx, oy + ty) for tx, ty in box_set(*column)}
    return sorted(found)


IMAGE = sorted({s for column in COLUMNS for s in image_set(*column)})
IMAGE_PAIRS = (len(IMAGE) + 1) // 2
STAR = [(0, 1), (0, -1), (0, 0), (1, 0), (-1, 0)]


def column_of(tx, ty):
    return ((tx + 1) // 2, (ty + 1) // 2)


def blocks_of(tx, ty):
    return IMAGE if (tx, ty) in STAR else image_set(*column_of(tx, ty))


TO_Y_FIRST = [((tx, 1), s) for tx in (0, -1, 1) for s in blocks_of(tx, 1)]
TO_Y_SECOND = [((0, -1), s) for s in blocks_of(0, -1)]
TO_C_FIRST = [((1, -1), s) for s in blocks_of(1, -1)]
TO_C_SECOND = [((-1, -1), s) for s in blocks_of(-1, -1)]


def relayed(tx):
    return {(s[0], 1 - s[1]): row for row, (t, s) in enumerate(TO_Y_FIRST) if t[0] == tx}


TO_X = {tx: sorted(set(IMAGE) | set(relayed(tx))) for tx in (1, -1)}
STENCIL = [(jx, jy) for jx in range(-3, 4) for jy in range(-3, 4) if abs(jx) + abs(jy) <= 3]
OWN = sorted(
    set(IMAGE)
    | set(relayed(0))
    | {(s[0], -1 - s[1]) for _, s in TO_Y_SECOND}
    | {(1 - s[0], -1 - s[1]) for _, s in TO_C_FIRST}
    | {(-1 - s[0], -1 - s[1]) for _, s in TO_C_SECOND}
)


def low_half(shape):
    return lax.broadcasted_iota(jnp.int32, shape, len(shape) - 1) < B


def swap_halves(value):
    return pltpu.roll(value, B, value.ndim - 1)


def pair_lanes(left, right):
    return jnp.concatenate([left, right], axis=-1)


def mirrored():
    return lax.axis_index("sx") % 2, lax.axis_index("sy") % 2


def slot_here(m, z, odd_x, odd_y):
    if m in (1, 2):
        return jnp.where(odd_x == 1, 3 - m, m)
    if m in (3, 4):
        return jnp.where(odd_y == 1, 7 - m, m)
    return 6 - z if m == 5 else m


def fill_rows(rows, values):
    shape = (rows, PAIR)
    row = lax.broadcasted_iota(jnp.int32, shape, 0)
    half = low_half(shape)
    filled = jnp.zeros(shape, jnp.float32)
    for index, (low, high) in enumerate(values):
        filled = jnp.where(row == index, jnp.where(half, low, high), filled)
    return filled


def pack_kernel(
    boxes_y,
    aggregate_hbm,
    links_hbm,
    p_hbm,
    rows_ref,
    meta_ref,
    x_first,
    x_second,
    y_first,
    y_second,
    p_ref,
    aggregate_ref,
    links_ref,
    p_sems,
    sems,
):
    odd_x, odd_y = mirrored()
    own = lax.axis_index("sx") * boxes_y + lax.axis_index("sy")
    place = {(px, py): (px ^ odd_x, py ^ odd_y) for px, py in COLUMNS}
    copies = [
        pltpu.make_async_copy(p_hbm.at[place[column]], p_ref.at[index], p_sems.at[index])
        for index, column in enumerate(COLUMNS)
    ]
    small = [
        pltpu.make_async_copy(aggregate_hbm, aggregate_ref, sems.at[0]),
        pltpu.make_async_copy(links_hbm, links_ref, sems.at[1]),
    ]
    for copy in small + copies:
        copy.start()
    for copy in small:
        copy.wait()

    def state(column, z):
        shift = aggregate_ref[place[column] + (z,)] - own
        across_x = (shift == boxes_y) | (shift == -boxes_y)
        return jnp.where(shift == 0, 0, jnp.where(across_x, 1, 2)).astype(jnp.float32)

    def link(column, m):
        faces = [slot_here(m, z, odd_x, odd_y) - 1 for z in (0, 1)]
        return tuple(links_ref[place[column] + (z, faces[z])].astype(jnp.float32) for z in (0, 1))

    states = [tuple(state(column, z) for z in (0, 1)) for column in COLUMNS]
    links = {column: [link(column, m) for m in range(1, SLOTS)] for column in COLUMNS}
    meta_ref[...] = fill_rows(32, states + sum((links[column] for column in COLUMNS), []))
    messages = (
        (x_first, ((1, 0), (1, 1))),
        (x_second, ((0, 0), (0, 1))),
        (y_first, ((0, 1), (1, 1))),
        (y_second, ((0, 0), (1, 0))),
    )
    for ref, columns in messages:
        tail = fill_rows(TAIL, states + links[columns[0]] + links[columns[1]])
        ref[BODY : BODY + TAIL, :] = tail.astype(jnp.bfloat16)
    for index, column in enumerate(COLUMNS):
        copies[index].wait()
        for m in range(SLOTS):
            packed = pair_lanes(*(p_ref[index, z, slot_here(m, z, odd_x, odd_y)] for z in (0, 1)))
            rows_ref[index, m * B : (m + 1) * B, :] = packed
            for ref, columns in messages:
                if column in columns:
                    start = columns.index(column) * BLOCK_ROWS + m * B
                    ref[start : start + B, :] = packed


def notes_kernel(x_first, x_second, _, notes_ref):
    notes_ref[0:TAIL, :] = x_first[BODY : BODY + TAIL, :]
    notes_ref[TAIL : 2 * TAIL, :] = x_second[BODY : BODY + TAIL, :]


def pack_matrix_kernel(links_hbm, a_hbm, out_ref, whole_hbm, a_ref, links_ref, zeros, a_sems, sems):
    fetches = [
        pltpu.make_async_copy(links_hbm, links_ref, a_sems.at[4]),
        *(
            pltpu.make_async_copy(a_hbm.at[px, py], a_ref.at[px, py], a_sems.at[index])
            for index, (px, py) in enumerate(COLUMNS)
        ),
    ]
    for fetch in fetches:
        fetch.start()
    zeros[...] = jnp.zeros(zeros.shape, zeros.dtype)
    copies = []
    for jx in range(-3, 4):
        width = abs(jx)
        if width:
            for start in (0, 7 - width):
                copies.append(
                    pltpu.make_async_copy(
                        zeros.at[pl.ds(0, width)], whole_hbm.at[jx + 3, pl.ds(start, width)], sems.at[len(copies)]
                    )
                )
    for copy in copies:
        copy.start()
    for fetch in fetches:
        fetch.wait()
    odd_x, odd_y = mirrored()
    for index, (px, py) in enumerate(COLUMNS):
        place = (px ^ odd_x, py ^ odd_y)
        for z in (0, 1):
            blocks = []
            for m, _, _ in around(px, py):
                slot = slot_here(m, z, odd_x, odd_y)
                block = a_ref[place + (z, slot)]
                if m > 0:
                    present = links_ref[place + (z, slot - 1)] == 1
                    block = jnp.where(present, block, jnp.zeros_like(block))
                blocks.append(block)
            for pair in range(3):
                out_ref[index, z * B : (z + 1) * B, pair * PAIR : (pair + 1) * PAIR] = pair_lanes(
                    blocks[2 * pair], blocks[2 * pair + 1]
                )
    for copy in copies:
        copy.wait()


def there(ox, oy, px, py):
    return (1 - px if ox else px, 1 - py if oy else py)


def slot_there(ox, oy, m):
    m = SIDES_X[m] if ox else m
    return SIDES_Y[m] if oy else m


class Rows:
    def __init__(self, rows_ref, meta_ref, from_x, from_y, corners):
        self.rows_ref, self.from_x, self.from_y = rows_ref, from_x, from_y
        self.notes = {(0, 0): meta_ref[...]}
        for side, ref in from_x.items():
            self.notes[side, 0] = ref[BODY : BODY + TAIL, :].astype(jnp.float32)
        for side, ref in from_y.items():
            self.notes[0, side] = ref[BODY : BODY + TAIL, :].astype(jnp.float32)
        for oy, ref in corners.items():
            self.notes[1, oy] = ref[0:TAIL, :].astype(jnp.float32)
            self.notes[-1, oy] = ref[TAIL : 2 * TAIL, :].astype(jnp.float32)

    def state_row(self, ox, oy, px, py):
        index = COLUMNS.index(there(ox, oy, px, py))
        return self.notes[ox, oy][index : index + 1]

    def link_row(self, ox, oy, px, py, m):
        if (ox, oy) == (0, 0):
            index = (SLOTS - 1) * COLUMNS.index((px, py))
        else:
            index = (SLOTS - 1) * (py if ox else px)
        index += 4 + slot_there(ox, oy, m) - 1
        return self.notes[ox, oy][index : index + 1]

    def block(self, ox, oy, px, py, m, chunk):
        start = slot_there(ox, oy, m) * B + chunk * 16
        if (ox, oy) == (0, 0):
            return self.rows_ref[COLUMNS.index((px, py)), start : start + 16, :]
        start += (py if ox else px) * BLOCK_ROWS
        ref = self.from_x[ox] if ox else self.from_y[oy]
        return ref[start : start + 16, :]

    def sums(self, box, column, slots, begun=None):
        (ox, oy), (px, py) = box, column
        weights = {}
        for m in slots:
            dx, dy = FACES[m]
            bx, nx = divmod(2 * ox + px + dx, 2)
            by, ny = divmod(2 * oy + py + dy, 2)
            state = self.state_row(bx, by, nx, ny)
            if m == 5:
                state = swap_halves(state)
            for kind in range(3):
                weight = jnp.where(state == kind, 1.0, 0.0)
                if m > 0:
                    weight = weight * self.link_row(ox, oy, px, py, m)
                weights[m, kind] = jnp.broadcast_to(weight, (16, PAIR))
        reach = targets(px, py)
        chunks = {}
        for chunk in range(4):
            values = {m: self.block(ox, oy, px, py, m, chunk).astype(jnp.float32) for m in slots}
            for t in box_set(px, py):
                total = begun[t][chunk * 16 : chunk * 16 + 16] if begun and t in begun else None
                for m in slots:
                    for kind in range(3):
                        if reach[m][kind] == t:
                            term = values[m] * weights[m, kind]
                            total = term if total is None else total + term
                if total is not None:
                    chunks.setdefault(t, []).append(total)
        return {t: jnp.concatenate(parts, axis=0) for t, parts in chunks.items()}


IMAGES = {column: image_set(*column) for column in COLUMNS}
USERS = {}
for _index, _column in enumerate(COLUMNS):
    for _place, (_, _box, _other) in enumerate(around(*_column)):
        USERS.setdefault((_box, _other), []).append((_index, _column, _place))
BEGUN = [key for key in USERS if key[1][1] == 0 and key[0][1] == 0]
LATE = [key for key in USERS if key[0][1] == -1]
BEGUN_SLOT = 3


def place_rows(found, box, other, store, left_star, left_corner):
    unit = None
    if box == (0, 0):
        square = (PAIR, PAIR)
        diagonal = lax.broadcasted_iota(jnp.int32, square, 0) == lax.broadcasted_iota(jnp.int32, square, 1)
        unit = jnp.where(diagonal, 1.0, 0.0).astype(jnp.bfloat16)
    own = COLUMNS.index(other)
    for t, value in found.items():
        rounded = value.astype(jnp.bfloat16)
        for index, column, place in USERS[box, other]:
            position = IMAGES[column].index((box[0] + t[0], box[1] + t[1]))
            store(index, place, position, swap_halves(value).astype(jnp.bfloat16) if place == 5 else rounded)
        if box == (0, 0):
            turned = lax.dot_general(
                unit, rounded, (((1,), (1,)), ((), ())), preferred_element_type=jnp.float32
            ).astype(jnp.bfloat16)
            turned = pair_lanes(turned[:B], turned[B:])
            if t in STAR:
                left_star[STAR.index(t) * B : (STAR.index(t) + 1) * B, own * PAIR : (own + 1) * PAIR] = turned
            else:
                left_corner[own] = turned


def lanes_of(position):
    return slice(position * PAIR, (position + 1) * PAIR)


def fold_image(parts, column):
    half = low_half((B, PAIR))

    def part(s, z):
        return parts[s][z * B : (z + 1) * B] if s in parts else jnp.zeros((B, PAIR), jnp.float32)

    tiles = []
    for pair in range(IMAGE_PAIRS):
        one = IMAGE[2 * pair]
        two = IMAGE[2 * pair + 1] if 2 * pair + 1 < len(IMAGE) else None
        low = jnp.where(half, part(one, 0), swap_halves(part(two, 0)))
        high = jnp.where(half, swap_halves(part(one, 1)), part(two, 1))
        tiles.append((low, high))
    return tiles


def split_image(product, column):
    return {s: product[:, lanes_of(position)] for position, s in enumerate(IMAGES[column])}


INNER_Y = 3
LATE_IMAGE = {index: targets(px, 0)[BEGUN_SLOT] for index, (px, py) in enumerate(COLUMNS) if py == 1}


def begin_kernel(
    a_ref,
    rows_ref,
    meta_ref,
    x_first,
    x_second,
    y_first,
    c_first,
    right_late,
    left_star,
    left_corner,
    begun_ref,
    image_early,
    begun_image,
    right_early,
):
    rows = Rows(rows_ref, meta_ref, {1: x_first, -1: x_second}, {1: y_first}, {1: c_first})

    def store(index, place, position, value):
        ref = right_early if index in LATE_IMAGE else right_late
        ref[index // 2, place * B : (place + 1) * B, lanes_of(position)] = value

    for index, column in enumerate(COLUMNS):
        for place, (_, box, other) in enumerate(around(*column)):
            reached = {(box[0] + tx, box[1] + ty) for tx, ty in box_set(*other)}
            if index in LATE_IMAGE and place == INNER_Y:
                reached -= set(LATE_IMAGE[index])
            for position, s in enumerate(IMAGES[column]):
                if s not in reached:
                    store(index, place, position, jnp.zeros((B, PAIR), jnp.bfloat16))
    for box, other in USERS:
        if (box, other) in LATE:
            continue
        slots = list(range(SLOTS))
        open_targets = []
        if (box, other) in BEGUN:
            slots.remove(BEGUN_SLOT)
            open_targets = targets(*other)[BEGUN_SLOT]
        found = rows.sums(box, other, slots)
        for place, t in enumerate(open_targets):
            begun_ref[BEGUN.index((box, other)), place] = found.pop(t)
        place_rows(found, box, other, store, left_star, left_corner)
    for index, late in LATE_IMAGE.items():
        product = jnp.dot(a_ref[index], right_early[index // 2], preferred_element_type=jnp.float32)
        parts = split_image(product, COLUMNS[index])
        for place, s in enumerate(late):
            begun_image[index // 2, place] = parts.pop(s)
        for pair, (low, high) in enumerate(fold_image(parts, COLUMNS[index])):
            image_early[index // 2, 0:B, lanes_of(pair)] = low.astype(jnp.bfloat16)
            image_early[index // 2, B:PAIR, lanes_of(pair)] = high.astype(jnp.bfloat16)


def main_kernel(
    a_ref,
    rows_ref,
    meta_ref,
    x_first,
    x_second,
    y_second,
    c_second,
    begun_ref,
    image_early,
    begun_image,
    right_in,
    left_star_in,
    left_corner_in,
    to_y_first,
    to_y_second,
    to_c_first,
    to_c_second,
    rest_ref,
    right_late,
    left_star,
    left_corner,
    image,
):
    rows = Rows(rows_ref, meta_ref, {1: x_first, -1: x_second}, {-1: y_second}, {-1: c_second})
    late_rows = {index: {} for index in LATE_IMAGE}

    def store(index, place, position, value):
        if index in LATE_IMAGE:
            late_rows[index][IMAGES[COLUMNS[index]][position]] = value
        else:
            right_late[index // 2, place * B : (place + 1) * B, lanes_of(position)] = value

    for box, other in BEGUN:
        begun = {
            t: begun_ref[BEGUN.index((box, other)), place] for place, t in enumerate(targets(*other)[BEGUN_SLOT])
        }
        place_rows(rows.sums(box, other, [BEGUN_SLOT], begun), box, other, store, left_star, left_corner)
    for box, other in LATE:
        place_rows(rows.sums(box, other, list(range(SLOTS))), box, other, store, left_star, left_corner)
    half = low_half((B, PAIR))
    for index, column in enumerate(COLUMNS):
        start = index * PAIR
        if index in LATE_IMAGE:
            late = LATE_IMAGE[index]
            more = jnp.dot(
                a_ref[index, :, INNER_Y * B : (INNER_Y + 1) * B],
                jnp.concatenate([late_rows[index][s] for s in late], axis=1),
                preferred_element_type=jnp.float32,
            )
            parts = {
                s: begun_image[index // 2, place] + more[:, lanes_of(place)] for place, s in enumerate(late)
            }
        else:
            product = jnp.dot(a_ref[index], right_late[index // 2], preferred_element_type=jnp.float32)
            parts = split_image(product, column)
        for pair, (low, high) in enumerate(fold_image(parts, column)):
            blocks = IMAGE[2 * pair : 2 * pair + 2]
            for rows_here, tile in ((slice(0, B), low), (slice(B, PAIR), high)):
                new = tile.astype(jnp.bfloat16)
                if index in LATE_IMAGE:
                    old = image_early[index // 2, rows_here, lanes_of(pair)]
                    changed = [s in parts for s in blocks]
                    if not any(changed):
                        new = old
                    elif not all(changed):
                        new = jnp.where(half == changed[0], new, old)
                image[start + rows_here.start : start + rows_here.stop, lanes_of(pair)] = new
    folded_half = low_half((HALF, PAIR))

    def fold(product):
        blocks = {}
        for pair in range(IMAGE_PAIRS):
            tile = product[:, pair * PAIR : (pair + 1) * PAIR]
            top, bottom = tile[:HALF], tile[HALF:]
            blocks[IMAGE[2 * pair]] = jnp.where(folded_half, top, swap_halves(bottom))
            if 2 * pair + 1 < len(IMAGE):
                blocks[IMAGE[2 * pair + 1]] = jnp.where(folded_half, swap_halves(top), bottom)
        return blocks

    star = jnp.dot(left_star[...], image[...], preferred_element_type=jnp.float32)

    def contribution(t):
        if t in STAR:
            return fold(star[STAR.index(t) * B : (STAR.index(t) + 1) * B])
        index = COLUMNS.index(column_of(*t))
        return fold(
            jnp.dot(
                left_corner[index], image[index * PAIR : (index + 1) * PAIR, :], preferred_element_type=jnp.float32
            )
        )

    for ref, sent in (
        (to_y_first, TO_Y_FIRST),
        (to_y_second, TO_Y_SECOND),
        (to_c_first, TO_C_FIRST),
        (to_c_second, TO_C_SECOND),
    ):
        parts = {t: contribution(t) for t in sorted({t for t, _ in sent})}
        for row, (t, s) in enumerate(sent):
            ref[row * HALF : (row + 1) * HALF, :] = parts[t][s].astype(jnp.bfloat16)
    for group, tx in enumerate((0, -1, 1)):
        parts = contribution((tx, 0))
        for position, s in enumerate(IMAGE):
            rest_ref[group, position] = parts[s]


def message_block(ref, row):
    return ref[row * HALF : (row + 1) * HALF, :].astype(jnp.float32)


def relay_kernel(rest_ref, y_first, x_first, x_second):
    for ref, tx in ((x_first, 1), (x_second, -1)):
        arrived = relayed(tx)
        for row, s in enumerate(TO_X[tx]):
            value = None
            if s in IMAGE:
                value = rest_ref[(0, -1, 1).index(tx), IMAGE.index(s)]
            if s in arrived:
                more = message_block(y_first, arrived[s])
                value = more if value is None else value + more
            ref[row * HALF : (row + 1) * HALF, :] = value.astype(jnp.bfloat16)


def gathered(terms):
    total = None
    for ref, row, flag in terms:
        value = message_block(ref, row) if row is not None else ref
        if flag is not None:
            value = value * flag
        total = value if total is None else total + value
    return total


def inside():
    x, y = lax.axis_index("sx"), lax.axis_index("sy")
    return (
        ((x > 0) & (x < lax.axis_size("sx") - 1)).astype(jnp.float32),
        ((y > 0) & (y < lax.axis_size("sy") - 1)).astype(jnp.float32),
    )


def own_kernel(rest_ref, y_first, y_second, c_first, c_second, own_ref):
    has_x, has_y = inside()
    terms = {block: [] for block in STENCIL}
    for position, s in enumerate(IMAGE):
        terms[s].append((rest_ref[0, position], None, None))
    for s, row in relayed(0).items():
        terms[s].append((y_first, row, None))
    for row, (_, s) in enumerate(TO_Y_SECOND):
        terms[s[0], -1 - s[1]].append((y_second, row, has_y))
    for row, (_, s) in enumerate(TO_C_FIRST):
        terms[1 - s[0], -1 - s[1]].append((c_first, row, has_y))
    for row, (_, s) in enumerate(TO_C_SECOND):
        terms[-1 - s[0], -1 - s[1]].append((c_second, row, has_x * has_y))
    for position, block in enumerate(OWN):
        own_ref[position] = gathered(terms[block])


def finish_kernel(own_ref, x_first, x_second, _, out_hbm, rows, sems):
    odd_x, odd_y = mirrored()
    has_x, _ = inside()
    terms = {block: [] for block in STENCIL}
    for position, block in enumerate(OWN):
        terms[block].append((own_ref[position], None, None))
    for row, s in enumerate(TO_X[1]):
        terms[1 - s[0], s[1]].append((x_first, row, None))
    for row, s in enumerate(TO_X[-1]):
        terms[-1 - s[0], s[1]].append((x_second, row, has_x))
    copies = []
    for jx in (0, 1, -1, 2, -2, 3, -3):
        row_here = jnp.where(odd_x == 1, 3 - jx, 3 + jx)
        reach = 3 - abs(jx)
        for jy in range(-reach, reach + 1):
            value = gathered(terms[jx, jy])
            column_here = jnp.where(odd_y == 1, 3 - jy, 3 + jy)
            rows[jx + 3, column_here, 0:HALF, :] = value[:, :B].astype(jnp.bfloat16)
            rows[jx + 3, column_here, HALF:B, :] = swap_halves(value)[:, :B].astype(jnp.bfloat16)
        span = pl.ds(3 - reach, 2 * reach + 1)
        copy = pltpu.make_async_copy(rows.at[jx + 3, span], out_hbm.at[row_here, span], sems.at[jx + 3])
        copy.start()
        copies.append(copy)
    for copy in copies:
        copy.wait()


def swapped(value, move_x, move_y):
    count_x, count_y = lax.axis_size("sx"), lax.axis_size("sy")

    def partner(index, move, count):
        if move == 0:
            return index
        found = index ^ 1 if move == 1 else ((index + 1) ^ 1) - 1
        return found if 0 <= found < count else None

    pairs = []
    for x in range(count_x):
        for y in range(count_y):
            to_x, to_y = partner(x, move_x, count_x), partner(y, move_y, count_y)
            if to_x is None:
                to_x, to_y = x, y ^ 1
            elif to_y is None:
                to_x, to_y = (x ^ 1 if move_x == 0 else to_x), y
            pairs.append((x * count_y + y, to_x * count_y + to_y))
    return lax.ppermute(value, ("sx", "sy"), pairs)


SMEM = pl.BlockSpec(memory_space=pltpu.SMEM)
VMEM = pl.BlockSpec(memory_space=pltpu.VMEM)
HBM = pl.BlockSpec(memory_space=pltpu.HBM)
ANY = pl.BlockSpec(memory_space=pl.ANY)


def call(kernel, in_specs, outs, scratch=(), out_specs=None, aliases=None, cost=None):
    return pl.pallas_call(
        kernel,
        out_shape=[jax.ShapeDtypeStruct(shape, dtype) for shape, dtype in outs],
        in_specs=in_specs,
        out_specs=out_specs or [VMEM] * len(outs),
        scratch_shapes=list(scratch),
        input_output_aliases=aliases or {},
        compiler_params=pltpu.CompilerParams(vmem_limit_bytes=VMEM_LIMIT),
        cost_estimate=None if cost is None else pl.CostEstimate(flops=cost, bytes_accessed=1, transcendentals=0),
    )


def in_hbm(*values):
    return [pltpu.with_memory_space_constraint(value, pltpu.HBM) for value in values]


def per_device(fine_matrix, prolongator, aggregate, face_links):
    bf16, f32 = jnp.bfloat16, jnp.float32
    message = ((BODY + TAIL, PAIR), bf16)
    longer = ((BODY + 2 * TAIL, PAIR), bf16)
    rows, meta, x_first, x_second, y_first, y_second = call(
        functools.partial(pack_kernel, lax.axis_size("sy")),
        [HBM, HBM, HBM],
        [((4, BLOCK_ROWS, PAIR), bf16), ((32, PAIR), f32), message, message, message, longer],
        [
            pltpu.VMEM((4, 2, 7, B, B), bf16),
            pltpu.SMEM((2, 2, 2), jnp.int32),
            pltpu.SMEM((2, 2, 2, 6), jnp.int32),
            pltpu.SemaphoreType.DMA((4,)),
            pltpu.SemaphoreType.DMA((2,)),
        ],
    )(*in_hbm(aggregate, face_links, prolongator))
    y_second = swapped(y_second, 0, 2)
    x_first, x_second = swapped(x_first, 1, 0), swapped(x_second, 2, 0)
    y_first = swapped(y_first, 0, 1)
    whole = ((7, 7, B, B), bf16)
    matrix, out = call(
        pack_matrix_kernel,
        [HBM, HBM],
        [((4, PAIR, 6 * B), bf16), whole],
        [
            pltpu.VMEM((2, 2, 2, 7, B, B), bf16),
            pltpu.SMEM((2, 2, 2, 6), jnp.int32),
            pltpu.VMEM((3, B, B), bf16),
            pltpu.SemaphoreType.DMA((5,)),
            pltpu.SemaphoreType.DMA((12,)),
        ],
        [VMEM, HBM],
    )(*in_hbm(face_links, fine_matrix))
    (notes,) = call(notes_kernel, [VMEM, VMEM, ANY], [((2 * TAIL, PAIR), bf16)])(x_first, x_second, matrix)
    c_first, c_second = swapped(notes, 0, 1), swapped(notes, 0, 2)

    def sent(blocks):
        return ((len(blocks) * HALF, PAIR), bf16)

    product_rows, tiles = (2, SLOTS * B, 10 * PAIR), IMAGE_PAIRS * PAIR
    lefts = [
        (product_rows, bf16),
        ((len(STAR) * B, 4 * PAIR), bf16),
        ((4, B, PAIR), bf16),
    ]
    *lefts_begun, begun, image_early, begun_image = call(
        begin_kernel,
        [VMEM] * 7,
        lefts
        + [((len(BEGUN), 3, B, PAIR), f32), ((2, PAIR, tiles), bf16), ((2, 3, PAIR, PAIR), f32)],
        [pltpu.VMEM(product_rows, bf16)],
    )(matrix, rows, meta, x_first, x_second, y_first, c_first)
    y_first, y_second, c_first, c_second, rest, *_ = call(
        main_kernel,
        [VMEM] * 13,
        [
            sent(TO_Y_FIRST),
            sent(TO_Y_SECOND),
            sent(TO_C_FIRST),
            sent(TO_C_SECOND),
            ((3, len(IMAGE), HALF, PAIR), f32),
        ]
        + lefts,
        [pltpu.VMEM((4 * PAIR, tiles), bf16)],
        aliases={10: 5, 11: 6, 12: 7},
    )(
        matrix,
        rows,
        meta,
        x_first,
        x_second,
        y_second,
        c_second,
        begun,
        image_early,
        begun_image,
        *(pltpu.with_memory_space_constraint(left, pltpu.VMEM) for left in lefts_begun),
    )
    y_second = swapped(y_second, 0, 2)
    c_first, c_second = swapped(c_first, 1, 2), swapped(c_second, 2, 2)
    y_first = swapped(y_first, 0, 1)
    x_first, x_second = call(relay_kernel, [VMEM] * 2, [sent(TO_X[1]), sent(TO_X[-1])])(rest, y_first)
    x_first, x_second = swapped(x_first, 1, 0), swapped(x_second, 2, 0)
    (own,) = call(own_kernel, [VMEM] * 5, [((len(OWN), HALF, PAIR), f32)], cost=3_000_000_000)(
        rest, y_first, y_second, c_first, c_second
    )
    (out,) = call(
        finish_kernel,
        [VMEM] * 3 + [HBM],
        [whole],
        [pltpu.VMEM((7, 7, B, B), bf16), pltpu.SemaphoreType.DMA((7,))],
        [HBM],
        {3: 0},
    )(own, x_first, x_second, out)
    return out[None, None]


def solution(mesh):
    return jax.shard_map(
        per_device,
        mesh=mesh,
        in_specs=(
            P("sx", "sy", None, None, None, None),
            P("sx", "sy", None, None, None, None),
            P("sx", "sy", None),
            P("sx", "sy", None, None),
        ),
        out_specs=P("sx", "sy", None, None, None, None),
        check_vma=False,
    )
```

```python
import functools

import jax
import jax.numpy as jnp
from jax import lax
from jax.experimental import pallas as pl
from jax.experimental.pallas import tpu as pltpu
from jax.sharding import PartitionSpec as P


B = 64
HALF = B // 2
PAIR = 2 * B
SLOTS = 6
BLOCK_ROWS = SLOTS * B
BODY = 2 * BLOCK_ROWS
TAIL = 16
VMEM_LIMIT = 20 * 1024 * 1024

FACES = [(0, 0), (-1, 0), (1, 0), (0, -1), (0, 1), (0, 0)]
COLUMNS = [(0, 0), (0, 1), (1, 0), (1, 1)]
SIDES_X = (0, 2, 1, 3, 4, 5)
SIDES_Y = (0, 1, 2, 4, 3, 5)


def targets(px, py):
    table = []
    for dx, dy in FACES:
        ox, nx = divmod(px + dx, 2)
        oy, ny = divmod(py + dy, 2)
        table.append([(ox, oy), (ox + 2 * nx - 1, oy), (ox, oy + 2 * ny - 1)])
    return table


def box_set(px, py):
    return sorted({t for row in targets(px, py) for t in row})


def around(px, py):
    found = [(0, (0, 0), (px, py))]
    for m in (2, 1) if px == 0 else (1, 2):
        ox, nx = divmod(px + FACES[m][0], 2)
        found.append((m, (ox, 0), (nx, py)))
    for m in (4, 3) if py == 0 else (3, 4):
        oy, ny = divmod(py + FACES[m][1], 2)
        found.append((m, (0, oy), (px, ny)))
    found.append((5, (0, 0), (px, py)))
    return found


def image_set(px, py):
    found = set()
    for _, (ox, oy), column in around(px, py):
        found |= {(ox + tx, oy + ty) for tx, ty in box_set(*column)}
    return sorted(found)


IMAGE = sorted({s for column in COLUMNS for s in image_set(*column)})
IMAGE_PAIRS = (len(IMAGE) + 1) // 2
STAR = [(0, 1), (0, -1), (0, 0), (1, 0), (-1, 0)]


def column_of(tx, ty):
    return ((tx + 1) // 2, (ty + 1) // 2)


def blocks_of(tx, ty):
    return IMAGE if (tx, ty) in STAR else image_set(*column_of(tx, ty))


TO_Y_FIRST = [((tx, 1), s) for tx in (0, -1, 1) for s in blocks_of(tx, 1)]
TO_Y_SECOND = [((0, -1), s) for s in blocks_of(0, -1)]
TO_C_FIRST = [((1, -1), s) for s in blocks_of(1, -1)]
TO_C_SECOND = [((-1, -1), s) for s in blocks_of(-1, -1)]


def relayed(tx):
    return {(s[0], 1 - s[1]): row for row, (t, s) in enumerate(TO_Y_FIRST) if t[0] == tx}


TO_X = {tx: sorted(set(IMAGE) | set(relayed(tx))) for tx in (1, -1)}
STENCIL = [(jx, jy) for jx in range(-3, 4) for jy in range(-3, 4) if abs(jx) + abs(jy) <= 3]
OWN = sorted(
    set(IMAGE)
    | set(relayed(0))
    | {(s[0], -1 - s[1]) for _, s in TO_Y_SECOND}
    | {(1 - s[0], -1 - s[1]) for _, s in TO_C_FIRST}
    | {(-1 - s[0], -1 - s[1]) for _, s in TO_C_SECOND}
)


def low_half(shape):
    return lax.broadcasted_iota(jnp.int32, shape, len(shape) - 1) < B


def swap_halves(value):
    return pltpu.roll(value, B, value.ndim - 1)


def pair_lanes(left, right):
    return jnp.concatenate([left, right], axis=-1)


def mirrored():
    return lax.axis_index("sx") % 2, lax.axis_index("sy") % 2


def slot_here(m, z, odd_x, odd_y):
    if m in (1, 2):
        return jnp.where(odd_x == 1, 3 - m, m)
    if m in (3, 4):
        return jnp.where(odd_y == 1, 7 - m, m)
    return 6 - z if m == 5 else m


def fill_rows(rows, values):
    shape = (rows, PAIR)
    row = lax.broadcasted_iota(jnp.int32, shape, 0)
    half = low_half(shape)
    filled = jnp.zeros(shape, jnp.float32)
    for index, (low, high) in enumerate(values):
        filled = jnp.where(row == index, jnp.where(half, low, high), filled)
    return filled


def pack_kernel(
    boxes_y,
    aggregate_hbm,
    links_hbm,
    p_hbm,
    rows_ref,
    meta_ref,
    x_first,
    x_second,
    y_first,
    y_second,
    p_ref,
    aggregate_ref,
    links_ref,
    p_sems,
    sems,
):
    odd_x, odd_y = mirrored()
    own = lax.axis_index("sx") * boxes_y + lax.axis_index("sy")
    place = {(px, py): (px ^ odd_x, py ^ odd_y) for px, py in COLUMNS}
    copies = [
        pltpu.make_async_copy(p_hbm.at[place[column]], p_ref.at[index], p_sems.at[index])
        for index, column in enumerate(COLUMNS)
    ]
    small = [
        pltpu.make_async_copy(aggregate_hbm, aggregate_ref, sems.at[0]),
        pltpu.make_async_copy(links_hbm, links_ref, sems.at[1]),
    ]
    for copy in small + copies:
        copy.start()
    for copy in small:
        copy.wait()

    def state(column, z):
        shift = aggregate_ref[place[column] + (z,)] - own
        across_x = (shift == boxes_y) | (shift == -boxes_y)
        return jnp.where(shift == 0, 0, jnp.where(across_x, 1, 2)).astype(jnp.float32)

    def link(column, m):
        faces = [slot_here(m, z, odd_x, odd_y) - 1 for z in (0, 1)]
        return tuple(links_ref[place[column] + (z, faces[z])].astype(jnp.float32) for z in (0, 1))

    states = [tuple(state(column, z) for z in (0, 1)) for column in COLUMNS]
    links = {column: [link(column, m) for m in range(1, SLOTS)] for column in COLUMNS}
    meta_ref[...] = fill_rows(32, states + sum((links[column] for column in COLUMNS), []))
    messages = (
        (x_first, ((1, 0), (1, 1))),
        (x_second, ((0, 0), (0, 1))),
        (y_first, ((0, 1), (1, 1))),
        (y_second, ((0, 0), (1, 0))),
    )
    for ref, columns in messages:
        tail = fill_rows(TAIL, states + links[columns[0]] + links[columns[1]])
        ref[BODY : BODY + TAIL, :] = tail.astype(jnp.bfloat16)
    for index, column in enumerate(COLUMNS):
        copies[index].wait()
        for m in range(SLOTS):
            packed = pair_lanes(*(p_ref[index, z, slot_here(m, z, odd_x, odd_y)] for z in (0, 1)))
            rows_ref[index, m * B : (m + 1) * B, :] = packed
            for ref, columns in messages:
                if column in columns:
                    start = columns.index(column) * BLOCK_ROWS + m * B
                    ref[start : start + B, :] = packed


def notes_kernel(x_first, x_second, _, notes_ref, again_ref):
    for ref in (notes_ref, again_ref):
        ref[0:TAIL, :] = x_first[BODY : BODY + TAIL, :]
        ref[TAIL : 2 * TAIL, :] = x_second[BODY : BODY + TAIL, :]


def pack_matrix_kernel(links_hbm, a_hbm, out_ref, whole_hbm, a_ref, links_ref, zeros, a_sems, sems):
    fetches = [
        pltpu.make_async_copy(links_hbm, links_ref, a_sems.at[4]),
        *(
            pltpu.make_async_copy(a_hbm.at[px, py], a_ref.at[px, py], a_sems.at[index])
            for index, (px, py) in enumerate(COLUMNS)
        ),
    ]
    for fetch in fetches:
        fetch.start()
    zeros[...] = jnp.zeros(zeros.shape, zeros.dtype)
    copies = []
    for jx in range(-3, 4):
        width = abs(jx)
        if width:
            for start in (0, 7 - width):
                copies.append(
                    pltpu.make_async_copy(
                        zeros.at[pl.ds(0, width)], whole_hbm.at[jx + 3, pl.ds(start, width)], sems.at[len(copies)]
                    )
                )
    for copy in copies:
        copy.start()
    for fetch in fetches:
        fetch.wait()
    odd_x, odd_y = mirrored()
    for index, (px, py) in enumerate(COLUMNS):
        place = (px ^ odd_x, py ^ odd_y)
        for z in (0, 1):
            blocks = []
            for m, _, _ in around(px, py):
                slot = slot_here(m, z, odd_x, odd_y)
                block = a_ref[place + (z, slot)]
                if m > 0:
                    present = links_ref[place + (z, slot - 1)] == 1
                    block = jnp.where(present, block, jnp.zeros_like(block))
                blocks.append(block)
            for pair in range(3):
                out_ref[index, z * B : (z + 1) * B, pair * PAIR : (pair + 1) * PAIR] = pair_lanes(
                    blocks[2 * pair], blocks[2 * pair + 1]
                )
    for copy in copies:
        copy.wait()


def there(ox, oy, px, py):
    return (1 - px if ox else px, 1 - py if oy else py)


def slot_there(ox, oy, m):
    m = SIDES_X[m] if ox else m
    return SIDES_Y[m] if oy else m


class Rows:
    def __init__(self, rows_ref, meta_ref, from_x, from_y, corners):
        self.rows_ref, self.from_x, self.from_y = rows_ref, from_x, from_y
        self.notes = {(0, 0): meta_ref[...]}
        for side, ref in from_x.items():
            self.notes[side, 0] = ref[BODY : BODY + TAIL, :].astype(jnp.float32)
        for side, ref in from_y.items():
            self.notes[0, side] = ref[BODY : BODY + TAIL, :].astype(jnp.float32)
        for oy, ref in corners.items():
            self.notes[1, oy] = ref[0:TAIL, :].astype(jnp.float32)
            self.notes[-1, oy] = ref[TAIL : 2 * TAIL, :].astype(jnp.float32)

    def state_row(self, ox, oy, px, py):
        index = COLUMNS.index(there(ox, oy, px, py))
        return self.notes[ox, oy][index : index + 1]

    def link_row(self, ox, oy, px, py, m):
        if (ox, oy) == (0, 0):
            index = (SLOTS - 1) * COLUMNS.index((px, py))
        else:
            index = (SLOTS - 1) * (py if ox else px)
        index += 4 + slot_there(ox, oy, m) - 1
        return self.notes[ox, oy][index : index + 1]

    def block(self, ox, oy, px, py, m, chunk):
        start = slot_there(ox, oy, m) * B + chunk * 16
        if (ox, oy) == (0, 0):
            return self.rows_ref[COLUMNS.index((px, py)), start : start + 16, :]
        start += (py if ox else px) * BLOCK_ROWS
        ref = self.from_x[ox] if ox else self.from_y[oy]
        return ref[start : start + 16, :]

    def sums(self, box, column, slots, begun=None):
        (ox, oy), (px, py) = box, column
        weights = {}
        for m in slots:
            dx, dy = FACES[m]
            bx, nx = divmod(2 * ox + px + dx, 2)
            by, ny = divmod(2 * oy + py + dy, 2)
            state = self.state_row(bx, by, nx, ny)
            if m == 5:
                state = swap_halves(state)
            for kind in range(3):
                weight = jnp.where(state == kind, 1.0, 0.0)
                if m > 0:
                    weight = weight * self.link_row(ox, oy, px, py, m)
                weights[m, kind] = jnp.broadcast_to(weight, (16, PAIR))
        reach = targets(px, py)
        chunks = {}
        for chunk in range(4):
            values = {m: self.block(ox, oy, px, py, m, chunk).astype(jnp.float32) for m in slots}
            for t in box_set(px, py):
                total = begun[t][chunk * 16 : chunk * 16 + 16] if begun and t in begun else None
                for m in slots:
                    for kind in range(3):
                        if reach[m][kind] == t:
                            term = values[m] * weights[m, kind]
                            total = term if total is None else total + term
                if total is not None:
                    chunks.setdefault(t, []).append(total)
        return {t: jnp.concatenate(parts, axis=0) for t, parts in chunks.items()}


IMAGES = {column: image_set(*column) for column in COLUMNS}
USERS = {}
for _index, _column in enumerate(COLUMNS):
    for _place, (_, _box, _other) in enumerate(around(*_column)):
        USERS.setdefault((_box, _other), []).append((_index, _column, _place))
BEGUN = {
    (box, (px, py)): (1 if px == 0 else 2) if box == (0, 1) else (3 if py == 0 else 4)
    for box, (px, py) in USERS
    if box[1] == 1 or box[0] or (box == (0, 0) and py == 0)
}
LATE = [key for key in USERS if key[0][1] == -1]


def begun_targets(key):
    return targets(*key[1])[BEGUN[key]]


def place_rows(found, box, other, right, left_star, left_corner):
    unit = None
    if box == (0, 0):
        square = (PAIR, PAIR)
        diagonal = lax.broadcasted_iota(jnp.int32, square, 0) == lax.broadcasted_iota(jnp.int32, square, 1)
        unit = jnp.where(diagonal, 1.0, 0.0).astype(jnp.bfloat16)
    own = COLUMNS.index(other)
    for t, value in found.items():
        rounded = value.astype(jnp.bfloat16)
        for index, column, place in USERS[box, other]:
            position = IMAGES[column].index((box[0] + t[0], box[1] + t[1]))
            stored = swap_halves(value).astype(jnp.bfloat16) if place == 5 else rounded
            right[index, place * B : (place + 1) * B, position * PAIR : (position + 1) * PAIR] = stored
        if box == (0, 0):
            turned = lax.dot_general(
                unit, rounded, (((1,), (1,)), ((), ())), preferred_element_type=jnp.float32
            ).astype(jnp.bfloat16)
            turned = pair_lanes(turned[:B], turned[B:])
            if t in STAR:
                left_star[STAR.index(t) * B : (STAR.index(t) + 1) * B, own * PAIR : (own + 1) * PAIR] = turned
            else:
                left_corner[own] = turned


def begin_kernel(rows_ref, meta_ref, x_first, x_second, y_first, right, left_star, left_corner, begun_ref):
    rows = Rows(rows_ref, meta_ref, {1: x_first, -1: x_second}, {1: y_first}, {})
    for index, column in enumerate(COLUMNS):
        for place, (_, box, other) in enumerate(around(*column)):
            reached = {(box[0] + tx, box[1] + ty) for tx, ty in box_set(*other)}
            for position, s in enumerate(IMAGES[column]):
                if s not in reached:
                    right[index, place * B : (place + 1) * B, position * PAIR : (position + 1) * PAIR] = jnp.zeros(
                        (B, PAIR), jnp.bfloat16
                    )
    for box, other in USERS:
        if (box, other) in LATE:
            continue
        slots = list(range(SLOTS))
        open_targets = []
        if (box, other) in BEGUN:
            slots.remove(BEGUN[box, other])
            open_targets = begun_targets((box, other))
        found = rows.sums(box, other, slots)
        for place, t in enumerate(open_targets):
            begun_ref[list(BEGUN).index((box, other)), place] = found.pop(t)
        place_rows(found, box, other, right, left_star, left_corner)


def main_kernel(
    a_ref,
    rows_ref,
    meta_ref,
    x_first,
    x_second,
    y_first,
    y_second,
    c_first,
    c_second,
    begun_ref,
    right_in,
    left_star_in,
    left_corner_in,
    to_y_first,
    to_y_second,
    to_c_first,
    to_c_second,
    rest_ref,
    right,
    left_star,
    left_corner,
    image,
):
    images = IMAGES
    rows = Rows(rows_ref, meta_ref, {1: x_first, -1: x_second}, {1: y_first, -1: y_second}, {1: c_first, -1: c_second})
    for number, ((box, other), slot) in enumerate(BEGUN.items()):
        begun = {t: begun_ref[number, place] for place, t in enumerate(begun_targets((box, other)))}
        place_rows(rows.sums(box, other, [slot], begun), box, other, right, left_star, left_corner)
    for box, other in LATE:
        place_rows(rows.sums(box, other, list(range(SLOTS))), box, other, right, left_star, left_corner)
    half = low_half((B, PAIR))
    for index, column in enumerate(COLUMNS):
        product = jnp.dot(a_ref[index], right[index], preferred_element_type=jnp.float32)

        def part(s, z):
            if s not in images[column]:
                return jnp.zeros((B, PAIR), jnp.float32)
            position = images[column].index(s)
            return product[z * B : (z + 1) * B, position * PAIR : (position + 1) * PAIR]

        for pair in range(IMAGE_PAIRS):
            one = IMAGE[2 * pair]
            two = IMAGE[2 * pair + 1] if 2 * pair + 1 < len(IMAGE) else None
            low = jnp.where(half, part(one, 0), swap_halves(part(two, 0)))
            high = jnp.where(half, swap_halves(part(one, 1)), part(two, 1))
            start = index * PAIR
            lanes = slice(pair * PAIR, (pair + 1) * PAIR)
            image[start : start + B, lanes] = low.astype(jnp.bfloat16)
            image[start + B : start + PAIR, lanes] = high.astype(jnp.bfloat16)
    folded_half = low_half((HALF, PAIR))

    def fold(product):
        blocks = {}
        for pair in range(IMAGE_PAIRS):
            tile = product[:, pair * PAIR : (pair + 1) * PAIR]
            top, bottom = tile[:HALF], tile[HALF:]
            blocks[IMAGE[2 * pair]] = jnp.where(folded_half, top, swap_halves(bottom))
            if 2 * pair + 1 < len(IMAGE):
                blocks[IMAGE[2 * pair + 1]] = jnp.where(folded_half, swap_halves(top), bottom)
        return blocks

    star = jnp.dot(left_star[...], image[...], preferred_element_type=jnp.float32)

    def contribution(t):
        if t in STAR:
            return fold(star[STAR.index(t) * B : (STAR.index(t) + 1) * B])
        index = COLUMNS.index(column_of(*t))
        return fold(
            jnp.dot(
                left_corner[index], image[index * PAIR : (index + 1) * PAIR, :], preferred_element_type=jnp.float32
            )
        )

    for ref, sent in (
        (to_y_first, TO_Y_FIRST),
        (to_y_second, TO_Y_SECOND),
        (to_c_first, TO_C_FIRST),
        (to_c_second, TO_C_SECOND),
    ):
        parts = {t: contribution(t) for t in sorted({t for t, _ in sent})}
        for row, (t, s) in enumerate(sent):
            ref[row * HALF : (row + 1) * HALF, :] = parts[t][s].astype(jnp.bfloat16)
    for group, tx in enumerate((0, -1, 1)):
        parts = contribution((tx, 0))
        for position, s in enumerate(IMAGE):
            rest_ref[group, position] = parts[s]


def message_block(ref, row):
    return ref[row * HALF : (row + 1) * HALF, :].astype(jnp.float32)


def relay_kernel(rest_ref, y_first, x_first, x_second):
    for ref, tx in ((x_first, 1), (x_second, -1)):
        arrived = relayed(tx)
        for row, s in enumerate(TO_X[tx]):
            value = None
            if s in IMAGE:
                value = rest_ref[(0, -1, 1).index(tx), IMAGE.index(s)]
            if s in arrived:
                more = message_block(y_first, arrived[s])
                value = more if value is None else value + more
            ref[row * HALF : (row + 1) * HALF, :] = value.astype(jnp.bfloat16)


def gathered(terms):
    total = None
    for ref, row, flag in terms:
        value = message_block(ref, row) if row is not None else ref
        if flag is not None:
            value = value * flag
        total = value if total is None else total + value
    return total


def inside():
    x, y = lax.axis_index("sx"), lax.axis_index("sy")
    return (
        ((x > 0) & (x < lax.axis_size("sx") - 1)).astype(jnp.float32),
        ((y > 0) & (y < lax.axis_size("sy") - 1)).astype(jnp.float32),
    )


def own_kernel(rest_ref, y_first, y_second, c_first, c_second, own_ref):
    has_x, has_y = inside()
    terms = {block: [] for block in STENCIL}
    for position, s in enumerate(IMAGE):
        terms[s].append((rest_ref[0, position], None, None))
    for s, row in relayed(0).items():
        terms[s].append((y_first, row, None))
    for row, (_, s) in enumerate(TO_Y_SECOND):
        terms[s[0], -1 - s[1]].append((y_second, row, has_y))
    for row, (_, s) in enumerate(TO_C_FIRST):
        terms[1 - s[0], -1 - s[1]].append((c_first, row, has_y))
    for row, (_, s) in enumerate(TO_C_SECOND):
        terms[-1 - s[0], -1 - s[1]].append((c_second, row, has_x * has_y))
    for position, block in enumerate(OWN):
        own_ref[position] = gathered(terms[block])


def finish_kernel(own_ref, x_first, x_second, _, out_hbm, rows, sems):
    odd_x, odd_y = mirrored()
    has_x, _ = inside()
    terms = {block: [] for block in STENCIL}
    for position, block in enumerate(OWN):
        terms[block].append((own_ref[position], None, None))
    for row, s in enumerate(TO_X[1]):
        terms[1 - s[0], s[1]].append((x_first, row, None))
    for row, s in enumerate(TO_X[-1]):
        terms[-1 - s[0], s[1]].append((x_second, row, has_x))
    copies = []
    for jx in (0, 1, -1, 2, -2, 3, -3):
        row_here = jnp.where(odd_x == 1, 3 - jx, 3 + jx)
        reach = 3 - abs(jx)
        for jy in range(-reach, reach + 1):
            value = gathered(terms[jx, jy])
            column_here = jnp.where(odd_y == 1, 3 - jy, 3 + jy)
            rows[jx + 3, column_here, 0:HALF, :] = value[:, :B].astype(jnp.bfloat16)
            rows[jx + 3, column_here, HALF:B, :] = swap_halves(value)[:, :B].astype(jnp.bfloat16)
        span = pl.ds(3 - reach, 2 * reach + 1)
        copy = pltpu.make_async_copy(rows.at[jx + 3, span], out_hbm.at[row_here, span], sems.at[jx + 3])
        copy.start()
        copies.append(copy)
    for copy in copies:
        copy.wait()


def swapped(value, move_x, move_y):
    count_x, count_y = lax.axis_size("sx"), lax.axis_size("sy")

    def partner(index, move, count):
        if move == 0:
            return index
        found = index ^ 1 if move == 1 else ((index + 1) ^ 1) - 1
        return found if 0 <= found < count else None

    pairs = []
    for x in range(count_x):
        for y in range(count_y):
            to_x, to_y = partner(x, move_x, count_x), partner(y, move_y, count_y)
            if to_x is None:
                to_x, to_y = x, y ^ 1
            elif to_y is None:
                to_x, to_y = (x ^ 1 if move_x == 0 else to_x), y
            pairs.append((x * count_y + y, to_x * count_y + to_y))
    return lax.ppermute(value, ("sx", "sy"), pairs)


SMEM = pl.BlockSpec(memory_space=pltpu.SMEM)
VMEM = pl.BlockSpec(memory_space=pltpu.VMEM)
HBM = pl.BlockSpec(memory_space=pltpu.HBM)
ANY = pl.BlockSpec(memory_space=pl.ANY)


def call(kernel, in_specs, outs, scratch=(), out_specs=None, aliases=None, cost=None):
    return pl.pallas_call(
        kernel,
        out_shape=[jax.ShapeDtypeStruct(shape, dtype) for shape, dtype in outs],
        in_specs=in_specs,
        out_specs=out_specs or [VMEM] * len(outs),
        scratch_shapes=list(scratch),
        input_output_aliases=aliases or {},
        compiler_params=pltpu.CompilerParams(vmem_limit_bytes=VMEM_LIMIT),
        cost_estimate=None if cost is None else pl.CostEstimate(flops=cost, bytes_accessed=1, transcendentals=0),
    )


def in_hbm(*values):
    return [pltpu.with_memory_space_constraint(value, pltpu.HBM) for value in values]


def per_device(fine_matrix, prolongator, aggregate, face_links):
    bf16, f32 = jnp.bfloat16, jnp.float32
    message = ((BODY + TAIL, PAIR), bf16)
    longer = ((BODY + 2 * TAIL, PAIR), bf16)
    rows, meta, x_first, x_second, y_first, y_second = call(
        functools.partial(pack_kernel, lax.axis_size("sy")),
        [HBM, HBM, HBM],
        [((4, BLOCK_ROWS, PAIR), bf16), ((32, PAIR), f32), message, message, message, longer],
        [
            pltpu.VMEM((4, 2, 7, B, B), bf16),
            pltpu.SMEM((2, 2, 2), jnp.int32),
            pltpu.SMEM((2, 2, 2, 6), jnp.int32),
            pltpu.SemaphoreType.DMA((4,)),
            pltpu.SemaphoreType.DMA((2,)),
        ],
    )(*in_hbm(aggregate, face_links, prolongator))
    y_second = swapped(y_second, 0, 2)
    x_first, x_second = swapped(x_first, 1, 0), swapped(x_second, 2, 0)
    y_first = swapped(y_first, 0, 1)
    whole = ((7, 7, B, B), bf16)
    matrix, out = call(
        pack_matrix_kernel,
        [HBM, HBM],
        [((4, PAIR, 6 * B), bf16), whole],
        [
            pltpu.VMEM((2, 2, 2, 7, B, B), bf16),
            pltpu.SMEM((2, 2, 2, 6), jnp.int32),
            pltpu.VMEM((3, B, B), bf16),
            pltpu.SemaphoreType.DMA((5,)),
            pltpu.SemaphoreType.DMA((12,)),
        ],
        [VMEM, HBM],
    )(*in_hbm(face_links, fine_matrix))
    note = ((2 * TAIL, PAIR), bf16)
    notes, notes_again = call(notes_kernel, [VMEM, VMEM, ANY], [note, ((48, PAIR), bf16)])(
        x_first, x_second, matrix
    )
    c_first, c_second = swapped(notes, 0, 1), swapped(notes_again, 0, 2)

    def sent(blocks):
        return ((len(blocks) * HALF, PAIR), bf16)

    lefts = [
        ((4, SLOTS * B, 10 * PAIR), bf16),
        ((len(STAR) * B, 4 * PAIR), bf16),
        ((4, B, PAIR), bf16),
    ]
    *lefts_begun, begun = call(begin_kernel, [VMEM] * 5, lefts + [((len(BEGUN), 3, B, PAIR), f32)], cost=1)(
        rows, meta, x_first, x_second, y_first
    )
    y_first, y_second, c_first, c_second, rest, *_ = call(
        main_kernel,
        [VMEM] * 13,
        [
            sent(TO_Y_FIRST),
            sent(TO_Y_SECOND),
            sent(TO_C_FIRST),
            sent(TO_C_SECOND),
            ((3, len(IMAGE), HALF, PAIR), f32),
        ]
        + lefts,
        [pltpu.VMEM((4 * PAIR, IMAGE_PAIRS * PAIR), bf16)],
        aliases={10: 5, 11: 6, 12: 7},
    )(
        matrix,
        rows,
        meta,
        x_first,
        x_second,
        y_first,
        y_second,
        c_first,
        c_second,
        begun,
        *(pltpu.with_memory_space_constraint(left, pltpu.VMEM) for left in lefts_begun),
    )
    y_second = swapped(y_second, 0, 2)
    c_first, c_second = swapped(c_first, 1, 2), swapped(c_second, 2, 2)
    y_first = swapped(y_first, 0, 1)
    x_first, x_second = call(relay_kernel, [VMEM] * 2, [sent(TO_X[1]), sent(TO_X[-1])])(rest, y_first)
    x_first, x_second = swapped(x_first, 1, 0), swapped(x_second, 2, 0)
    (own,) = call(own_kernel, [VMEM] * 5, [((len(OWN), HALF, PAIR), f32)], cost=3_000_000_000)(
        rest, y_first, y_second, c_first, c_second
    )
    (out,) = call(
        finish_kernel,
        [VMEM] * 3 + [HBM],
        [whole],
        [pltpu.VMEM((7, 7, B, B), bf16), pltpu.SemaphoreType.DMA((7,))],
        [HBM],
        {3: 0},
    )(own, x_first, x_second, out)
    return out[None, None]


def solution(mesh):
    return jax.shard_map(
        per_device,
        mesh=mesh,
        in_specs=(
            P("sx", "sy", None, None, None, None),
            P("sx", "sy", None, None, None, None),
            P("sx", "sy", None),
            P("sx", "sy", None, None),
        ),
        out_specs=P("sx", "sy", None, None, None, None),
        check_vma=False,
    )
```

```python
import functools

import jax
import jax.numpy as jnp
from jax import lax
from jax.experimental import pallas as pl
from jax.experimental.pallas import tpu as pltpu
from jax.sharding import PartitionSpec as P


B = 64
HALF = B // 2
PAIR = 2 * B
SLOTS = 6
BLOCK_ROWS = SLOTS * B
BODY = 2 * BLOCK_ROWS
TAIL = 16
VMEM_LIMIT = 20 * 1024 * 1024

FACES = [(0, 0), (-1, 0), (1, 0), (0, -1), (0, 1), (0, 0)]
COLUMNS = [(0, 0), (0, 1), (1, 0), (1, 1)]
SIDES_X = (0, 2, 1, 3, 4, 5)
SIDES_Y = (0, 1, 2, 4, 3, 5)


def targets(px, py):
    table = []
    for dx, dy in FACES:
        ox, nx = divmod(px + dx, 2)
        oy, ny = divmod(py + dy, 2)
        table.append([(ox, oy), (ox + 2 * nx - 1, oy), (ox, oy + 2 * ny - 1)])
    return table


def box_set(px, py):
    return sorted({t for row in targets(px, py) for t in row})


def around(px, py):
    (mx, out_x), (my, out_y) = (2, 1) if px == 0 else (1, 2), (4, 3) if py == 0 else (3, 4)
    found = []
    for m in (0, 5, mx, my, out_x, out_y):
        ox, nx = divmod(px + FACES[m][0], 2)
        oy, ny = divmod(py + FACES[m][1], 2)
        found.append((m, (ox, oy), (nx, ny)))
    return found


def image_set(px, py):
    found = set()
    for _, (ox, oy), column in around(px, py):
        found |= {(ox + tx, oy + ty) for tx, ty in box_set(*column)}
    return sorted(found)


IMAGE = sorted({s for column in COLUMNS for s in image_set(*column)})
IMAGE_PAIRS = (len(IMAGE) + 1) // 2
STAR = [(0, 1), (0, -1), (1, 0), (-1, 0), (0, 0)]


def column_of(tx, ty):
    return ((tx + 1) // 2, (ty + 1) // 2)


def blocks_of(tx, ty):
    return IMAGE if (tx, ty) in STAR else image_set(*column_of(tx, ty))


TO_Y_FIRST = [((tx, 1), s) for tx in (0, -1, 1) for s in blocks_of(tx, 1)]
TO_Y_SECOND = [((0, -1), s) for s in blocks_of(0, -1)]
TO_C_FIRST = [((1, -1), s) for s in blocks_of(1, -1)]
TO_C_SECOND = [((-1, -1), s) for s in blocks_of(-1, -1)]


def relayed(tx):
    return {(s[0], 1 - s[1]): row for row, (t, s) in enumerate(TO_Y_FIRST) if t[0] == tx}


TO_X = {tx: sorted(set(IMAGE) | set(relayed(tx))) for tx in (1, -1)}
STENCIL = [(jx, jy) for jx in range(-3, 4) for jy in range(-3, 4) if abs(jx) + abs(jy) <= 3]
OWN = sorted(
    set(IMAGE)
    | set(relayed(0))
    | {(s[0], -1 - s[1]) for _, s in TO_Y_SECOND}
    | {(1 - s[0], -1 - s[1]) for _, s in TO_C_FIRST}
    | {(-1 - s[0], -1 - s[1]) for _, s in TO_C_SECOND}
)


def low_half(shape):
    return lax.broadcasted_iota(jnp.int32, shape, len(shape) - 1) < B


def swap_halves(value):
    return pltpu.roll(value, B, value.ndim - 1)


def pair_lanes(left, right):
    return jnp.concatenate([left, right], axis=-1)


def mirrored():
    return lax.axis_index("sx") % 2, lax.axis_index("sy") % 2


def slot_here(m, z, odd_x, odd_y):
    if m in (1, 2):
        return jnp.where(odd_x == 1, 3 - m, m)
    if m in (3, 4):
        return jnp.where(odd_y == 1, 7 - m, m)
    return 6 - z if m == 5 else m


def fill_rows(rows, values):
    shape = (rows, PAIR)
    row = lax.broadcasted_iota(jnp.int32, shape, 0)
    half = low_half(shape)
    filled = jnp.zeros(shape, jnp.float32)
    for index, (low, high) in enumerate(values):
        filled = jnp.where(row == index, jnp.where(half, low, high), filled)
    return filled


def pack_kernel(
    boxes_y,
    aggregate_hbm,
    links_hbm,
    p_hbm,
    rows_ref,
    meta_ref,
    x_first,
    x_second,
    y_first,
    y_second,
    p_ref,
    aggregate_ref,
    links_ref,
    p_sems,
    sems,
):
    odd_x, odd_y = mirrored()
    own = lax.axis_index("sx") * boxes_y + lax.axis_index("sy")
    place = {(px, py): (px ^ odd_x, py ^ odd_y) for px, py in COLUMNS}
    copies = [
        pltpu.make_async_copy(p_hbm.at[place[column]], p_ref.at[index], p_sems.at[index])
        for index, column in enumerate(COLUMNS)
    ]
    small = [
        pltpu.make_async_copy(aggregate_hbm, aggregate_ref, sems.at[0]),
        pltpu.make_async_copy(links_hbm, links_ref, sems.at[1]),
    ]
    for copy in small + copies:
        copy.start()
    for copy in small:
        copy.wait()

    def state(column, z):
        shift = aggregate_ref[place[column] + (z,)] - own
        across_x = (shift == boxes_y) | (shift == -boxes_y)
        return jnp.where(shift == 0, 0, jnp.where(across_x, 1, 2)).astype(jnp.float32)

    def link(column, m):
        faces = [slot_here(m, z, odd_x, odd_y) - 1 for z in (0, 1)]
        return tuple(links_ref[place[column] + (z, faces[z])].astype(jnp.float32) for z in (0, 1))

    states = [tuple(state(column, z) for z in (0, 1)) for column in COLUMNS]
    links = {column: [link(column, m) for m in range(1, SLOTS)] for column in COLUMNS}
    meta_ref[...] = fill_rows(32, states + sum((links[column] for column in COLUMNS), []))
    messages = (
        (x_first, ((1, 0), (1, 1))),
        (x_second, ((0, 0), (0, 1))),
        (y_first, ((0, 1), (1, 1))),
        (y_second, ((0, 0), (1, 0))),
    )
    for ref, columns in messages:
        tail = fill_rows(TAIL, states + links[columns[0]] + links[columns[1]])
        ref[BODY : BODY + TAIL, :] = tail.astype(jnp.bfloat16)
    for index, column in enumerate(COLUMNS):
        copies[index].wait()
        for m in range(SLOTS):
            packed = pair_lanes(*(p_ref[index, z, slot_here(m, z, odd_x, odd_y)] for z in (0, 1)))
            rows_ref[index, m * B : (m + 1) * B, :] = packed
            for ref, columns in messages:
                if column in columns:
                    start = columns.index(column) * BLOCK_ROWS + m * B
                    ref[start : start + B, :] = packed


def notes_kernel(x_first, x_second, _, notes_ref, again_ref):
    for ref in (notes_ref, again_ref):
        ref[0:TAIL, :] = x_first[BODY : BODY + TAIL, :]
        ref[TAIL : 2 * TAIL, :] = x_second[BODY : BODY + TAIL, :]


def pack_matrix_kernel(links_hbm, a_hbm, out_ref, whole_hbm, a_ref, links_ref, zeros, a_sems, sems):
    fetches = [
        pltpu.make_async_copy(links_hbm, links_ref, a_sems.at[4]),
        *(
            pltpu.make_async_copy(a_hbm.at[px, py], a_ref.at[px, py], a_sems.at[index])
            for index, (px, py) in enumerate(COLUMNS)
        ),
    ]
    for fetch in fetches:
        fetch.start()
    zeros[...] = jnp.zeros(zeros.shape, zeros.dtype)
    copies = []
    for jx in range(-3, 4):
        width = abs(jx)
        if width:
            for start in (0, 7 - width):
                copies.append(
                    pltpu.make_async_copy(
                        zeros.at[pl.ds(0, width)], whole_hbm.at[jx + 3, pl.ds(start, width)], sems.at[len(copies)]
                    )
                )
    for copy in copies:
        copy.start()
    for fetch in fetches:
        fetch.wait()
    odd_x, odd_y = mirrored()
    for index, (px, py) in enumerate(COLUMNS):
        place = (px ^ odd_x, py ^ odd_y)
        for z in (0, 1):
            blocks = []
            for m, _, _ in around(px, py):
                slot = slot_here(m, z, odd_x, odd_y)
                block = a_ref[place + (z, slot)]
                if m > 0:
                    present = links_ref[place + (z, slot - 1)] == 1
                    block = jnp.where(present, block, jnp.zeros_like(block))
                blocks.append(block)
            for pair in range(3):
                out_ref[index, z * B : (z + 1) * B, pair * PAIR : (pair + 1) * PAIR] = pair_lanes(
                    blocks[2 * pair], blocks[2 * pair + 1]
                )
    for copy in copies:
        copy.wait()


def there(ox, oy, px, py):
    return (1 - px if ox else px, 1 - py if oy else py)


def slot_there(ox, oy, m):
    m = SIDES_X[m] if ox else m
    return SIDES_Y[m] if oy else m


class Rows:
    def __init__(self, rows_ref, meta_ref, from_x, from_y, corners):
        self.rows_ref, self.from_x, self.from_y = rows_ref, from_x, from_y
        self.notes = {(0, 0): meta_ref[...]}
        for side, ref in from_x.items():
            self.notes[side, 0] = ref[BODY : BODY + TAIL, :].astype(jnp.float32)
        for side, ref in from_y.items():
            self.notes[0, side] = ref[BODY : BODY + TAIL, :].astype(jnp.float32)
        for oy, ref in corners.items():
            self.notes[1, oy] = ref[0:TAIL, :].astype(jnp.float32)
            self.notes[-1, oy] = ref[TAIL : 2 * TAIL, :].astype(jnp.float32)

    def state_row(self, ox, oy, px, py):
        index = COLUMNS.index(there(ox, oy, px, py))
        return self.notes[ox, oy][index : index + 1]

    def link_row(self, ox, oy, px, py, m):
        if (ox, oy) == (0, 0):
            index = (SLOTS - 1) * COLUMNS.index((px, py))
        else:
            index = (SLOTS - 1) * (py if ox else px)
        index += 4 + slot_there(ox, oy, m) - 1
        return self.notes[ox, oy][index : index + 1]

    def block(self, ox, oy, px, py, m, chunk):
        start = slot_there(ox, oy, m) * B + chunk * 16
        if (ox, oy) == (0, 0):
            return self.rows_ref[COLUMNS.index((px, py)), start : start + 16, :]
        start += (py if ox else px) * BLOCK_ROWS
        ref = self.from_x[ox] if ox else self.from_y[oy]
        return ref[start : start + 16, :]

    def sums(self, box, column, slots, begun=None):
        (ox, oy), (px, py) = box, column
        weights = {}
        for m in slots:
            dx, dy = FACES[m]
            bx, nx = divmod(2 * ox + px + dx, 2)
            by, ny = divmod(2 * oy + py + dy, 2)
            state = self.state_row(bx, by, nx, ny)
            if m == 5:
                state = swap_halves(state)
            for kind in range(3):
                weight = jnp.where(state == kind, 1.0, 0.0)
                if m > 0:
                    weight = weight * self.link_row(ox, oy, px, py, m)
                weights[m, kind] = jnp.broadcast_to(weight, (16, PAIR))
        reach = targets(px, py)
        chunks = {}
        for chunk in range(4):
            values = {m: self.block(ox, oy, px, py, m, chunk).astype(jnp.float32) for m in slots}
            for t in box_set(px, py):
                total = begun[t][chunk * 16 : chunk * 16 + 16] if begun and t in begun else None
                for m in slots:
                    for kind in range(3):
                        if reach[m][kind] == t:
                            term = values[m] * weights[m, kind]
                            total = term if total is None else total + term
                if total is not None:
                    chunks.setdefault(t, []).append(total)
        return {t: jnp.concatenate(parts, axis=0) for t, parts in chunks.items()}


def couplings_of(column, s):
    return [
        place
        for place, (_, (ox, oy), other) in enumerate(around(*column))
        if (s[0] - ox, s[1] - oy) in box_set(*other)
    ]


def grouped_images(column):
    groups = [[], [], []]
    for s in image_set(*column):
        places = couplings_of(column, s)
        groups[1 if max(places) < 4 else 2 if min(places) > 1 else 0].append(s)
    return groups


GROUPS = {column: grouped_images(column) for column in COLUMNS}
SPANS = (slice(0, 6 * B), slice(0, 4 * B), slice(2 * B, 6 * B))
IMAGES = {column: sum(GROUPS[column], []) for column in COLUMNS}
USERS = {}
for _index, _column in enumerate(COLUMNS):
    for _place, (_, _box, _other) in enumerate(around(*_column)):
        USERS.setdefault((_box, _other), []).append((_index, _column, _place))
BEGUN = {
    (box, (px, py)): (1 if px == 0 else 2) if box == (0, 1) else (3 if py == 0 else 4)
    for box, (px, py) in USERS
    if box[1] == 1 or box[0] or (box == (0, 0) and py == 0)
}
LATE = [key for key in USERS if key[0][1] == -1]


def begun_targets(key):
    return targets(*key[1])[BEGUN[key]]


def place_rows(found, box, other, right, left_star, left_corner):
    unit = None
    if box == (0, 0):
        square = (PAIR, PAIR)
        diagonal = lax.broadcasted_iota(jnp.int32, square, 0) == lax.broadcasted_iota(jnp.int32, square, 1)
        unit = jnp.where(diagonal, 1.0, 0.0).astype(jnp.bfloat16)
    own = COLUMNS.index(other)
    for t, value in found.items():
        rounded = value.astype(jnp.bfloat16)
        for index, column, place in USERS[box, other]:
            position = IMAGES[column].index((box[0] + t[0], box[1] + t[1]))
            stored = swap_halves(value).astype(jnp.bfloat16) if place == 1 else rounded
            right[index, place * B : (place + 1) * B, position * PAIR : (position + 1) * PAIR] = stored
        if box == (0, 0):
            turned = lax.dot_general(
                unit, rounded, (((1,), (1,)), ((), ())), preferred_element_type=jnp.float32
            ).astype(jnp.bfloat16)
            turned = pair_lanes(turned[:B], turned[B:])
            if t in STAR:
                left_star[STAR.index(t) * B : (STAR.index(t) + 1) * B, own * PAIR : (own + 1) * PAIR] = turned
            else:
                left_corner[own] = turned


def fold(product):
    folded_half = low_half((HALF, PAIR))
    blocks = {}
    for pair in range(IMAGE_PAIRS):
        tile = product[:, pair * PAIR : (pair + 1) * PAIR]
        top, bottom = tile[:HALF], tile[HALF:]
        blocks[IMAGE[2 * pair]] = jnp.where(folded_half, top, swap_halves(bottom))
        if 2 * pair + 1 < len(IMAGE):
            blocks[IMAGE[2 * pair + 1]] = jnp.where(folded_half, swap_halves(top), bottom)
    return blocks


def begin_kernel(rows_ref, meta_ref, x_first, x_second, y_first, right, left_star, left_corner, begun_ref):
    rows = Rows(rows_ref, meta_ref, {1: x_first, -1: x_second}, {1: y_first}, {})
    for index, column in enumerate(COLUMNS):
        for place, (_, box, other) in enumerate(around(*column)):
            reached = {(box[0] + tx, box[1] + ty) for tx, ty in box_set(*other)}
            spans = sum(([span] * len(group) for span, group in zip(SPANS, GROUPS[column])), [])
            for position, s in enumerate(IMAGES[column]):
                if s not in reached and spans[position].start <= place * B < spans[position].stop:
                    right[index, place * B : (place + 1) * B, position * PAIR : (position + 1) * PAIR] = jnp.zeros(
                        (B, PAIR), jnp.bfloat16
                    )
    for box, other in USERS:
        if (box, other) in LATE:
            continue
        slots = list(range(SLOTS))
        open_targets = []
        if (box, other) in BEGUN:
            slots.remove(BEGUN[box, other])
            open_targets = begun_targets((box, other))
        found = rows.sums(box, other, slots)
        for place, t in enumerate(open_targets):
            begun_ref[list(BEGUN).index((box, other)), place] = found.pop(t)
        place_rows(found, box, other, right, left_star, left_corner)


def main_kernel(
    a_ref,
    rows_ref,
    meta_ref,
    x_first,
    x_second,
    y_first,
    y_second,
    c_first,
    c_second,
    begun_ref,
    right_in,
    left_star_in,
    left_corner_in,
    to_y_first,
    to_y_second,
    to_c_first,
    to_c_second,
    rest_ref,
    right,
    left_star,
    left_corner,
    image,
):
    rows = Rows(rows_ref, meta_ref, {1: x_first, -1: x_second}, {1: y_first, -1: y_second}, {1: c_first, -1: c_second})
    for number, ((box, other), slot) in enumerate(BEGUN.items()):
        begun = {t: begun_ref[number, place] for place, t in enumerate(begun_targets((box, other)))}
        place_rows(rows.sums(box, other, [slot], begun), box, other, right, left_star, left_corner)
    for box, other in LATE:
        place_rows(rows.sums(box, other, list(range(SLOTS))), box, other, right, left_star, left_corner)
    half = low_half((B, PAIR))
    for index, column in enumerate(COLUMNS):
        products, start = {}, 0
        for span, group in zip(SPANS, GROUPS[column]):
            lanes = slice(start * PAIR, (start + len(group)) * PAIR)
            product = jnp.dot(a_ref[index, :, span], right[index, span, lanes], preferred_element_type=jnp.float32)
            for place, s in enumerate(group):
                products[s] = product[:, place * PAIR : (place + 1) * PAIR]
            start += len(group)

        def part(s, z):
            if s not in products:
                return jnp.zeros((B, PAIR), jnp.float32)
            return products[s][z * B : (z + 1) * B]

        for pair in range(IMAGE_PAIRS):
            one = IMAGE[2 * pair]
            two = IMAGE[2 * pair + 1] if 2 * pair + 1 < len(IMAGE) else None
            low = jnp.where(half, part(one, 0), swap_halves(part(two, 0)))
            high = jnp.where(half, swap_halves(part(one, 1)), part(two, 1))
            start = index * PAIR
            lanes = slice(pair * PAIR, (pair + 1) * PAIR)
            image[start : start + B, lanes] = low.astype(jnp.bfloat16)
            image[start + B : start + PAIR, lanes] = high.astype(jnp.bfloat16)
    star = jnp.dot(left_star[0 : 4 * B, :], image[...], preferred_element_type=jnp.float32)

    def contribution(t):
        if t in STAR:
            return fold(star[STAR.index(t) * B : (STAR.index(t) + 1) * B])
        index = COLUMNS.index(column_of(*t))
        return fold(
            jnp.dot(
                left_corner[index], image[index * PAIR : (index + 1) * PAIR, :], preferred_element_type=jnp.float32
            )
        )

    for ref, sent in (
        (to_y_first, TO_Y_FIRST),
        (to_y_second, TO_Y_SECOND),
        (to_c_first, TO_C_FIRST),
        (to_c_second, TO_C_SECOND),
    ):
        parts = {t: contribution(t) for t in sorted({t for t, _ in sent})}
        for row, (t, s) in enumerate(sent):
            ref[row * HALF : (row + 1) * HALF, :] = parts[t][s].astype(jnp.bfloat16)
    for group, tx in enumerate((-1, 1)):
        parts = contribution((tx, 0))
        for position, s in enumerate(IMAGE):
            rest_ref[group, position] = parts[s]


def message_block(ref, row):
    return ref[row * HALF : (row + 1) * HALF, :].astype(jnp.float32)


def relay_kernel(rest_ref, y_first, x_first, x_second):
    for ref, tx in ((x_first, 1), (x_second, -1)):
        arrived = relayed(tx)
        for row, s in enumerate(TO_X[tx]):
            value = None
            if s in IMAGE:
                value = rest_ref[(-1, 1).index(tx), IMAGE.index(s)]
            if s in arrived:
                more = message_block(y_first, arrived[s])
                value = more if value is None else value + more
            ref[row * HALF : (row + 1) * HALF, :] = value.astype(jnp.bfloat16)


def gathered(terms):
    total = None
    for ref, row, flag in terms:
        value = message_block(ref, row) if row is not None else ref
        if flag is not None:
            value = value * flag
        total = value if total is None else total + value
    return total


def inside():
    x, y = lax.axis_index("sx"), lax.axis_index("sy")
    return (
        ((x > 0) & (x < lax.axis_size("sx") - 1)).astype(jnp.float32),
        ((y > 0) & (y < lax.axis_size("sy") - 1)).astype(jnp.float32),
    )


def own_kernel(left_star, image, y_first, y_second, c_first, c_second, own_ref):
    centre = jnp.dot(left_star[4 * B : 5 * B, :], image[...], preferred_element_type=jnp.float32)
    has_x, has_y = inside()
    terms = {block: [] for block in STENCIL}
    for s, value in fold(centre).items():
        terms[s].append((value, None, None))
    for s, row in relayed(0).items():
        terms[s].append((y_first, row, None))
    for row, (_, s) in enumerate(TO_Y_SECOND):
        terms[s[0], -1 - s[1]].append((y_second, row, has_y))
    for row, (_, s) in enumerate(TO_C_FIRST):
        terms[1 - s[0], -1 - s[1]].append((c_first, row, has_y))
    for row, (_, s) in enumerate(TO_C_SECOND):
        terms[-1 - s[0], -1 - s[1]].append((c_second, row, has_x * has_y))
    for position, block in enumerate(OWN):
        own_ref[position] = gathered(terms[block])


def finish_kernel(own_ref, x_first, x_second, _, out_hbm, rows, sems):
    odd_x, odd_y = mirrored()
    has_x, _ = inside()
    terms = {block: [] for block in STENCIL}
    for position, block in enumerate(OWN):
        terms[block].append((own_ref[position], None, None))
    for row, s in enumerate(TO_X[1]):
        terms[1 - s[0], s[1]].append((x_first, row, None))
    for row, s in enumerate(TO_X[-1]):
        terms[-1 - s[0], s[1]].append((x_second, row, has_x))
    copies = []
    for jx in (0, 1, -1, 2, -2, 3, -3):
        row_here = jnp.where(odd_x == 1, 3 - jx, 3 + jx)
        reach = 3 - abs(jx)
        for jy in range(-reach, reach + 1):
            value = gathered(terms[jx, jy])
            column_here = jnp.where(odd_y == 1, 3 - jy, 3 + jy)
            rows[jx + 3, column_here, 0:HALF, :] = value[:, :B].astype(jnp.bfloat16)
            rows[jx + 3, column_here, HALF:B, :] = swap_halves(value)[:, :B].astype(jnp.bfloat16)
        span = pl.ds(3 - reach, 2 * reach + 1)
        copy = pltpu.make_async_copy(rows.at[jx + 3, span], out_hbm.at[row_here, span], sems.at[jx + 3])
        copy.start()
        copies.append(copy)
    for copy in copies:
        copy.wait()


def swapped(value, move_x, move_y):
    count_x, count_y = lax.axis_size("sx"), lax.axis_size("sy")

    def partner(index, move, count):
        if move == 0:
            return index
        found = index ^ 1 if move == 1 else ((index + 1) ^ 1) - 1
        return found if 0 <= found < count else None

    pairs = []
    for x in range(count_x):
        for y in range(count_y):
            to_x, to_y = partner(x, move_x, count_x), partner(y, move_y, count_y)
            if to_x is None:
                to_x, to_y = x, y ^ 1
            elif to_y is None:
                to_x, to_y = (x ^ 1 if move_x == 0 else to_x), y
            pairs.append((x * count_y + y, to_x * count_y + to_y))
    return lax.ppermute(value, ("sx", "sy"), pairs)


SMEM = pl.BlockSpec(memory_space=pltpu.SMEM)
VMEM = pl.BlockSpec(memory_space=pltpu.VMEM)
HBM = pl.BlockSpec(memory_space=pltpu.HBM)
ANY = pl.BlockSpec(memory_space=pl.ANY)


def call(kernel, in_specs, outs, scratch=(), out_specs=None, aliases=None, cost=None):
    return pl.pallas_call(
        kernel,
        out_shape=[jax.ShapeDtypeStruct(shape, dtype) for shape, dtype in outs],
        in_specs=in_specs,
        out_specs=out_specs or [VMEM] * len(outs),
        scratch_shapes=list(scratch),
        input_output_aliases=aliases or {},
        compiler_params=pltpu.CompilerParams(vmem_limit_bytes=VMEM_LIMIT),
        cost_estimate=None if cost is None else pl.CostEstimate(flops=cost, bytes_accessed=1, transcendentals=0),
    )


def in_hbm(*values):
    return [pltpu.with_memory_space_constraint(value, pltpu.HBM) for value in values]


def per_device(fine_matrix, prolongator, aggregate, face_links):
    bf16, f32 = jnp.bfloat16, jnp.float32
    message = ((BODY + TAIL, PAIR), bf16)
    longer = ((BODY + 2 * TAIL, PAIR), bf16)
    rows, meta, x_first, x_second, y_first, y_second = call(
        functools.partial(pack_kernel, lax.axis_size("sy")),
        [HBM, HBM, HBM],
        [((4, BLOCK_ROWS, PAIR), bf16), ((32, PAIR), f32), message, message, message, longer],
        [
            pltpu.VMEM((4, 2, 7, B, B), bf16),
            pltpu.SMEM((2, 2, 2), jnp.int32),
            pltpu.SMEM((2, 2, 2, 6), jnp.int32),
            pltpu.SemaphoreType.DMA((4,)),
            pltpu.SemaphoreType.DMA((2,)),
        ],
    )(*in_hbm(aggregate, face_links, prolongator))
    y_second = swapped(y_second, 0, 2)
    x_first, x_second = swapped(x_first, 1, 0), swapped(x_second, 2, 0)
    y_first = swapped(y_first, 0, 1)
    whole = ((7, 7, B, B), bf16)
    matrix, out = call(
        pack_matrix_kernel,
        [HBM, HBM],
        [((4, PAIR, 6 * B), bf16), whole],
        [
            pltpu.VMEM((2, 2, 2, 7, B, B), bf16),
            pltpu.SMEM((2, 2, 2, 6), jnp.int32),
            pltpu.VMEM((3, B, B), bf16),
            pltpu.SemaphoreType.DMA((5,)),
            pltpu.SemaphoreType.DMA((12,)),
        ],
        [VMEM, HBM],
    )(*in_hbm(face_links, fine_matrix))
    note = ((2 * TAIL, PAIR), bf16)
    notes, notes_again = call(notes_kernel, [VMEM, VMEM, ANY], [note, ((48, PAIR), bf16)])(
        x_first, x_second, matrix
    )
    c_first, c_second = swapped(notes, 0, 1), swapped(notes_again, 0, 2)

    def sent(blocks):
        return ((len(blocks) * HALF, PAIR), bf16)

    lefts = [
        ((4, SLOTS * B, 10 * PAIR), bf16),
        ((len(STAR) * B, 4 * PAIR), bf16),
        ((4, B, PAIR), bf16),
    ]
    *lefts_begun, begun = call(begin_kernel, [VMEM] * 5, lefts + [((len(BEGUN), 3, B, PAIR), f32)], cost=1)(
        rows, meta, x_first, x_second, y_first
    )
    y_first, y_second, c_first, c_second, rest, _, left_star, _, image = call(
        main_kernel,
        [VMEM] * 13,
        [
            sent(TO_Y_FIRST),
            sent(TO_Y_SECOND),
            sent(TO_C_FIRST),
            sent(TO_C_SECOND),
            ((2, len(IMAGE), HALF, PAIR), f32),
        ]
        + lefts
        + [((4 * PAIR, IMAGE_PAIRS * PAIR), bf16)],
        aliases={10: 5, 11: 6, 12: 7},
    )(
        matrix,
        rows,
        meta,
        x_first,
        x_second,
        y_first,
        y_second,
        c_first,
        c_second,
        begun,
        *(pltpu.with_memory_space_constraint(left, pltpu.VMEM) for left in lefts_begun),
    )
    y_second = swapped(y_second, 0, 2)
    c_first, c_second = swapped(c_first, 1, 2), swapped(c_second, 2, 2)
    y_first = swapped(y_first, 0, 1)
    x_first, x_second = call(relay_kernel, [VMEM] * 2, [sent(TO_X[1]), sent(TO_X[-1])])(rest, y_first)
    x_first, x_second = swapped(x_first, 1, 0), swapped(x_second, 2, 0)
    (own,) = call(own_kernel, [VMEM] * 6, [((len(OWN), HALF, PAIR), f32)], cost=3_000_000_000)(
        left_star, image, y_first, y_second, c_first, c_second
    )
    (out,) = call(
        finish_kernel,
        [VMEM] * 3 + [HBM],
        [whole],
        [pltpu.VMEM((7, 7, B, B), bf16), pltpu.SemaphoreType.DMA((7,))],
        [HBM],
        {3: 0},
    )(own, x_first, x_second, out)
    return out[None, None]


def solution(mesh):
    return jax.shard_map(
        per_device,
        mesh=mesh,
        in_specs=(
            P("sx", "sy", None, None, None, None),
            P("sx", "sy", None, None, None, None),
            P("sx", "sy", None),
            P("sx", "sy", None, None),
        ),
        out_specs=P("sx", "sy", None, None, None, None),
        check_vma=False,
    )
```

```python
import functools

import jax
import jax.numpy as jnp
from jax import lax
from jax.experimental import pallas as pl
from jax.experimental.pallas import tpu as pltpu
from jax.sharding import PartitionSpec as P


B = 64
HALF = B // 2
PAIR = 2 * B
SLOTS = 6
BLOCK_ROWS = SLOTS * B
BODY = 2 * BLOCK_ROWS
TAIL = 16
VMEM_LIMIT = 20 * 1024 * 1024

FACES = [(0, 0), (-1, 0), (1, 0), (0, -1), (0, 1), (0, 0)]
COLUMNS = [(0, 0), (0, 1), (1, 0), (1, 1)]
SIDES_X = (0, 2, 1, 3, 4, 5)
SIDES_Y = (0, 1, 2, 4, 3, 5)


def targets(px, py):
    table = []
    for dx, dy in FACES:
        ox, nx = divmod(px + dx, 2)
        oy, ny = divmod(py + dy, 2)
        table.append([(ox, oy), (ox + 2 * nx - 1, oy), (ox, oy + 2 * ny - 1)])
    return table


def box_set(px, py):
    return sorted({t for row in targets(px, py) for t in row})


def around(px, py):
    (mx, out_x), (my, out_y) = (2, 1) if px == 0 else (1, 2), (4, 3) if py == 0 else (3, 4)
    found = []
    for m in (0, 5, mx, my, out_x, out_y):
        ox, nx = divmod(px + FACES[m][0], 2)
        oy, ny = divmod(py + FACES[m][1], 2)
        found.append((m, (ox, oy), (nx, ny)))
    return found


def image_set(px, py):
    found = set()
    for _, (ox, oy), column in around(px, py):
        found |= {(ox + tx, oy + ty) for tx, ty in box_set(*column)}
    return sorted(found)


IMAGE = sorted({s for column in COLUMNS for s in image_set(*column)})
IMAGE_PAIRS = (len(IMAGE) + 1) // 2
STAR = [(0, 1), (0, -1), (1, 0), (-1, 0), (0, 0)]


def column_of(tx, ty):
    return ((tx + 1) // 2, (ty + 1) // 2)


def blocks_of(tx, ty):
    return IMAGE if (tx, ty) in STAR else image_set(*column_of(tx, ty))


TO_Y_FIRST = [((tx, 1), s) for tx in (0, -1, 1) for s in blocks_of(tx, 1)]
TO_Y_SECOND = [((0, -1), s) for s in blocks_of(0, -1)]
TO_C_FIRST = [((1, -1), s) for s in blocks_of(1, -1)]
TO_C_SECOND = [((-1, -1), s) for s in blocks_of(-1, -1)]


def relayed(tx):
    return {(s[0], 1 - s[1]): row for row, (t, s) in enumerate(TO_Y_FIRST) if t[0] == tx}


TO_X = {tx: sorted(set(IMAGE) | set(relayed(tx))) for tx in (1, -1)}
STENCIL = [(jx, jy) for jx in range(-3, 4) for jy in range(-3, 4) if abs(jx) + abs(jy) <= 3]
OWN = sorted(
    set(IMAGE)
    | set(relayed(0))
    | {(s[0], -1 - s[1]) for _, s in TO_Y_SECOND}
    | {(1 - s[0], -1 - s[1]) for _, s in TO_C_FIRST}
    | {(-1 - s[0], -1 - s[1]) for _, s in TO_C_SECOND}
)


def low_half(shape):
    return lax.broadcasted_iota(jnp.int32, shape, len(shape) - 1) < B


def swap_halves(value):
    return pltpu.roll(value, B, value.ndim - 1)


def pair_lanes(left, right):
    return jnp.concatenate([left, right], axis=-1)


def mirrored():
    return lax.axis_index("sx") % 2, lax.axis_index("sy") % 2


def slot_here(m, z, odd_x, odd_y):
    if m in (1, 2):
        return jnp.where(odd_x == 1, 3 - m, m)
    if m in (3, 4):
        return jnp.where(odd_y == 1, 7 - m, m)
    return 6 - z if m == 5 else m


def fill_rows(rows, values):
    shape = (rows, PAIR)
    row = lax.broadcasted_iota(jnp.int32, shape, 0)
    half = low_half(shape)
    filled = jnp.zeros(shape, jnp.float32)
    for index, (low, high) in enumerate(values):
        filled = jnp.where(row == index, jnp.where(half, low, high), filled)
    return filled


def pack_kernel(
    boxes_y,
    aggregate_hbm,
    links_hbm,
    p_hbm,
    rows_ref,
    meta_ref,
    x_first,
    x_second,
    y_first,
    y_second,
    p_ref,
    aggregate_ref,
    links_ref,
    p_sems,
    sems,
):
    odd_x, odd_y = mirrored()
    own = lax.axis_index("sx") * boxes_y + lax.axis_index("sy")
    place = {(px, py): (px ^ odd_x, py ^ odd_y) for px, py in COLUMNS}
    copies = [
        pltpu.make_async_copy(p_hbm.at[place[column]], p_ref.at[index], p_sems.at[index])
        for index, column in enumerate(COLUMNS)
    ]
    small = [
        pltpu.make_async_copy(aggregate_hbm, aggregate_ref, sems.at[0]),
        pltpu.make_async_copy(links_hbm, links_ref, sems.at[1]),
    ]
    for copy in small + copies:
        copy.start()
    for copy in small:
        copy.wait()

    def state(column, z):
        shift = aggregate_ref[place[column] + (z,)] - own
        across_x = (shift == boxes_y) | (shift == -boxes_y)
        return jnp.where(shift == 0, 0, jnp.where(across_x, 1, 2)).astype(jnp.float32)

    def link(column, m):
        faces = [slot_here(m, z, odd_x, odd_y) - 1 for z in (0, 1)]
        return tuple(links_ref[place[column] + (z, faces[z])].astype(jnp.float32) for z in (0, 1))

    states = [tuple(state(column, z) for z in (0, 1)) for column in COLUMNS]
    links = {column: [link(column, m) for m in range(1, SLOTS)] for column in COLUMNS}
    meta_ref[...] = fill_rows(32, states + sum((links[column] for column in COLUMNS), []))
    messages = (
        (x_first, ((1, 0), (1, 1))),
        (x_second, ((0, 0), (0, 1))),
        (y_first, ((0, 1), (1, 1))),
        (y_second, ((0, 0), (1, 0))),
    )
    for ref, columns in messages:
        tail = fill_rows(TAIL, states + links[columns[0]] + links[columns[1]])
        ref[BODY : BODY + TAIL, :] = tail.astype(jnp.bfloat16)
    for index, column in enumerate(COLUMNS):
        copies[index].wait()
        for m in range(SLOTS):
            packed = pair_lanes(*(p_ref[index, z, slot_here(m, z, odd_x, odd_y)] for z in (0, 1)))
            rows_ref[index, m * B : (m + 1) * B, :] = packed
            for ref, columns in messages:
                if column in columns:
                    start = columns.index(column) * BLOCK_ROWS + m * B
                    ref[start : start + B, :] = packed


def notes_kernel(x_first, x_second, _, notes_ref, again_ref):
    for ref in (notes_ref, again_ref):
        ref[0:TAIL, :] = x_first[BODY : BODY + TAIL, :]
        ref[TAIL : 2 * TAIL, :] = x_second[BODY : BODY + TAIL, :]


def pack_matrix_kernel(links_hbm, a_hbm, out_ref, whole_hbm, a_ref, links_ref, zeros, a_sems, sems):
    fetches = [
        pltpu.make_async_copy(links_hbm, links_ref, a_sems.at[4]),
        *(
            pltpu.make_async_copy(a_hbm.at[px, py], a_ref.at[px, py], a_sems.at[index])
            for index, (px, py) in enumerate(COLUMNS)
        ),
    ]
    for fetch in fetches:
        fetch.start()
    zeros[...] = jnp.zeros(zeros.shape, zeros.dtype)
    copies = []
    for jx in range(-3, 4):
        width = abs(jx)
        if width:
            for start in (0, 7 - width):
                copies.append(
                    pltpu.make_async_copy(
                        zeros.at[pl.ds(0, width)], whole_hbm.at[jx + 3, pl.ds(start, width)], sems.at[len(copies)]
                    )
                )
    for copy in copies:
        copy.start()
    for fetch in fetches:
        fetch.wait()
    odd_x, odd_y = mirrored()
    for index, (px, py) in enumerate(COLUMNS):
        place = (px ^ odd_x, py ^ odd_y)
        for z in (0, 1):
            blocks = []
            for m, _, _ in around(px, py):
                slot = slot_here(m, z, odd_x, odd_y)
                block = a_ref[place + (z, slot)]
                if m > 0:
                    present = links_ref[place + (z, slot - 1)] == 1
                    block = jnp.where(present, block, jnp.zeros_like(block))
                blocks.append(block)
            for pair in range(3):
                out_ref[index, z * B : (z + 1) * B, pair * PAIR : (pair + 1) * PAIR] = pair_lanes(
                    blocks[2 * pair], blocks[2 * pair + 1]
                )
    for copy in copies:
        copy.wait()


def there(ox, oy, px, py):
    return (1 - px if ox else px, 1 - py if oy else py)


def slot_there(ox, oy, m):
    m = SIDES_X[m] if ox else m
    return SIDES_Y[m] if oy else m


class Rows:
    def __init__(self, rows_ref, meta_ref, from_x, from_y, corners):
        self.rows_ref, self.from_x, self.from_y = rows_ref, from_x, from_y
        self.notes = {(0, 0): meta_ref[...]}
        for side, ref in from_x.items():
            self.notes[side, 0] = ref[BODY : BODY + TAIL, :].astype(jnp.float32)
        for side, ref in from_y.items():
            self.notes[0, side] = ref[BODY : BODY + TAIL, :].astype(jnp.float32)
        for oy, ref in corners.items():
            self.notes[1, oy] = ref[0:TAIL, :].astype(jnp.float32)
            self.notes[-1, oy] = ref[TAIL : 2 * TAIL, :].astype(jnp.float32)

    def state_row(self, ox, oy, px, py):
        index = COLUMNS.index(there(ox, oy, px, py))
        return self.notes[ox, oy][index : index + 1]

    def link_row(self, ox, oy, px, py, m):
        if (ox, oy) == (0, 0):
            index = (SLOTS - 1) * COLUMNS.index((px, py))
        else:
            index = (SLOTS - 1) * (py if ox else px)
        index += 4 + slot_there(ox, oy, m) - 1
        return self.notes[ox, oy][index : index + 1]

    def block(self, ox, oy, px, py, m, chunk):
        start = slot_there(ox, oy, m) * B + chunk * 16
        if (ox, oy) == (0, 0):
            return self.rows_ref[COLUMNS.index((px, py)), start : start + 16, :]
        start += (py if ox else px) * BLOCK_ROWS
        ref = self.from_x[ox] if ox else self.from_y[oy]
        return ref[start : start + 16, :]

    def sums(self, box, column, slots, begun=None):
        (ox, oy), (px, py) = box, column
        weights = {}
        for m in slots:
            dx, dy = FACES[m]
            bx, nx = divmod(2 * ox + px + dx, 2)
            by, ny = divmod(2 * oy + py + dy, 2)
            state = self.state_row(bx, by, nx, ny)
            if m == 5:
                state = swap_halves(state)
            for kind in range(3):
                weight = jnp.where(state == kind, 1.0, 0.0)
                if m > 0:
                    weight = weight * self.link_row(ox, oy, px, py, m)
                weights[m, kind] = jnp.broadcast_to(weight, (16, PAIR))
        reach = targets(px, py)
        chunks = {}
        for chunk in range(4):
            values = {m: self.block(ox, oy, px, py, m, chunk).astype(jnp.float32) for m in slots}
            for t in box_set(px, py):
                total = begun[t][chunk * 16 : chunk * 16 + 16] if begun and t in begun else None
                for m in slots:
                    for kind in range(3):
                        if reach[m][kind] == t:
                            term = values[m] * weights[m, kind]
                            total = term if total is None else total + term
                if total is not None:
                    chunks.setdefault(t, []).append(total)
        return {t: jnp.concatenate(parts, axis=0) for t, parts in chunks.items()}


def couplings_of(column, s):
    return [
        place
        for place, (_, (ox, oy), other) in enumerate(around(*column))
        if (s[0] - ox, s[1] - oy) in box_set(*other)
    ]


def grouped_images(column):
    groups = [[], [], []]
    for s in image_set(*column):
        places = couplings_of(column, s)
        groups[1 if max(places) < 4 else 2 if min(places) > 1 else 0].append(s)
    return groups


GROUPS = {column: grouped_images(column) for column in COLUMNS}
SPANS = (slice(0, 6 * B), slice(0, 4 * B), slice(2 * B, 6 * B))
IMAGES = {column: sum(GROUPS[column], []) for column in COLUMNS}
USERS = {}
for _index, _column in enumerate(COLUMNS):
    for _place, (_, _box, _other) in enumerate(around(*_column)):
        USERS.setdefault((_box, _other), []).append((_index, _column, _place))
BEGUN = {
    (box, (px, py)): (1 if px == 0 else 2) if box == (0, 1) else (3 if py == 0 else 4)
    for box, (px, py) in USERS
    if box[1] == 1 or box[0] or (box == (0, 0) and py == 0)
}
LATE = [key for key in USERS if key[0][1] == -1]


def begun_targets(key):
    return targets(*key[1])[BEGUN[key]]


def place_rows(found, box, other, right, left_star, left_corner):
    unit = None
    if box == (0, 0):
        square = (PAIR, PAIR)
        diagonal = lax.broadcasted_iota(jnp.int32, square, 0) == lax.broadcasted_iota(jnp.int32, square, 1)
        unit = jnp.where(diagonal, 1.0, 0.0).astype(jnp.bfloat16)
    own = COLUMNS.index(other)
    for t, value in found.items():
        rounded = value.astype(jnp.bfloat16)
        for index, column, place in USERS[box, other]:
            position = IMAGES[column].index((box[0] + t[0], box[1] + t[1]))
            stored = swap_halves(value).astype(jnp.bfloat16) if place == 1 else rounded
            right[index, place * B : (place + 1) * B, position * PAIR : (position + 1) * PAIR] = stored
        if box == (0, 0):
            turned = lax.dot_general(
                unit, rounded, (((1,), (1,)), ((), ())), preferred_element_type=jnp.float32
            ).astype(jnp.bfloat16)
            turned = pair_lanes(turned[:B], turned[B:])
            if t in STAR:
                left_star[STAR.index(t) * B : (STAR.index(t) + 1) * B, own * PAIR : (own + 1) * PAIR] = turned
            else:
                left_corner[own] = turned


def fold(product):
    folded_half = low_half((HALF, PAIR))
    blocks = {}
    for pair in range(IMAGE_PAIRS):
        tile = product[:, pair * PAIR : (pair + 1) * PAIR]
        top, bottom = tile[:HALF], tile[HALF:]
        blocks[IMAGE[2 * pair]] = jnp.where(folded_half, top, swap_halves(bottom))
        if 2 * pair + 1 < len(IMAGE):
            blocks[IMAGE[2 * pair + 1]] = jnp.where(folded_half, swap_halves(top), bottom)
    return blocks


def begin_kernel(rows_ref, meta_ref, x_first, x_second, y_first, right, left_star, left_corner, begun_ref):
    rows = Rows(rows_ref, meta_ref, {1: x_first, -1: x_second}, {1: y_first}, {})
    for index, column in enumerate(COLUMNS):
        for place, (_, box, other) in enumerate(around(*column)):
            reached = {(box[0] + tx, box[1] + ty) for tx, ty in box_set(*other)}
            spans = sum(([span] * len(group) for span, group in zip(SPANS, GROUPS[column])), [])
            for position, s in enumerate(IMAGES[column]):
                if s not in reached and spans[position].start <= place * B < spans[position].stop:
                    right[index, place * B : (place + 1) * B, position * PAIR : (position + 1) * PAIR] = jnp.zeros(
                        (B, PAIR), jnp.bfloat16
                    )
    for box, other in USERS:
        if (box, other) in LATE:
            continue
        slots = list(range(SLOTS))
        open_targets = []
        if (box, other) in BEGUN:
            slots.remove(BEGUN[box, other])
            open_targets = begun_targets((box, other))
        found = rows.sums(box, other, slots)
        for place, t in enumerate(open_targets):
            begun_ref[list(BEGUN).index((box, other)), place] = found.pop(t)
        place_rows(found, box, other, right, left_star, left_corner)


def main_kernel(
    a_ref,
    rows_ref,
    meta_ref,
    x_first,
    x_second,
    y_first,
    y_second,
    c_first,
    c_second,
    begun_ref,
    right_in,
    left_star_in,
    left_corner_in,
    to_y_first,
    to_y_second,
    to_c_first,
    to_c_second,
    right,
    left_star,
    left_corner,
    image,
):
    rows = Rows(rows_ref, meta_ref, {1: x_first, -1: x_second}, {1: y_first, -1: y_second}, {1: c_first, -1: c_second})
    for number, ((box, other), slot) in enumerate(BEGUN.items()):
        begun = {t: begun_ref[number, place] for place, t in enumerate(begun_targets((box, other)))}
        place_rows(rows.sums(box, other, [slot], begun), box, other, right, left_star, left_corner)
    for box, other in LATE:
        place_rows(rows.sums(box, other, list(range(SLOTS))), box, other, right, left_star, left_corner)
    half = low_half((B, PAIR))
    for index, column in enumerate(COLUMNS):
        products, start = {}, 0
        for span, group in zip(SPANS, GROUPS[column]):
            lanes = slice(start * PAIR, (start + len(group)) * PAIR)
            product = jnp.dot(a_ref[index, :, span], right[index, span, lanes], preferred_element_type=jnp.float32)
            for place, s in enumerate(group):
                products[s] = product[:, place * PAIR : (place + 1) * PAIR]
            start += len(group)

        def part(s, z):
            if s not in products:
                return jnp.zeros((B, PAIR), jnp.float32)
            return products[s][z * B : (z + 1) * B]

        for pair in range(IMAGE_PAIRS):
            one = IMAGE[2 * pair]
            two = IMAGE[2 * pair + 1] if 2 * pair + 1 < len(IMAGE) else None
            low = jnp.where(half, part(one, 0), swap_halves(part(two, 0)))
            high = jnp.where(half, swap_halves(part(one, 1)), part(two, 1))
            start = index * PAIR
            lanes = slice(pair * PAIR, (pair + 1) * PAIR)
            image[start : start + B, lanes] = low.astype(jnp.bfloat16)
            image[start + B : start + PAIR, lanes] = high.astype(jnp.bfloat16)
    star = jnp.dot(left_star[0 : 2 * B, :], image[...], preferred_element_type=jnp.float32)

    def contribution(t):
        if t in STAR:
            return fold(star[STAR.index(t) * B : (STAR.index(t) + 1) * B])
        index = COLUMNS.index(column_of(*t))
        return fold(
            jnp.dot(
                left_corner[index], image[index * PAIR : (index + 1) * PAIR, :], preferred_element_type=jnp.float32
            )
        )

    for ref, sent in (
        (to_y_first, TO_Y_FIRST),
        (to_y_second, TO_Y_SECOND),
        (to_c_first, TO_C_FIRST),
        (to_c_second, TO_C_SECOND),
    ):
        parts = {t: contribution(t) for t in sorted({t for t, _ in sent})}
        for row, (t, s) in enumerate(sent):
            ref[row * HALF : (row + 1) * HALF, :] = parts[t][s].astype(jnp.bfloat16)


def message_block(ref, row):
    return ref[row * HALF : (row + 1) * HALF, :].astype(jnp.float32)


def relay_kernel(left_star, image, y_first, x_first, x_second):
    beside = jnp.dot(left_star[2 * B : 4 * B, :], image[...], preferred_element_type=jnp.float32)
    parts = {1: fold(beside[:B]), -1: fold(beside[B:])}
    for ref, tx in ((x_first, 1), (x_second, -1)):
        arrived = relayed(tx)
        for row, s in enumerate(TO_X[tx]):
            value = None
            if s in IMAGE:
                value = parts[tx][s]
            if s in arrived:
                more = message_block(y_first, arrived[s])
                value = more if value is None else value + more
            ref[row * HALF : (row + 1) * HALF, :] = value.astype(jnp.bfloat16)


def gathered(terms):
    total = None
    for ref, row, flag in terms:
        value = message_block(ref, row) if row is not None else ref
        if flag is not None:
            value = value * flag
        total = value if total is None else total + value
    return total


def inside():
    x, y = lax.axis_index("sx"), lax.axis_index("sy")
    return (
        ((x > 0) & (x < lax.axis_size("sx") - 1)).astype(jnp.float32),
        ((y > 0) & (y < lax.axis_size("sy") - 1)).astype(jnp.float32),
    )


def own_kernel(left_star, image, y_first, y_second, c_first, c_second, own_ref):
    centre = jnp.dot(left_star[4 * B : 5 * B, :], image[...], preferred_element_type=jnp.float32)
    has_x, has_y = inside()
    terms = {block: [] for block in STENCIL}
    for s, value in fold(centre).items():
        terms[s].append((value, None, None))
    for s, row in relayed(0).items():
        terms[s].append((y_first, row, None))
    for row, (_, s) in enumerate(TO_Y_SECOND):
        terms[s[0], -1 - s[1]].append((y_second, row, has_y))
    for row, (_, s) in enumerate(TO_C_FIRST):
        terms[1 - s[0], -1 - s[1]].append((c_first, row, has_y))
    for row, (_, s) in enumerate(TO_C_SECOND):
        terms[-1 - s[0], -1 - s[1]].append((c_second, row, has_x * has_y))
    for position, block in enumerate(OWN):
        own_ref[position] = gathered(terms[block])


def finish_kernel(own_ref, x_first, x_second, _, out_hbm, rows, sems):
    odd_x, odd_y = mirrored()
    has_x, _ = inside()
    terms = {block: [] for block in STENCIL}
    for position, block in enumerate(OWN):
        terms[block].append((own_ref[position], None, None))
    for row, s in enumerate(TO_X[1]):
        terms[1 - s[0], s[1]].append((x_first, row, None))
    for row, s in enumerate(TO_X[-1]):
        terms[-1 - s[0], s[1]].append((x_second, row, has_x))
    copies = []
    for jx in (0, 1, -1, 2, -2, 3, -3):
        row_here = jnp.where(odd_x == 1, 3 - jx, 3 + jx)
        reach = 3 - abs(jx)
        for jy in range(-reach, reach + 1):
            value = gathered(terms[jx, jy])
            column_here = jnp.where(odd_y == 1, 3 - jy, 3 + jy)
            rows[jx + 3, column_here, 0:HALF, :] = value[:, :B].astype(jnp.bfloat16)
            rows[jx + 3, column_here, HALF:B, :] = swap_halves(value)[:, :B].astype(jnp.bfloat16)
        span = pl.ds(3 - reach, 2 * reach + 1)
        copy = pltpu.make_async_copy(rows.at[jx + 3, span], out_hbm.at[row_here, span], sems.at[jx + 3])
        copy.start()
        copies.append(copy)
    for copy in copies:
        copy.wait()


def swapped(value, move_x, move_y):
    count_x, count_y = lax.axis_size("sx"), lax.axis_size("sy")

    def partner(index, move, count):
        if move == 0:
            return index
        found = index ^ 1 if move == 1 else ((index + 1) ^ 1) - 1
        return found if 0 <= found < count else None

    pairs = []
    for x in range(count_x):
        for y in range(count_y):
            to_x, to_y = partner(x, move_x, count_x), partner(y, move_y, count_y)
            if to_x is None:
                to_x, to_y = x, y ^ 1
            elif to_y is None:
                to_x, to_y = (x ^ 1 if move_x == 0 else to_x), y
            pairs.append((x * count_y + y, to_x * count_y + to_y))
    return lax.ppermute(value, ("sx", "sy"), pairs)


SMEM = pl.BlockSpec(memory_space=pltpu.SMEM)
VMEM = pl.BlockSpec(memory_space=pltpu.VMEM)
HBM = pl.BlockSpec(memory_space=pltpu.HBM)
ANY = pl.BlockSpec(memory_space=pl.ANY)


def call(kernel, in_specs, outs, scratch=(), out_specs=None, aliases=None, cost=None):
    return pl.pallas_call(
        kernel,
        out_shape=[jax.ShapeDtypeStruct(shape, dtype) for shape, dtype in outs],
        in_specs=in_specs,
        out_specs=out_specs or [VMEM] * len(outs),
        scratch_shapes=list(scratch),
        input_output_aliases=aliases or {},
        compiler_params=pltpu.CompilerParams(vmem_limit_bytes=VMEM_LIMIT),
        cost_estimate=None if cost is None else pl.CostEstimate(flops=cost, bytes_accessed=1, transcendentals=0),
    )


def in_hbm(*values):
    return [pltpu.with_memory_space_constraint(value, pltpu.HBM) for value in values]


def per_device(fine_matrix, prolongator, aggregate, face_links):
    bf16, f32 = jnp.bfloat16, jnp.float32
    message = ((BODY + TAIL, PAIR), bf16)
    longer = ((BODY + 2 * TAIL, PAIR), bf16)
    rows, meta, x_first, x_second, y_first, y_second = call(
        functools.partial(pack_kernel, lax.axis_size("sy")),
        [HBM, HBM, HBM],
        [((4, BLOCK_ROWS, PAIR), bf16), ((32, PAIR), f32), message, message, message, longer],
        [
            pltpu.VMEM((4, 2, 7, B, B), bf16),
            pltpu.SMEM((2, 2, 2), jnp.int32),
            pltpu.SMEM((2, 2, 2, 6), jnp.int32),
            pltpu.SemaphoreType.DMA((4,)),
            pltpu.SemaphoreType.DMA((2,)),
        ],
    )(*in_hbm(aggregate, face_links, prolongator))
    y_second = swapped(y_second, 0, 2)
    x_first, x_second = swapped(x_first, 1, 0), swapped(x_second, 2, 0)
    y_first = swapped(y_first, 0, 1)
    whole = ((7, 7, B, B), bf16)
    matrix, out = call(
        pack_matrix_kernel,
        [HBM, HBM],
        [((4, PAIR, 6 * B), bf16), whole],
        [
            pltpu.VMEM((2, 2, 2, 7, B, B), bf16),
            pltpu.SMEM((2, 2, 2, 6), jnp.int32),
            pltpu.VMEM((3, B, B), bf16),
            pltpu.SemaphoreType.DMA((5,)),
            pltpu.SemaphoreType.DMA((12,)),
        ],
        [VMEM, HBM],
    )(*in_hbm(face_links, fine_matrix))
    note = ((2 * TAIL, PAIR), bf16)
    notes, notes_again = call(notes_kernel, [VMEM, VMEM, ANY], [note, ((48, PAIR), bf16)])(
        x_first, x_second, matrix
    )
    c_first, c_second = swapped(notes, 0, 1), swapped(notes_again, 0, 2)

    def sent(blocks):
        return ((len(blocks) * HALF, PAIR), bf16)

    lefts = [
        ((4, SLOTS * B, 10 * PAIR), bf16),
        ((len(STAR) * B, 4 * PAIR), bf16),
        ((4, B, PAIR), bf16),
    ]
    *lefts_begun, begun = call(begin_kernel, [VMEM] * 5, lefts + [((len(BEGUN), 3, B, PAIR), f32)], cost=1)(
        rows, meta, x_first, x_second, y_first
    )
    y_first, y_second, c_first, c_second, _, left_star, _, image = call(
        main_kernel,
        [VMEM] * 13,
        [
            sent(TO_Y_FIRST),
            sent(TO_Y_SECOND),
            sent(TO_C_FIRST),
            sent(TO_C_SECOND),
        ]
        + lefts
        + [((4 * PAIR, IMAGE_PAIRS * PAIR), bf16)],
        aliases={10: 4, 11: 5, 12: 6},
    )(
        matrix,
        rows,
        meta,
        x_first,
        x_second,
        y_first,
        y_second,
        c_first,
        c_second,
        begun,
        *(pltpu.with_memory_space_constraint(left, pltpu.VMEM) for left in lefts_begun),
    )
    y_second = swapped(y_second, 0, 2)
    c_first, c_second = swapped(c_first, 1, 2), swapped(c_second, 2, 2)
    y_first = swapped(y_first, 0, 1)
    x_first, x_second = call(relay_kernel, [VMEM] * 3, [sent(TO_X[1]), sent(TO_X[-1])])(left_star, image, y_first)
    x_first, x_second = swapped(x_first, 1, 0), swapped(x_second, 2, 0)
    (own,) = call(own_kernel, [VMEM] * 6, [((len(OWN), HALF, PAIR), f32)], cost=3_000_000_000)(
        left_star, image, y_first, y_second, c_first, c_second
    )
    (out,) = call(
        finish_kernel,
        [VMEM] * 3 + [HBM],
        [whole],
        [pltpu.VMEM((7, 7, B, B), bf16), pltpu.SemaphoreType.DMA((7,))],
        [HBM],
        {3: 0},
    )(own, x_first, x_second, out)
    return out[None, None]


def solution(mesh):
    return jax.shard_map(
        per_device,
        mesh=mesh,
        in_specs=(
            P("sx", "sy", None, None, None, None),
            P("sx", "sy", None, None, None, None),
            P("sx", "sy", None),
            P("sx", "sy", None, None),
        ),
        out_specs=P("sx", "sy", None, None, None, None),
        check_vma=False,
    )
```

```python
import functools

import jax
import jax.numpy as jnp
from jax import lax
from jax.experimental import pallas as pl
from jax.experimental.pallas import tpu as pltpu
from jax.sharding import PartitionSpec as P


B = 64
HALF = B // 2
PAIR = 2 * B
SLOTS = 6
BLOCK_ROWS = SLOTS * B
BODY = 2 * BLOCK_ROWS
TAIL = 16
VMEM_LIMIT = 20 * 1024 * 1024

FACES = [(0, 0), (-1, 0), (1, 0), (0, -1), (0, 1), (0, 0)]
COLUMNS = [(0, 0), (0, 1), (1, 0), (1, 1)]
SIDES_X = (0, 2, 1, 3, 4, 5)
SIDES_Y = (0, 1, 2, 4, 3, 5)


def targets(px, py):
    table = []
    for dx, dy in FACES:
        ox, nx = divmod(px + dx, 2)
        oy, ny = divmod(py + dy, 2)
        table.append([(ox, oy), (ox + 2 * nx - 1, oy), (ox, oy + 2 * ny - 1)])
    return table


def box_set(px, py):
    return sorted({t for row in targets(px, py) for t in row})


def around(px, py):
    (mx, out_x), (my, out_y) = (2, 1) if px == 0 else (1, 2), (4, 3) if py == 0 else (3, 4)
    found = []
    for m in (0, 5, mx, my, out_x, out_y):
        ox, nx = divmod(px + FACES[m][0], 2)
        oy, ny = divmod(py + FACES[m][1], 2)
        found.append((m, (ox, oy), (nx, ny)))
    return found


def image_set(px, py):
    found = set()
    for _, (ox, oy), column in around(px, py):
        found |= {(ox + tx, oy + ty) for tx, ty in box_set(*column)}
    return sorted(found)


IMAGE = sorted({s for column in COLUMNS for s in image_set(*column)})
IMAGE_PAIRS = (len(IMAGE) + 1) // 2
STAR = [(0, 1), (0, -1), (1, 0), (-1, 0), (0, 0)]


def column_of(tx, ty):
    return ((tx + 1) // 2, (ty + 1) // 2)


def blocks_of(tx, ty):
    return IMAGE if (tx, ty) in STAR else image_set(*column_of(tx, ty))


TO_Y_FIRST = [((tx, 1), s) for tx in (0, -1, 1) for s in blocks_of(tx, 1)]
TO_Y_SECOND = [((0, -1), s) for s in blocks_of(0, -1)]
TO_C_FIRST = [((1, -1), s) for s in blocks_of(1, -1)]
TO_C_SECOND = [((-1, -1), s) for s in blocks_of(-1, -1)]


def relayed(tx):
    return {(s[0], 1 - s[1]): row for row, (t, s) in enumerate(TO_Y_FIRST) if t[0] == tx}


TO_X = {tx: sorted(set(IMAGE) | set(relayed(tx))) for tx in (1, -1)}
STENCIL = [(jx, jy) for jx in range(-3, 4) for jy in range(-3, 4) if abs(jx) + abs(jy) <= 3]
OWN = sorted(
    set(IMAGE)
    | set(relayed(0))
    | {(s[0], -1 - s[1]) for _, s in TO_Y_SECOND}
    | {(1 - s[0], -1 - s[1]) for _, s in TO_C_FIRST}
    | {(-1 - s[0], -1 - s[1]) for _, s in TO_C_SECOND}
)


def low_half(shape):
    return lax.broadcasted_iota(jnp.int32, shape, len(shape) - 1) < B


def swap_halves(value):
    return pltpu.roll(value, B, value.ndim - 1)


def pair_lanes(left, right):
    return jnp.concatenate([left, right], axis=-1)


def mirrored():
    return lax.axis_index("sx") % 2, lax.axis_index("sy") % 2


def slot_here(m, z, odd_x, odd_y):
    if m in (1, 2):
        return jnp.where(odd_x == 1, 3 - m, m)
    if m in (3, 4):
        return jnp.where(odd_y == 1, 7 - m, m)
    return 6 - z if m == 5 else m


def fill_rows(rows, values):
    shape = (rows, PAIR)
    row = lax.broadcasted_iota(jnp.int32, shape, 0)
    half = low_half(shape)
    filled = jnp.zeros(shape, jnp.float32)
    for index, (low, high) in enumerate(values):
        filled = jnp.where(row == index, jnp.where(half, low, high), filled)
    return filled


def pack_kernel(
    boxes_y,
    aggregate_hbm,
    links_hbm,
    p_hbm,
    rows_ref,
    meta_ref,
    x_first,
    x_second,
    p_ref,
    aggregate_ref,
    links_ref,
    p_sems,
    sems,
):
    odd_x, odd_y = mirrored()
    own = lax.axis_index("sx") * boxes_y + lax.axis_index("sy")
    place = {(px, py): (px ^ odd_x, py ^ odd_y) for px, py in COLUMNS}
    copies = [
        pltpu.make_async_copy(p_hbm.at[place[column]], p_ref.at[index], p_sems.at[index])
        for index, column in enumerate(COLUMNS)
    ]
    small = [
        pltpu.make_async_copy(aggregate_hbm, aggregate_ref, sems.at[0]),
        pltpu.make_async_copy(links_hbm, links_ref, sems.at[1]),
    ]
    for copy in small + copies:
        copy.start()
    for copy in small:
        copy.wait()

    def state(column, z):
        shift = aggregate_ref[place[column] + (z,)] - own
        across_x = (shift == boxes_y) | (shift == -boxes_y)
        return jnp.where(shift == 0, 0, jnp.where(across_x, 1, 2)).astype(jnp.float32)

    def link(column, m):
        faces = [slot_here(m, z, odd_x, odd_y) - 1 for z in (0, 1)]
        return tuple(links_ref[place[column] + (z, faces[z])].astype(jnp.float32) for z in (0, 1))

    states = [tuple(state(column, z) for z in (0, 1)) for column in COLUMNS]
    links = {column: [link(column, m) for m in range(1, SLOTS)] for column in COLUMNS}
    meta_ref[...] = fill_rows(32, states + sum((links[column] for column in COLUMNS), []))
    messages = (
        (x_first, ((1, 0), (1, 1))),
        (x_second, ((0, 0), (0, 1))),
    )
    for ref, columns in messages:
        tail = fill_rows(TAIL, states + links[columns[0]] + links[columns[1]])
        ref[BODY : BODY + TAIL, :] = tail.astype(jnp.bfloat16)
    for index, column in enumerate(COLUMNS):
        copies[index].wait()
        for m in range(SLOTS):
            packed = pair_lanes(*(p_ref[index, z, slot_here(m, z, odd_x, odd_y)] for z in (0, 1)))
            rows_ref[index, m * B : (m + 1) * B, :] = packed
            for ref, columns in messages:
                if column in columns:
                    start = columns.index(column) * BLOCK_ROWS + m * B
                    ref[start : start + B, :] = packed


def pack_y_kernel(rows_ref, meta_ref, y_first, y_second):
    meta = meta_ref[...]
    for ref, columns in ((y_first, (1, 3)), (y_second, (0, 2))):
        parts = [meta[0:4]]
        for place, index in enumerate(columns):
            ref[place * BLOCK_ROWS : (place + 1) * BLOCK_ROWS, :] = rows_ref[index]
            parts.append(meta[4 + (SLOTS - 1) * index : 4 + (SLOTS - 1) * (index + 1)])
        parts.append(jnp.zeros((2, PAIR), jnp.float32))
        ref[BODY : BODY + TAIL, :] = jnp.concatenate(parts, axis=0).astype(jnp.bfloat16)


def notes_kernel(x_first, x_second, _, notes_ref, again_ref):
    for ref in (notes_ref, again_ref):
        ref[0:TAIL, :] = x_first[BODY : BODY + TAIL, :]
        ref[TAIL : 2 * TAIL, :] = x_second[BODY : BODY + TAIL, :]


def pack_matrix_kernel(links_hbm, a_hbm, out_ref, whole_hbm, a_ref, links_ref, zeros, a_sems, sems):
    fetches = [
        pltpu.make_async_copy(links_hbm, links_ref, a_sems.at[4]),
        *(
            pltpu.make_async_copy(a_hbm.at[px, py], a_ref.at[px, py], a_sems.at[index])
            for index, (px, py) in enumerate(COLUMNS)
        ),
    ]
    for fetch in fetches:
        fetch.start()
    zeros[...] = jnp.zeros(zeros.shape, zeros.dtype)
    copies = []
    for jx in range(-3, 4):
        width = abs(jx)
        if width:
            for start in (0, 7 - width):
                copies.append(
                    pltpu.make_async_copy(
                        zeros.at[pl.ds(0, width)], whole_hbm.at[jx + 3, pl.ds(start, width)], sems.at[len(copies)]
                    )
                )
    for copy in copies:
        copy.start()
    for fetch in fetches:
        fetch.wait()
    odd_x, odd_y = mirrored()
    for index, (px, py) in enumerate(COLUMNS):
        place = (px ^ odd_x, py ^ odd_y)
        for z in (0, 1):
            blocks = []
            for m, _, _ in around(px, py):
                slot = slot_here(m, z, odd_x, odd_y)
                block = a_ref[place + (z, slot)]
                if m > 0:
                    present = links_ref[place + (z, slot - 1)] == 1
                    block = jnp.where(present, block, jnp.zeros_like(block))
                blocks.append(block)
            for pair in range(3):
                out_ref[index, z * B : (z + 1) * B, pair * PAIR : (pair + 1) * PAIR] = pair_lanes(
                    blocks[2 * pair], blocks[2 * pair + 1]
                )
    for copy in copies:
        copy.wait()


def there(ox, oy, px, py):
    return (1 - px if ox else px, 1 - py if oy else py)


def slot_there(ox, oy, m):
    m = SIDES_X[m] if ox else m
    return SIDES_Y[m] if oy else m


class Rows:
    def __init__(self, rows_ref, meta_ref, from_x, from_y, corners):
        self.rows_ref, self.from_x, self.from_y = rows_ref, from_x, from_y
        self.notes = {(0, 0): meta_ref[...]}
        for side, ref in from_x.items():
            self.notes[side, 0] = ref[BODY : BODY + TAIL, :].astype(jnp.float32)
        for side, ref in from_y.items():
            self.notes[0, side] = ref[BODY : BODY + TAIL, :].astype(jnp.float32)
        for oy, ref in corners.items():
            self.notes[1, oy] = ref[0:TAIL, :].astype(jnp.float32)
            self.notes[-1, oy] = ref[TAIL : 2 * TAIL, :].astype(jnp.float32)

    def state_row(self, ox, oy, px, py):
        index = COLUMNS.index(there(ox, oy, px, py))
        return self.notes[ox, oy][index : index + 1]

    def link_row(self, ox, oy, px, py, m):
        if (ox, oy) == (0, 0):
            index = (SLOTS - 1) * COLUMNS.index((px, py))
        else:
            index = (SLOTS - 1) * (py if ox else px)
        index += 4 + slot_there(ox, oy, m) - 1
        return self.notes[ox, oy][index : index + 1]

    def block(self, ox, oy, px, py, m, chunk):
        start = slot_there(ox, oy, m) * B + chunk * 16
        if (ox, oy) == (0, 0):
            return self.rows_ref[COLUMNS.index((px, py)), start : start + 16, :]
        start += (py if ox else px) * BLOCK_ROWS
        ref = self.from_x[ox] if ox else self.from_y[oy]
        return ref[start : start + 16, :]

    def sums(self, box, column, slots, begun=None):
        (ox, oy), (px, py) = box, column
        weights = {}
        for m in slots:
            dx, dy = FACES[m]
            bx, nx = divmod(2 * ox + px + dx, 2)
            by, ny = divmod(2 * oy + py + dy, 2)
            state = self.state_row(bx, by, nx, ny)
            if m == 5:
                state = swap_halves(state)
            for kind in range(3):
                weight = jnp.where(state == kind, 1.0, 0.0)
                if m > 0:
                    weight = weight * self.link_row(ox, oy, px, py, m)
                weights[m, kind] = jnp.broadcast_to(weight, (16, PAIR))
        reach = targets(px, py)
        chunks = {}
        for chunk in range(4):
            values = {m: self.block(ox, oy, px, py, m, chunk).astype(jnp.float32) for m in slots}
            for t in box_set(px, py):
                total = begun[t][chunk * 16 : chunk * 16 + 16] if begun and t in begun else None
                for m in slots:
                    for kind in range(3):
                        if reach[m][kind] == t:
                            term = values[m] * weights[m, kind]
                            total = term if total is None else total + term
                if total is not None:
                    chunks.setdefault(t, []).append(total)
        return {t: jnp.concatenate(parts, axis=0) for t, parts in chunks.items()}


def couplings_of(column, s):
    return [
        place
        for place, (_, (ox, oy), other) in enumerate(around(*column))
        if (s[0] - ox, s[1] - oy) in box_set(*other)
    ]


def grouped_images(column):
    groups = [[], [], []]
    for s in image_set(*column):
        places = couplings_of(column, s)
        groups[1 if max(places) < 4 else 2 if min(places) > 1 else 0].append(s)
    return groups


GROUPS = {column: grouped_images(column) for column in COLUMNS}
SPANS = (slice(0, 6 * B), slice(0, 4 * B), slice(2 * B, 6 * B))
IMAGES = {column: sum(GROUPS[column], []) for column in COLUMNS}
USERS = {}
for _index, _column in enumerate(COLUMNS):
    for _place, (_, _box, _other) in enumerate(around(*_column)):
        USERS.setdefault((_box, _other), []).append((_index, _column, _place))
BEGUN = {
    (box, (px, py)): (1 if px == 0 else 2) if box == (0, 1) else (3 if py == 0 else 4)
    for box, (px, py) in USERS
    if box[1] == 1 or box[0] or (box == (0, 0) and py == 0)
}
LATE = [key for key in USERS if key[0][1] == -1]


def begun_targets(key):
    return targets(*key[1])[BEGUN[key]]


def place_rows(found, box, other, right, left_star, left_corner):
    unit = None
    if box == (0, 0):
        square = (PAIR, PAIR)
        diagonal = lax.broadcasted_iota(jnp.int32, square, 0) == lax.broadcasted_iota(jnp.int32, square, 1)
        unit = jnp.where(diagonal, 1.0, 0.0).astype(jnp.bfloat16)
    own = COLUMNS.index(other)
    for t, value in found.items():
        rounded = value.astype(jnp.bfloat16)
        for index, column, place in USERS[box, other]:
            position = IMAGES[column].index((box[0] + t[0], box[1] + t[1]))
            stored = swap_halves(value).astype(jnp.bfloat16) if place == 1 else rounded
            right[index, place * B : (place + 1) * B, position * PAIR : (position + 1) * PAIR] = stored
        if box == (0, 0):
            turned = lax.dot_general(
                unit, rounded, (((1,), (1,)), ((), ())), preferred_element_type=jnp.float32
            ).astype(jnp.bfloat16)
            turned = pair_lanes(turned[:B], turned[B:])
            if t in STAR:
                left_star[STAR.index(t) * B : (STAR.index(t) + 1) * B, own * PAIR : (own + 1) * PAIR] = turned
            else:
                left_corner[own] = turned


def fold(product):
    folded_half = low_half((HALF, PAIR))
    blocks = {}
    for pair in range(IMAGE_PAIRS):
        tile = product[:, pair * PAIR : (pair + 1) * PAIR]
        top, bottom = tile[:HALF], tile[HALF:]
        blocks[IMAGE[2 * pair]] = jnp.where(folded_half, top, swap_halves(bottom))
        if 2 * pair + 1 < len(IMAGE):
            blocks[IMAGE[2 * pair + 1]] = jnp.where(folded_half, swap_halves(top), bottom)
    return blocks


def begin_kernel(rows_ref, meta_ref, x_first, x_second, y_first, right, left_star, left_corner, begun_ref):
    rows = Rows(rows_ref, meta_ref, {1: x_first, -1: x_second}, {1: y_first}, {})
    for index, column in enumerate(COLUMNS):
        for place, (_, box, other) in enumerate(around(*column)):
            reached = {(box[0] + tx, box[1] + ty) for tx, ty in box_set(*other)}
            spans = sum(([span] * len(group) for span, group in zip(SPANS, GROUPS[column])), [])
            for position, s in enumerate(IMAGES[column]):
                if s not in reached and spans[position].start <= place * B < spans[position].stop:
                    right[index, place * B : (place + 1) * B, position * PAIR : (position + 1) * PAIR] = jnp.zeros(
                        (B, PAIR), jnp.bfloat16
                    )
    for box, other in USERS:
        if (box, other) in LATE:
            continue
        slots = list(range(SLOTS))
        open_targets = []
        if (box, other) in BEGUN:
            slots.remove(BEGUN[box, other])
            open_targets = begun_targets((box, other))
        found = rows.sums(box, other, slots)
        for place, t in enumerate(open_targets):
            begun_ref[list(BEGUN).index((box, other)), place] = found.pop(t)
        place_rows(found, box, other, right, left_star, left_corner)


def main_kernel(
    a_ref,
    rows_ref,
    meta_ref,
    x_first,
    x_second,
    y_first,
    y_second,
    c_first,
    c_second,
    begun_ref,
    right_in,
    left_star_in,
    left_corner_in,
    to_y_first,
    to_y_second,
    to_c_first,
    to_c_second,
    right,
    left_star,
    left_corner,
    image,
):
    rows = Rows(rows_ref, meta_ref, {1: x_first, -1: x_second}, {1: y_first, -1: y_second}, {1: c_first, -1: c_second})
    for number, ((box, other), slot) in enumerate(BEGUN.items()):
        begun = {t: begun_ref[number, place] for place, t in enumerate(begun_targets((box, other)))}
        place_rows(rows.sums(box, other, [slot], begun), box, other, right, left_star, left_corner)
    for box, other in LATE:
        place_rows(rows.sums(box, other, list(range(SLOTS))), box, other, right, left_star, left_corner)
    half = low_half((B, PAIR))
    for index, column in enumerate(COLUMNS):
        products, start = {}, 0
        for span, group in zip(SPANS, GROUPS[column]):
            lanes = slice(start * PAIR, (start + len(group)) * PAIR)
            product = jnp.dot(a_ref[index, :, span], right[index, span, lanes], preferred_element_type=jnp.float32)
            for place, s in enumerate(group):
                products[s] = product[:, place * PAIR : (place + 1) * PAIR]
            start += len(group)

        def part(s, z):
            if s not in products:
                return jnp.zeros((B, PAIR), jnp.float32)
            return products[s][z * B : (z + 1) * B]

        for pair in range(IMAGE_PAIRS):
            one = IMAGE[2 * pair]
            two = IMAGE[2 * pair + 1] if 2 * pair + 1 < len(IMAGE) else None
            low = jnp.where(half, part(one, 0), swap_halves(part(two, 0)))
            high = jnp.where(half, swap_halves(part(one, 1)), part(two, 1))
            start = index * PAIR
            lanes = slice(pair * PAIR, (pair + 1) * PAIR)
            image[start : start + B, lanes] = low.astype(jnp.bfloat16)
            image[start + B : start + PAIR, lanes] = high.astype(jnp.bfloat16)
    star = jnp.dot(left_star[0 : 2 * B, :], image[...], preferred_element_type=jnp.float32)

    def contribution(t):
        if t in STAR:
            return fold(star[STAR.index(t) * B : (STAR.index(t) + 1) * B])
        index = COLUMNS.index(column_of(*t))
        return fold(
            jnp.dot(
                left_corner[index], image[index * PAIR : (index + 1) * PAIR, :], preferred_element_type=jnp.float32
            )
        )

    for ref, sent in (
        (to_y_first, TO_Y_FIRST),
        (to_y_second, TO_Y_SECOND),
        (to_c_first, TO_C_FIRST),
        (to_c_second, TO_C_SECOND),
    ):
        parts = {t: contribution(t) for t in sorted({t for t, _ in sent})}
        for row, (t, s) in enumerate(sent):
            ref[row * HALF : (row + 1) * HALF, :] = parts[t][s].astype(jnp.bfloat16)


def message_block(ref, row):
    return ref[row * HALF : (row + 1) * HALF, :].astype(jnp.float32)


def relay_kernel(left_star, image, y_first, x_first, x_second):
    beside = jnp.dot(left_star[2 * B : 4 * B, :], image[...], preferred_element_type=jnp.float32)
    parts = {1: fold(beside[:B]), -1: fold(beside[B:])}
    for ref, tx in ((x_first, 1), (x_second, -1)):
        arrived = relayed(tx)
        for row, s in enumerate(TO_X[tx]):
            value = None
            if s in IMAGE:
                value = parts[tx][s]
            if s in arrived:
                more = message_block(y_first, arrived[s])
                value = more if value is None else value + more
            ref[row * HALF : (row + 1) * HALF, :] = value.astype(jnp.bfloat16)


def gathered(terms):
    total = None
    for ref, row, flag in terms:
        value = message_block(ref, row) if row is not None else ref
        if flag is not None:
            value = value * flag
        total = value if total is None else total + value
    return total


def inside():
    x, y = lax.axis_index("sx"), lax.axis_index("sy")
    return (
        ((x > 0) & (x < lax.axis_size("sx") - 1)).astype(jnp.float32),
        ((y > 0) & (y < lax.axis_size("sy") - 1)).astype(jnp.float32),
    )


def own_kernel(left_star, image, y_first, y_second, c_first, c_second, own_ref):
    centre = jnp.dot(left_star[4 * B : 5 * B, :], image[...], preferred_element_type=jnp.float32)
    has_x, has_y = inside()
    terms = {block: [] for block in STENCIL}
    for s, value in fold(centre).items():
        terms[s].append((value, None, None))
    for s, row in relayed(0).items():
        terms[s].append((y_first, row, None))
    for row, (_, s) in enumerate(TO_Y_SECOND):
        terms[s[0], -1 - s[1]].append((y_second, row, has_y))
    for row, (_, s) in enumerate(TO_C_FIRST):
        terms[1 - s[0], -1 - s[1]].append((c_first, row, has_y))
    for row, (_, s) in enumerate(TO_C_SECOND):
        terms[-1 - s[0], -1 - s[1]].append((c_second, row, has_x * has_y))
    for position, block in enumerate(OWN):
        own_ref[position] = gathered(terms[block])


def finish_kernel(own_ref, x_first, x_second, _, out_hbm, rows, sems):
    odd_x, odd_y = mirrored()
    has_x, _ = inside()
    terms = {block: [] for block in STENCIL}
    for position, block in enumerate(OWN):
        terms[block].append((own_ref[position], None, None))
    for row, s in enumerate(TO_X[1]):
        terms[1 - s[0], s[1]].append((x_first, row, None))
    for row, s in enumerate(TO_X[-1]):
        terms[-1 - s[0], s[1]].append((x_second, row, has_x))
    copies = []
    for jx in (0, 1, -1, 2, -2, 3, -3):
        row_here = jnp.where(odd_x == 1, 3 - jx, 3 + jx)
        reach = 3 - abs(jx)
        for jy in range(-reach, reach + 1):
            value = gathered(terms[jx, jy])
            column_here = jnp.where(odd_y == 1, 3 - jy, 3 + jy)
            rows[jx + 3, column_here, 0:HALF, :] = value[:, :B].astype(jnp.bfloat16)
            rows[jx + 3, column_here, HALF:B, :] = swap_halves(value)[:, :B].astype(jnp.bfloat16)
        span = pl.ds(3 - reach, 2 * reach + 1)
        copy = pltpu.make_async_copy(rows.at[jx + 3, span], out_hbm.at[row_here, span], sems.at[jx + 3])
        copy.start()
        copies.append(copy)
    for copy in copies:
        copy.wait()


def swapped(value, move_x, move_y):
    count_x, count_y = lax.axis_size("sx"), lax.axis_size("sy")

    def partner(index, move, count):
        if move == 0:
            return index
        found = index ^ 1 if move == 1 else ((index + 1) ^ 1) - 1
        return found if 0 <= found < count else None

    pairs = []
    for x in range(count_x):
        for y in range(count_y):
            to_x, to_y = partner(x, move_x, count_x), partner(y, move_y, count_y)
            if to_x is None:
                to_x, to_y = x, y ^ 1
            elif to_y is None:
                to_x, to_y = (x ^ 1 if move_x == 0 else to_x), y
            pairs.append((x * count_y + y, to_x * count_y + to_y))
    return lax.ppermute(value, ("sx", "sy"), pairs)


SMEM = pl.BlockSpec(memory_space=pltpu.SMEM)
VMEM = pl.BlockSpec(memory_space=pltpu.VMEM)
HBM = pl.BlockSpec(memory_space=pltpu.HBM)
ANY = pl.BlockSpec(memory_space=pl.ANY)


def call(kernel, in_specs, outs, scratch=(), out_specs=None, aliases=None, cost=None):
    return pl.pallas_call(
        kernel,
        out_shape=[jax.ShapeDtypeStruct(shape, dtype) for shape, dtype in outs],
        in_specs=in_specs,
        out_specs=out_specs or [VMEM] * len(outs),
        scratch_shapes=list(scratch),
        input_output_aliases=aliases or {},
        compiler_params=pltpu.CompilerParams(vmem_limit_bytes=VMEM_LIMIT),
        cost_estimate=None if cost is None else pl.CostEstimate(flops=cost, bytes_accessed=1, transcendentals=0),
    )


def in_hbm(*values):
    return [pltpu.with_memory_space_constraint(value, pltpu.HBM) for value in values]


def per_device(fine_matrix, prolongator, aggregate, face_links):
    bf16, f32 = jnp.bfloat16, jnp.float32
    message = ((BODY + TAIL, PAIR), bf16)
    longer = ((BODY + 2 * TAIL, PAIR), bf16)
    rows, meta, x_first, x_second = call(
        functools.partial(pack_kernel, lax.axis_size("sy")),
        [HBM, HBM, HBM],
        [((4, BLOCK_ROWS, PAIR), bf16), ((32, PAIR), f32), message, message],
        [
            pltpu.VMEM((4, 2, 7, B, B), bf16),
            pltpu.SMEM((2, 2, 2), jnp.int32),
            pltpu.SMEM((2, 2, 2, 6), jnp.int32),
            pltpu.SemaphoreType.DMA((4,)),
            pltpu.SemaphoreType.DMA((2,)),
        ],
    )(*in_hbm(aggregate, face_links, prolongator))
    y_first, y_second = call(pack_y_kernel, [VMEM] * 2, [message, longer])(rows, meta)
    y_second = swapped(y_second, 0, 2)
    x_first, x_second = swapped(x_first, 1, 0), swapped(x_second, 2, 0)
    y_first = swapped(y_first, 0, 1)
    whole = ((7, 7, B, B), bf16)
    matrix, out = call(
        pack_matrix_kernel,
        [HBM, HBM],
        [((4, PAIR, 6 * B), bf16), whole],
        [
            pltpu.VMEM((2, 2, 2, 7, B, B), bf16),
            pltpu.SMEM((2, 2, 2, 6), jnp.int32),
            pltpu.VMEM((3, B, B), bf16),
            pltpu.SemaphoreType.DMA((5,)),
            pltpu.SemaphoreType.DMA((12,)),
        ],
        [VMEM, HBM],
    )(*in_hbm(face_links, fine_matrix))
    note = ((2 * TAIL, PAIR), bf16)
    notes, notes_again = call(notes_kernel, [VMEM, VMEM, ANY], [note, ((48, PAIR), bf16)])(
        x_first, x_second, matrix
    )
    c_first, c_second = swapped(notes, 0, 1), swapped(notes_again, 0, 2)

    def sent(blocks):
        return ((len(blocks) * HALF, PAIR), bf16)

    lefts = [
        ((4, SLOTS * B, 10 * PAIR), bf16),
        ((len(STAR) * B, 4 * PAIR), bf16),
        ((4, B, PAIR), bf16),
    ]
    *lefts_begun, begun = call(begin_kernel, [VMEM] * 5, lefts + [((len(BEGUN), 3, B, PAIR), f32)], cost=1)(
        rows, meta, x_first, x_second, y_first
    )
    y_first, y_second, c_first, c_second, _, left_star, _, image = call(
        main_kernel,
        [VMEM] * 13,
        [
            sent(TO_Y_FIRST),
            sent(TO_Y_SECOND),
            sent(TO_C_FIRST),
            sent(TO_C_SECOND),
        ]
        + lefts
        + [((4 * PAIR, IMAGE_PAIRS * PAIR), bf16)],
        aliases={10: 4, 11: 5, 12: 6},
    )(
        matrix,
        rows,
        meta,
        x_first,
        x_second,
        y_first,
        y_second,
        c_first,
        c_second,
        begun,
        *(pltpu.with_memory_space_constraint(left, pltpu.VMEM) for left in lefts_begun),
    )
    y_second = swapped(y_second, 0, 2)
    c_first, c_second = swapped(c_first, 1, 2), swapped(c_second, 2, 2)
    y_first = swapped(y_first, 0, 1)
    x_first, x_second = call(relay_kernel, [VMEM] * 3, [sent(TO_X[1]), sent(TO_X[-1])])(left_star, image, y_first)
    x_first, x_second = swapped(x_first, 1, 0), swapped(x_second, 2, 0)
    (own,) = call(own_kernel, [VMEM] * 6, [((len(OWN), HALF, PAIR), f32)], cost=3_000_000_000)(
        left_star, image, y_first, y_second, c_first, c_second
    )
    (out,) = call(
        finish_kernel,
        [VMEM] * 3 + [HBM],
        [whole],
        [pltpu.VMEM((7, 7, B, B), bf16), pltpu.SemaphoreType.DMA((7,))],
        [HBM],
        {3: 0},
    )(own, x_first, x_second, out)
    return out[None, None]


def solution(mesh):
    return jax.shard_map(
        per_device,
        mesh=mesh,
        in_specs=(
            P("sx", "sy", None, None, None, None),
            P("sx", "sy", None, None, None, None),
            P("sx", "sy", None),
            P("sx", "sy", None, None),
        ),
        out_specs=P("sx", "sy", None, None, None, None),
        check_vma=False,
    )
```

```python
import functools

import jax
import jax.numpy as jnp
from jax import lax
from jax.experimental import pallas as pl
from jax.experimental.pallas import tpu as pltpu
from jax.sharding import PartitionSpec as P


B = 64
HALF = B // 2
PAIR = 2 * B
SLOTS = 6
BLOCK_ROWS = SLOTS * B
BODY = 2 * BLOCK_ROWS
TAIL = 16
VMEM_LIMIT = 20 * 1024 * 1024

FACES = [(0, 0), (-1, 0), (1, 0), (0, -1), (0, 1), (0, 0)]
COLUMNS = [(0, 0), (0, 1), (1, 0), (1, 1)]
SIDES_X = (0, 2, 1, 3, 4, 5)
SIDES_Y = (0, 1, 2, 4, 3, 5)


def targets(px, py):
    table = []
    for dx, dy in FACES:
        ox, nx = divmod(px + dx, 2)
        oy, ny = divmod(py + dy, 2)
        table.append([(ox, oy), (ox + 2 * nx - 1, oy), (ox, oy + 2 * ny - 1)])
    return table


def box_set(px, py):
    return sorted({t for row in targets(px, py) for t in row})


def around(px, py):
    (mx, out_x), (my, out_y) = (2, 1) if px == 0 else (1, 2), (4, 3) if py == 0 else (3, 4)
    found = []
    for m in (0, 5, mx, my, out_x, out_y):
        ox, nx = divmod(px + FACES[m][0], 2)
        oy, ny = divmod(py + FACES[m][1], 2)
        found.append((m, (ox, oy), (nx, ny)))
    return found


def image_set(px, py):
    found = set()
    for _, (ox, oy), column in around(px, py):
        found |= {(ox + tx, oy + ty) for tx, ty in box_set(*column)}
    return sorted(found)


IMAGE = sorted({s for column in COLUMNS for s in image_set(*column)})
IMAGE_PAIRS = (len(IMAGE) + 1) // 2
STAR = [(0, 1), (0, -1), (1, 0), (-1, 0), (0, 0)]


def column_of(tx, ty):
    return ((tx + 1) // 2, (ty + 1) // 2)


def blocks_of(tx, ty):
    return IMAGE if (tx, ty) in STAR else image_set(*column_of(tx, ty))


TO_Y_FIRST = [((tx, 1), s) for tx in (0, -1, 1) for s in blocks_of(tx, 1)]
TO_Y_SECOND = [((0, -1), s) for s in blocks_of(0, -1)]
TO_C_FIRST = [((1, -1), s) for s in blocks_of(1, -1)]
TO_C_SECOND = [((-1, -1), s) for s in blocks_of(-1, -1)]


def relayed(tx):
    return {(s[0], 1 - s[1]): row for row, (t, s) in enumerate(TO_Y_FIRST) if t[0] == tx}


TO_X = {tx: sorted(set(IMAGE) | set(relayed(tx))) for tx in (1, -1)}
STENCIL = [(jx, jy) for jx in range(-3, 4) for jy in range(-3, 4) if abs(jx) + abs(jy) <= 3]
OWN = sorted(
    set(IMAGE)
    | set(relayed(0))
    | {(s[0], -1 - s[1]) for _, s in TO_Y_SECOND}
    | {(1 - s[0], -1 - s[1]) for _, s in TO_C_FIRST}
    | {(-1 - s[0], -1 - s[1]) for _, s in TO_C_SECOND}
)


def low_half(shape):
    return lax.broadcasted_iota(jnp.int32, shape, len(shape) - 1) < B


def swap_halves(value):
    if value.dtype == jnp.bfloat16:
        return jnp.concatenate([value[..., B:], value[..., :B]], axis=-1)
    return pltpu.roll(value, B, value.ndim - 1)


def pair_lanes(left, right):
    return jnp.concatenate([left, right], axis=-1)


def mirrored():
    return lax.axis_index("sx") % 2, lax.axis_index("sy") % 2


def slot_here(m, z, odd_x, odd_y):
    if m in (1, 2):
        return jnp.where(odd_x == 1, 3 - m, m)
    if m in (3, 4):
        return jnp.where(odd_y == 1, 7 - m, m)
    return 6 - z if m == 5 else m


def fill_rows(rows, values):
    shape = (rows, PAIR)
    row = lax.broadcasted_iota(jnp.int32, shape, 0)
    half = low_half(shape)
    filled = jnp.zeros(shape, jnp.float32)
    for index, (low, high) in enumerate(values):
        filled = jnp.where(row == index, jnp.where(half, low, high), filled)
    return filled


def pack_kernel(
    boxes_y,
    aggregate_hbm,
    links_hbm,
    p_hbm,
    rows_ref,
    meta_ref,
    x_first,
    x_second,
    p_ref,
    aggregate_ref,
    links_ref,
    p_sems,
    sems,
):
    odd_x, odd_y = mirrored()
    own = lax.axis_index("sx") * boxes_y + lax.axis_index("sy")
    place = {(px, py): (px ^ odd_x, py ^ odd_y) for px, py in COLUMNS}
    copies = [
        pltpu.make_async_copy(p_hbm.at[place[column]], p_ref.at[index], p_sems.at[index])
        for index, column in enumerate(COLUMNS)
    ]
    small = [
        pltpu.make_async_copy(aggregate_hbm, aggregate_ref, sems.at[0]),
        pltpu.make_async_copy(links_hbm, links_ref, sems.at[1]),
    ]
    for copy in small + copies:
        copy.start()
    for copy in small:
        copy.wait()

    def state(column, z):
        shift = aggregate_ref[place[column] + (z,)] - own
        across_x = (shift == boxes_y) | (shift == -boxes_y)
        return jnp.where(shift == 0, 0, jnp.where(across_x, 1, 2)).astype(jnp.float32)

    def link(column, m):
        faces = [slot_here(m, z, odd_x, odd_y) - 1 for z in (0, 1)]
        return tuple(links_ref[place[column] + (z, faces[z])].astype(jnp.float32) for z in (0, 1))

    states = [tuple(state(column, z) for z in (0, 1)) for column in COLUMNS]
    links = {column: [link(column, m) for m in range(1, SLOTS)] for column in COLUMNS}
    meta_ref[...] = fill_rows(32, states + sum((links[column] for column in COLUMNS), []))
    messages = (
        (x_first, ((1, 0), (1, 1))),
        (x_second, ((0, 0), (0, 1))),
    )
    for ref, columns in messages:
        tail = fill_rows(TAIL, states + links[columns[0]] + links[columns[1]])
        ref[BODY : BODY + TAIL, :] = tail.astype(jnp.bfloat16)
    for index, column in enumerate(COLUMNS):
        copies[index].wait()
        for m in range(SLOTS):
            packed = pair_lanes(*(p_ref[index, z, slot_here(m, z, odd_x, odd_y)] for z in (0, 1)))
            rows_ref[index, m * B : (m + 1) * B, :] = packed
            for ref, columns in messages:
                if column in columns:
                    start = columns.index(column) * BLOCK_ROWS + m * B
                    ref[start : start + B, :] = packed


def pack_y_kernel(rows_ref, meta_ref, y_first, y_second):
    meta = meta_ref[...]
    for ref, columns in ((y_first, (1, 3)), (y_second, (0, 2))):
        parts = [meta[0:4]]
        for place, index in enumerate(columns):
            ref[place * BLOCK_ROWS : (place + 1) * BLOCK_ROWS, :] = rows_ref[index]
            parts.append(meta[4 + (SLOTS - 1) * index : 4 + (SLOTS - 1) * (index + 1)])
        parts.append(jnp.zeros((2, PAIR), jnp.float32))
        ref[BODY : BODY + TAIL, :] = jnp.concatenate(parts, axis=0).astype(jnp.bfloat16)


def notes_kernel(x_first, x_second, _, notes_ref, again_ref):
    for ref in (notes_ref, again_ref):
        ref[0:TAIL, :] = x_first[BODY : BODY + TAIL, :]
        ref[TAIL : 2 * TAIL, :] = x_second[BODY : BODY + TAIL, :]


def pack_matrix_kernel(links_hbm, a_hbm, out_ref, whole_hbm, a_ref, links_ref, zeros, a_sems, sems):
    fetches = [
        pltpu.make_async_copy(links_hbm, links_ref, a_sems.at[4]),
        *(
            pltpu.make_async_copy(a_hbm.at[px, py], a_ref.at[px, py], a_sems.at[index])
            for index, (px, py) in enumerate(COLUMNS)
        ),
    ]
    for fetch in fetches:
        fetch.start()
    zeros[...] = jnp.zeros(zeros.shape, zeros.dtype)
    copies = []
    for jx in range(-3, 4):
        width = abs(jx)
        if width:
            for start in (0, 7 - width):
                copies.append(
                    pltpu.make_async_copy(
                        zeros.at[pl.ds(0, width)], whole_hbm.at[jx + 3, pl.ds(start, width)], sems.at[len(copies)]
                    )
                )
    for copy in copies:
        copy.start()
    for fetch in fetches:
        fetch.wait()
    odd_x, odd_y = mirrored()
    for index, (px, py) in enumerate(COLUMNS):
        place = (px ^ odd_x, py ^ odd_y)
        for z in (0, 1):
            blocks = []
            for m, _, _ in around(px, py):
                slot = slot_here(m, z, odd_x, odd_y)
                block = a_ref[place + (z, slot)]
                if m > 0:
                    present = links_ref[place + (z, slot - 1)] == 1
                    block = jnp.where(present, block, jnp.zeros_like(block))
                blocks.append(block)
            for pair in range(3):
                out_ref[index, z * B : (z + 1) * B, pair * PAIR : (pair + 1) * PAIR] = pair_lanes(
                    blocks[2 * pair], blocks[2 * pair + 1]
                )
    for copy in copies:
        copy.wait()


def there(ox, oy, px, py):
    return (1 - px if ox else px, 1 - py if oy else py)


def slot_there(ox, oy, m):
    m = SIDES_X[m] if ox else m
    return SIDES_Y[m] if oy else m


class Rows:
    def __init__(self, rows_ref, meta_ref, from_x, from_y, corners):
        self.rows_ref, self.from_x, self.from_y = rows_ref, from_x, from_y
        self.notes = {(0, 0): meta_ref[...]}
        for side, ref in from_x.items():
            self.notes[side, 0] = ref[BODY : BODY + TAIL, :].astype(jnp.float32)
        for side, ref in from_y.items():
            self.notes[0, side] = ref[BODY : BODY + TAIL, :].astype(jnp.float32)
        for oy, ref in corners.items():
            self.notes[1, oy] = ref[0:TAIL, :].astype(jnp.float32)
            self.notes[-1, oy] = ref[TAIL : 2 * TAIL, :].astype(jnp.float32)

    def state_row(self, ox, oy, px, py):
        index = COLUMNS.index(there(ox, oy, px, py))
        return self.notes[ox, oy][index : index + 1]

    def link_row(self, ox, oy, px, py, m):
        if (ox, oy) == (0, 0):
            index = (SLOTS - 1) * COLUMNS.index((px, py))
        else:
            index = (SLOTS - 1) * (py if ox else px)
        index += 4 + slot_there(ox, oy, m) - 1
        return self.notes[ox, oy][index : index + 1]

    def block(self, ox, oy, px, py, m, chunk):
        start = slot_there(ox, oy, m) * B + chunk * 16
        if (ox, oy) == (0, 0):
            return self.rows_ref[COLUMNS.index((px, py)), start : start + 16, :]
        start += (py if ox else px) * BLOCK_ROWS
        ref = self.from_x[ox] if ox else self.from_y[oy]
        return ref[start : start + 16, :]

    def sums(self, box, column, slots, begun=None):
        (ox, oy), (px, py) = box, column
        weights = {}
        for m in slots:
            dx, dy = FACES[m]
            bx, nx = divmod(2 * ox + px + dx, 2)
            by, ny = divmod(2 * oy + py + dy, 2)
            state = self.state_row(bx, by, nx, ny)
            if m == 5:
                state = swap_halves(state)
            for kind in range(3):
                weight = jnp.where(state == kind, 1.0, 0.0)
                if m > 0:
                    weight = weight * self.link_row(ox, oy, px, py, m)
                weights[m, kind] = jnp.broadcast_to(weight, (16, PAIR))
        reach = targets(px, py)
        chunks = {}
        for chunk in range(4):
            values = {m: self.block(ox, oy, px, py, m, chunk).astype(jnp.float32) for m in slots}
            for t in box_set(px, py):
                total = begun[t][chunk * 16 : chunk * 16 + 16] if begun and t in begun else None
                for m in slots:
                    for kind in range(3):
                        if reach[m][kind] == t:
                            term = values[m] * weights[m, kind]
                            total = term if total is None else total + term
                if total is not None:
                    chunks.setdefault(t, []).append(total)
        return {t: jnp.concatenate(parts, axis=0) for t, parts in chunks.items()}


def couplings_of(column, s):
    return [
        place
        for place, (_, (ox, oy), other) in enumerate(around(*column))
        if (s[0] - ox, s[1] - oy) in box_set(*other)
    ]


def grouped_images(column):
    groups = [[], [], []]
    for s in image_set(*column):
        places = couplings_of(column, s)
        groups[1 if max(places) < 4 else 2 if min(places) > 1 else 0].append(s)
    return groups


GROUPS = {column: grouped_images(column) for column in COLUMNS}
SPANS = (slice(0, 6 * B), slice(0, 4 * B), slice(2 * B, 6 * B))
IMAGES = {column: sum(GROUPS[column], []) for column in COLUMNS}
USERS = {}
for _index, _column in enumerate(COLUMNS):
    for _place, (_, _box, _other) in enumerate(around(*_column)):
        USERS.setdefault((_box, _other), []).append((_index, _column, _place))
BEGUN = {
    (box, (px, py)): (1 if px == 0 else 2) if box == (0, 1) else (3 if py == 0 else 4)
    for box, (px, py) in USERS
    if box[1] == 1 or box[0] or (box == (0, 0) and py == 0)
}
LATE = [key for key in USERS if key[0][1] == -1]


def begun_targets(key):
    return targets(*key[1])[BEGUN[key]]


def place_rows(found, box, other, right, left_star, left_corner):
    unit = None
    if box == (0, 0):
        square = (PAIR, PAIR)
        diagonal = lax.broadcasted_iota(jnp.int32, square, 0) == lax.broadcasted_iota(jnp.int32, square, 1)
        unit = jnp.where(diagonal, 1.0, 0.0).astype(jnp.bfloat16)
    own = COLUMNS.index(other)
    for t, value in found.items():
        rounded = value.astype(jnp.bfloat16)
        for index, column, place in USERS[box, other]:
            position = IMAGES[column].index((box[0] + t[0], box[1] + t[1]))
            stored = swap_halves(value).astype(jnp.bfloat16) if place == 1 else rounded
            right[index, place * B : (place + 1) * B, position * PAIR : (position + 1) * PAIR] = stored
        if box == (0, 0):
            turned = lax.dot_general(
                unit, rounded, (((1,), (1,)), ((), ())), preferred_element_type=jnp.float32
            ).astype(jnp.bfloat16)
            turned = pair_lanes(turned[:B], turned[B:])
            if t in STAR:
                left_star[STAR.index(t) * B : (STAR.index(t) + 1) * B, own * PAIR : (own + 1) * PAIR] = turned
            else:
                left_corner[own] = turned


def fold(product):
    folded_half = low_half((HALF, PAIR))
    blocks = {}
    for pair in range(IMAGE_PAIRS):
        tile = product[:, pair * PAIR : (pair + 1) * PAIR]
        top, bottom = tile[:HALF], tile[HALF:]
        blocks[IMAGE[2 * pair]] = jnp.where(folded_half, top, swap_halves(bottom))
        if 2 * pair + 1 < len(IMAGE):
            blocks[IMAGE[2 * pair + 1]] = jnp.where(folded_half, swap_halves(top), bottom)
    return blocks


def begin_kernel(rows_ref, meta_ref, x_first, x_second, y_first, right, left_star, left_corner, begun_ref):
    rows = Rows(rows_ref, meta_ref, {1: x_first, -1: x_second}, {1: y_first}, {})
    for index, column in enumerate(COLUMNS):
        for place, (_, box, other) in enumerate(around(*column)):
            reached = {(box[0] + tx, box[1] + ty) for tx, ty in box_set(*other)}
            spans = sum(([span] * len(group) for span, group in zip(SPANS, GROUPS[column])), [])
            for position, s in enumerate(IMAGES[column]):
                if s not in reached and spans[position].start <= place * B < spans[position].stop:
                    right[index, place * B : (place + 1) * B, position * PAIR : (position + 1) * PAIR] = jnp.zeros(
                        (B, PAIR), jnp.bfloat16
                    )
    for box, other in USERS:
        if (box, other) in LATE:
            continue
        slots = list(range(SLOTS))
        open_targets = []
        if (box, other) in BEGUN:
            slots.remove(BEGUN[box, other])
            open_targets = begun_targets((box, other))
        found = rows.sums(box, other, slots)
        for place, t in enumerate(open_targets):
            begun_ref[list(BEGUN).index((box, other)), place] = found.pop(t)
        place_rows(found, box, other, right, left_star, left_corner)


def main_kernel(
    a_ref,
    rows_ref,
    meta_ref,
    x_first,
    x_second,
    y_first,
    y_second,
    c_first,
    c_second,
    begun_ref,
    right_in,
    left_star_in,
    left_corner_in,
    to_y_first,
    to_y_second,
    to_c_first,
    to_c_second,
    right,
    left_star,
    left_corner,
    image,
):
    rows = Rows(rows_ref, meta_ref, {1: x_first, -1: x_second}, {1: y_first, -1: y_second}, {1: c_first, -1: c_second})
    for number, ((box, other), slot) in enumerate(BEGUN.items()):
        begun = {t: begun_ref[number, place] for place, t in enumerate(begun_targets((box, other)))}
        place_rows(rows.sums(box, other, [slot], begun), box, other, right, left_star, left_corner)
    for box, other in LATE:
        place_rows(rows.sums(box, other, list(range(SLOTS))), box, other, right, left_star, left_corner)
    half = low_half((B, PAIR))
    for index, column in enumerate(COLUMNS):
        products, start = {}, 0
        for span, group in zip(SPANS, GROUPS[column]):
            lanes = slice(start * PAIR, (start + len(group)) * PAIR)
            product = jnp.dot(a_ref[index, :, span], right[index, span, lanes], preferred_element_type=jnp.float32)
            for place, s in enumerate(group):
                products[s] = product[:, place * PAIR : (place + 1) * PAIR].astype(jnp.bfloat16)
            start += len(group)

        def part(s, z):
            if s not in products:
                return jnp.zeros((B, PAIR), jnp.bfloat16)
            return products[s][z * B : (z + 1) * B]

        for pair in range(IMAGE_PAIRS):
            one = IMAGE[2 * pair]
            two = IMAGE[2 * pair + 1] if 2 * pair + 1 < len(IMAGE) else None
            low = jnp.where(half, part(one, 0), swap_halves(part(two, 0)))
            high = jnp.where(half, swap_halves(part(one, 1)), part(two, 1))
            start = index * PAIR
            lanes = slice(pair * PAIR, (pair + 1) * PAIR)
            image[start : start + B, lanes] = low
            image[start + B : start + PAIR, lanes] = high
    star = jnp.dot(left_star[0 : 2 * B, :], image[...], preferred_element_type=jnp.float32)

    def contribution(t):
        if t in STAR:
            return fold(star[STAR.index(t) * B : (STAR.index(t) + 1) * B])
        index = COLUMNS.index(column_of(*t))
        return fold(
            jnp.dot(
                left_corner[index], image[index * PAIR : (index + 1) * PAIR, :], preferred_element_type=jnp.float32
            )
        )

    for ref, sent in (
        (to_y_first, TO_Y_FIRST),
        (to_y_second, TO_Y_SECOND),
        (to_c_first, TO_C_FIRST),
        (to_c_second, TO_C_SECOND),
    ):
        parts = {t: contribution(t) for t in sorted({t for t, _ in sent})}
        for row, (t, s) in enumerate(sent):
            ref[row * HALF : (row + 1) * HALF, :] = parts[t][s].astype(jnp.bfloat16)


def message_block(ref, row):
    return ref[row * HALF : (row + 1) * HALF, :].astype(jnp.float32)


def relay_kernel(left_star, image, y_first, x_first, x_second):
    beside = jnp.dot(left_star[2 * B : 4 * B, :], image[...], preferred_element_type=jnp.float32)
    parts = {1: fold(beside[:B]), -1: fold(beside[B:])}
    for ref, tx in ((x_first, 1), (x_second, -1)):
        arrived = relayed(tx)
        for row, s in enumerate(TO_X[tx]):
            value = None
            if s in IMAGE:
                value = parts[tx][s]
            if s in arrived:
                more = message_block(y_first, arrived[s])
                value = more if value is None else value + more
            ref[row * HALF : (row + 1) * HALF, :] = value.astype(jnp.bfloat16)


def gathered(terms):
    total = None
    for ref, row, flag in terms:
        value = message_block(ref, row) if row is not None else ref
        if flag is not None:
            value = value * flag
        total = value if total is None else total + value
    return total


def inside():
    x, y = lax.axis_index("sx"), lax.axis_index("sy")
    return (
        ((x > 0) & (x < lax.axis_size("sx") - 1)).astype(jnp.float32),
        ((y > 0) & (y < lax.axis_size("sy") - 1)).astype(jnp.float32),
    )


def own_kernel(left_star, image, y_first, y_second, c_first, c_second, own_ref):
    centre = jnp.dot(left_star[4 * B : 5 * B, :], image[...], preferred_element_type=jnp.float32)
    has_x, has_y = inside()
    terms = {block: [] for block in STENCIL}
    for s, value in fold(centre).items():
        terms[s].append((value, None, None))
    for s, row in relayed(0).items():
        terms[s].append((y_first, row, None))
    for row, (_, s) in enumerate(TO_Y_SECOND):
        terms[s[0], -1 - s[1]].append((y_second, row, has_y))
    for row, (_, s) in enumerate(TO_C_FIRST):
        terms[1 - s[0], -1 - s[1]].append((c_first, row, has_y))
    for row, (_, s) in enumerate(TO_C_SECOND):
        terms[-1 - s[0], -1 - s[1]].append((c_second, row, has_x * has_y))
    for position, block in enumerate(OWN):
        own_ref[position] = gathered(terms[block])


def finish_kernel(own_ref, x_first, x_second, _, out_hbm, rows, sems):
    odd_x, odd_y = mirrored()
    has_x, _ = inside()
    terms = {block: [] for block in STENCIL}
    for position, block in enumerate(OWN):
        terms[block].append((own_ref[position], None, None))
    for row, s in enumerate(TO_X[1]):
        terms[1 - s[0], s[1]].append((x_first, row, None))
    for row, s in enumerate(TO_X[-1]):
        terms[-1 - s[0], s[1]].append((x_second, row, has_x))
    copies = []
    for jx in (0, 1, -1, 2, -2, 3, -3):
        row_here = jnp.where(odd_x == 1, 3 - jx, 3 + jx)
        reach = 3 - abs(jx)
        for jy in range(-reach, reach + 1):
            value = gathered(terms[jx, jy])
            column_here = jnp.where(odd_y == 1, 3 - jy, 3 + jy)
            rows[jx + 3, column_here, 0:HALF, :] = value[:, :B].astype(jnp.bfloat16)
            rows[jx + 3, column_here, HALF:B, :] = swap_halves(value)[:, :B].astype(jnp.bfloat16)
        span = pl.ds(3 - reach, 2 * reach + 1)
        copy = pltpu.make_async_copy(rows.at[jx + 3, span], out_hbm.at[row_here, span], sems.at[jx + 3])
        copy.start()
        copies.append(copy)
    for copy in copies:
        copy.wait()


def swapped(value, move_x, move_y):
    count_x, count_y = lax.axis_size("sx"), lax.axis_size("sy")

    def partner(index, move, count):
        if move == 0:
            return index
        found = index ^ 1 if move == 1 else ((index + 1) ^ 1) - 1
        return found if 0 <= found < count else None

    pairs = []
    for x in range(count_x):
        for y in range(count_y):
            to_x, to_y = partner(x, move_x, count_x), partner(y, move_y, count_y)
            if to_x is None:
                to_x, to_y = x, y ^ 1
            elif to_y is None:
                to_x, to_y = (x ^ 1 if move_x == 0 else to_x), y
            pairs.append((x * count_y + y, to_x * count_y + to_y))
    return lax.ppermute(value, ("sx", "sy"), pairs)


SMEM = pl.BlockSpec(memory_space=pltpu.SMEM)
VMEM = pl.BlockSpec(memory_space=pltpu.VMEM)
HBM = pl.BlockSpec(memory_space=pltpu.HBM)
ANY = pl.BlockSpec(memory_space=pl.ANY)


def call(kernel, in_specs, outs, scratch=(), out_specs=None, aliases=None, cost=None):
    return pl.pallas_call(
        kernel,
        out_shape=[jax.ShapeDtypeStruct(shape, dtype) for shape, dtype in outs],
        in_specs=in_specs,
        out_specs=out_specs or [VMEM] * len(outs),
        scratch_shapes=list(scratch),
        input_output_aliases=aliases or {},
        compiler_params=pltpu.CompilerParams(vmem_limit_bytes=VMEM_LIMIT),
        cost_estimate=None if cost is None else pl.CostEstimate(flops=cost, bytes_accessed=1, transcendentals=0),
    )


def in_hbm(*values):
    return [pltpu.with_memory_space_constraint(value, pltpu.HBM) for value in values]


def per_device(fine_matrix, prolongator, aggregate, face_links):
    bf16, f32 = jnp.bfloat16, jnp.float32
    message = ((BODY + TAIL, PAIR), bf16)
    longer = ((BODY + 2 * TAIL, PAIR), bf16)
    rows, meta, x_first, x_second = call(
        functools.partial(pack_kernel, lax.axis_size("sy")),
        [HBM, HBM, HBM],
        [((4, BLOCK_ROWS, PAIR), bf16), ((32, PAIR), f32), message, message],
        [
            pltpu.VMEM((4, 2, 7, B, B), bf16),
            pltpu.SMEM((2, 2, 2), jnp.int32),
            pltpu.SMEM((2, 2, 2, 6), jnp.int32),
            pltpu.SemaphoreType.DMA((4,)),
            pltpu.SemaphoreType.DMA((2,)),
        ],
    )(*in_hbm(aggregate, face_links, prolongator))
    y_first, y_second = call(pack_y_kernel, [VMEM] * 2, [message, longer])(rows, meta)
    y_second = swapped(y_second, 0, 2)
    x_first, x_second = swapped(x_first, 1, 0), swapped(x_second, 2, 0)
    y_first = swapped(y_first, 0, 1)
    whole = ((7, 7, B, B), bf16)
    matrix, out = call(
        pack_matrix_kernel,
        [HBM, HBM],
        [((4, PAIR, 6 * B), bf16), whole],
        [
            pltpu.VMEM((2, 2, 2, 7, B, B), bf16),
            pltpu.SMEM((2, 2, 2, 6), jnp.int32),
            pltpu.VMEM((3, B, B), bf16),
            pltpu.SemaphoreType.DMA((5,)),
            pltpu.SemaphoreType.DMA((12,)),
        ],
        [VMEM, HBM],
    )(*in_hbm(face_links, fine_matrix))
    note = ((2 * TAIL, PAIR), bf16)
    notes, notes_again = call(notes_kernel, [VMEM, VMEM, ANY], [note, ((48, PAIR), bf16)])(
        x_first, x_second, matrix
    )
    c_first, c_second = swapped(notes, 0, 1), swapped(notes_again, 0, 2)

    def sent(blocks):
        return ((len(blocks) * HALF, PAIR), bf16)

    lefts = [
        ((4, SLOTS * B, 10 * PAIR), bf16),
        ((len(STAR) * B, 4 * PAIR), bf16),
        ((4, B, PAIR), bf16),
    ]
    *lefts_begun, begun = call(begin_kernel, [VMEM] * 5, lefts + [((len(BEGUN), 3, B, PAIR), f32)], cost=1)(
        rows, meta, x_first, x_second, y_first
    )
    y_first, y_second, c_first, c_second, _, left_star, _, image = call(
        main_kernel,
        [VMEM] * 13,
        [
            sent(TO_Y_FIRST),
            sent(TO_Y_SECOND),
            sent(TO_C_FIRST),
            sent(TO_C_SECOND),
        ]
        + lefts
        + [((4 * PAIR, IMAGE_PAIRS * PAIR), bf16)],
        aliases={10: 4, 11: 5, 12: 6},
    )(
        matrix,
        rows,
        meta,
        x_first,
        x_second,
        y_first,
        y_second,
        c_first,
        c_second,
        begun,
        *(pltpu.with_memory_space_constraint(left, pltpu.VMEM) for left in lefts_begun),
    )
    y_second = swapped(y_second, 0, 2)
    c_first, c_second = swapped(c_first, 1, 2), swapped(c_second, 2, 2)
    y_first = swapped(y_first, 0, 1)
    x_first, x_second = call(relay_kernel, [VMEM] * 3, [sent(TO_X[1]), sent(TO_X[-1])])(left_star, image, y_first)
    x_first, x_second = swapped(x_first, 1, 0), swapped(x_second, 2, 0)
    (own,) = call(own_kernel, [VMEM] * 6, [((len(OWN), HALF, PAIR), f32)], cost=3_000_000_000)(
        left_star, image, y_first, y_second, c_first, c_second
    )
    (out,) = call(
        finish_kernel,
        [VMEM] * 3 + [HBM],
        [whole],
        [pltpu.VMEM((7, 7, B, B), bf16), pltpu.SemaphoreType.DMA((7,))],
        [HBM],
        {3: 0},
    )(own, x_first, x_second, out)
    return out[None, None]


def solution(mesh):
    return jax.shard_map(
        per_device,
        mesh=mesh,
        in_specs=(
            P("sx", "sy", None, None, None, None),
            P("sx", "sy", None, None, None, None),
            P("sx", "sy", None),
            P("sx", "sy", None, None),
        ),
        out_specs=P("sx", "sy", None, None, None, None),
        check_vma=False,
    )
```
